32 devices in a mesh: rows: 4 (over y, x), cols: 8 (over z, core).
Axes of the slice: x: 2, y: 2, z: 4, core: 2. Of those that a mesh axis runs over, the one named last changes fastest.
Arguments:
- file_pixels: bfloat16 [48, 128, 1024], P(None, ('rows', 'cols')), may hold values from -6 to 6
- patchify_weight: bfloat16 [64, 48], replicated, may hold values from -0.875 to 0.875
- patchify_bias: float32 [64], replicated, may hold values from -3 to 3
- norm_gain: float32 [64], replicated, may hold values from 0.5 to 1.5
- norm_offset_vector: float32 [64], replicated, may hold values from -3 to 3
- kernel: float32 [64, 49], replicated, may hold values from -0.875 to 0.875
- kernel_offset: float32 [64], replicated, may hold values from -3 to 3
- cotangent: bfloat16 [64, 128, 1024], P(None, 'rows', 'cols'), may hold values from -10 to 10, as said below
Outputs:
- stem_output: bfloat16 [64, 128, 1024], P(None, 'rows', 'cols')
- weight_grad: float32 [64, 48], replicated
- bias_grad: float32 [64], replicated
- norm_scale_gradient: float32 [64], replicated
- shift_grad: float32 [64], replicated
- kernel_grad: float32 [64, 49], replicated
- offset_grad: float32 [64], replicated
The draws below stay inside these ranges and needn't reach their ends.
Inputs may be any that keep to these rules, and one draw needn't show every extreme that they name: A cotangent of order one.
All inputs are finite; a program needn't handle non-finite values.
Results may differ from the reference program's by a relative error of at most 0.0055.
Values may be sent and summed in bfloat16 or wider, within the bound.
No kernel may reach another device: no remote copies, remote signals or barrier semaphores. Data moves between devices by JAX's collectives and lax.ppermute only.
A program may use at most 128 MiB of HBM per device.

```python
import math
import jax
import jax.numpy as jnp
from jax import lax

CH = 64
PIX = 48
KS = 7
H_DEV = 32
NH = 128
NW = 1024


def draw_cotangent(key, part):
    row_pos = jnp.arange(NH, dtype=jnp.float32)[:, None] / NH
    col_pos = jnp.arange(NW, dtype=jnp.float32)[None, :] / NW
    level = 0.5 + row_pos + col_pos
    base = jnp.clip(jax.random.normal(key, (CH, NH, NW), jnp.float32), -4.0, 4.0)
    return (base * level[None]).astype(jnp.bfloat16)


def steps_of(own_key, extent, split, smallest, largest):
    def one(axis_at, parts):
        heights = jax.random.uniform(jax.random.fold_in(jax.random.fold_in(own_key, 6), axis_at), (parts,), jnp.float32, smallest / len(split), largest / len(split))
        return jnp.repeat(jnp.exp(heights), extent[axis_at] // parts).reshape((-1,) + (1,) * (len(extent) - axis_at - 1))

    level = one(*split[0])
    for cut in split[1:]:
        level = level * one(*cut)
    return level


def normal_values(stream_key, dims, scale, most, pieces=(), kind=jnp.bfloat16):
    array = jax.random.normal(stream_key, dims, jnp.float32) * scale
    if len(pieces) > 0:
        array = steps_of(stream_key, dims, pieces, -0.22, 0.18) * array
    return jnp.clip(array, min=-most, max=most).astype(kind)


def setup_inputs(seed: int = 0) -> dict:
    arg_keys = jax.random.split(jax.random.key(seed), 9)
    return {
        "file_pixels": normal_values(arg_keys[0], (PIX, NH, NW), 1.0, 6.0, ((1, 32),)),
        "patchify_weight": normal_values(arg_keys[1], (CH, PIX), PIX ** -0.5, 0.875),
        "patchify_bias": normal_values(arg_keys[2], (CH,), 0.5, 3.0, (), jnp.float32),
        "norm_gain": jnp.clip(1.0 + 0.1 * jax.random.normal(arg_keys[3], (CH,), jnp.float32), 0.5, 1.5),
        "norm_offset_vector": normal_values(arg_keys[4], (CH,), 0.5, 3.0, (), jnp.float32),
        "kernel": normal_values(arg_keys[5], (CH, KS * KS), (KS * KS) ** -0.5, 0.875, (), jnp.float32),
        "kernel_offset": normal_values(arg_keys[6], (CH,), 0.5, 3.0, (), jnp.float32),
        "cotangent": draw_cotangent(jax.random.fold_in(arg_keys[8], 71), 0),
    }


norm_eps = 1e-06

def embed_patches(pixel_values, weight, bias):
    flat = pixel_values.reshape(pixel_values.shape[0], -1)
    mixed = jnp.dot(weight, flat, preferred_element_type=jnp.float32) + bias[:, None]
    return mixed.astype(jnp.bfloat16).reshape(weight.shape[0], pixel_values.shape[1], pixel_values.shape[2])

def apply_layer_norm(patch_embedding):
    values = patch_embedding.astype(jnp.float32)
    center = values - lax.optimization_barrier(jnp.mean(values, axis=0, keepdims=True))
    spread = lax.optimization_barrier(jnp.mean(center * center, axis=0, keepdims=True))
    inverse_deviation = lax.rsqrt(spread + norm_eps)
    return (center * inverse_deviation, inverse_deviation)

def reference(file_pixels, patchify_weight, patchify_bias, norm_gain, norm_offset_vector, kernel, kernel_offset, cotangent):
    blocks = NH // H_DEV
    pix_blocks = file_pixels.reshape(PIX, blocks, H_DEV, NW).transpose(1, 0, 2, 3)
    scale_factor = norm_gain[:, None, None]
    offset_vector = norm_offset_vector[:, None, None]

    def forward_block(pixel_values):
        centered_input, inverse_deviation = apply_layer_norm(embed_patches(pixel_values, patchify_weight, patchify_bias))
        return (centered_input * scale_factor + offset_vector).astype(jnp.bfloat16)
    normalized_output = lax.map(forward_block, pix_blocks).transpose(1, 0, 2, 3).reshape(CH, NH, NW)
    factor = 1.0 / math.sqrt(NH * NW)

    def per_channel(items):
        plane, cot, taps, offset = items
        padded = jnp.pad(plane, 3)
        cot_pad = jnp.pad(cot, 3)
        upstream = cot.astype(jnp.float32) * factor
        total = jnp.zeros((NH, NW), jnp.float32) + offset
        back = jnp.zeros((NH, NW), jnp.float32)
        grads = []
        for tap_row in range(KS):
            for tap_col in range(KS):
                window = padded[tap_row:tap_row + NH, tap_col:tap_col + NW].astype(jnp.float32)
                total = total + taps[tap_row * KS + tap_col] * window
                grads.append(jnp.sum(window * upstream))
                mirror = cot_pad[6 - tap_row:6 - tap_row + NH, 6 - tap_col:6 - tap_col + NW].astype(jnp.float32)
                back = back + taps[tap_row * KS + tap_col] * mirror
        return (total.astype(jnp.bfloat16), jnp.stack(grads), jnp.sum(upstream), back * factor)
    stem_output, kernel_grad, offset_grad, normalized_gradient = lax.map(per_channel, (normalized_output, cotangent, kernel, kernel_offset))
    grad_blocks = normalized_gradient.reshape(CH, blocks, H_DEV, NW).transpose(1, 0, 2, 3)

    def backward_block(carry, items):
        pixel_values, upper_bound = items
        centered_input, inverse_deviation = apply_layer_norm(embed_patches(pixel_values, patchify_weight, patchify_bias))
        input_gradient = upper_bound * scale_factor
        patch_gradient = inverse_deviation * (input_gradient - lax.optimization_barrier(jnp.mean(input_gradient, axis=0, keepdims=True)) - centered_input * lax.optimization_barrier(jnp.mean(input_gradient * centered_input, axis=0, keepdims=True)))
        patch_gradient = patch_gradient.astype(jnp.bfloat16)
        partial_weight = lax.dot_general(patch_gradient.reshape(CH, -1), pixel_values.reshape(PIX, -1), (((1,), (1,)), ((), ())), preferred_element_type=jnp.float32)
        partial_pieces = (partial_weight, lax.optimization_barrier(jnp.sum(patch_gradient.astype(jnp.float32), axis=(1, 2))), lax.optimization_barrier(jnp.sum(upper_bound * centered_input, axis=(1, 2))), lax.optimization_barrier(jnp.sum(upper_bound, axis=(1, 2))))
        return (jax.tree.map(lambda a, b: a + b, carry, partial_pieces), None)
    start = (jnp.zeros((CH, PIX), jnp.float32), jnp.zeros((CH,), jnp.float32), jnp.zeros((CH,), jnp.float32), jnp.zeros((CH,), jnp.float32))
    sums, unused = lax.scan(backward_block, start, (pix_blocks, grad_blocks))
    weight_grad, bias_grad, norm_scale_gradient, shift_grad = sums
    return (stem_output, weight_grad, bias_grad, norm_scale_gradient, shift_grad, kernel_grad, offset_grad)
```

```python
import functools
import math

import jax
import jax.numpy as jnp
from jax import lax
from jax.experimental import pallas as pl
from jax.experimental.pallas import tpu as pltpu
from jax.sharding import PartitionSpec as P

norm_eps = 1e-06
side = 7
LANES = 128
GROUP = 8
PITCH = 48
DEPTH = 8 * PITCH
VMEM = 56 * 1024 * 1024
bf16, f32 = jnp.bfloat16, jnp.float32

NN = (((1,), (0,)), ((), ()))
NT = (((1,), (1,)), ((), ()))
TN = (((0,), (0,)), ((), ()))


def mm(a, b, dims=NN):
    return lax.dot_general(a, b, dims, preferred_element_type=f32)


def iota(shape, axis):
    return lax.broadcasted_iota(jnp.int32, shape, axis)


def split2(x):
    high = x.astype(bf16)
    return high, (x - high.astype(f32)).astype(bf16)


def one_hot(cond):
    return jnp.where(cond, 1.0, 0.0).astype(bf16)


def cdiv(a, b):
    return -(-a // b)


def bucket(x, width, count):
    return sum((x >= width * n).astype(jnp.int32) for n in range(1, count))


def params_kernel(colors, file_rows, wt_ref, taps_ref, bias_ref, gain_ref, off_ref, koff_ref,
                  wk_ref, wh_ref, kb_ref, kf_ref, vec_ref):
    channels = wt_ref.shape[1]
    rows = channels * GROUP
    block = colors * file_rows
    per = GROUP // file_rows

    def weights(width, out_ref):
        lanes = per * width
        src = iota((colors, lanes), 1)
        part = bucket(src, width, per)
        inside = src - part * width
        color = bucket(inside, file_rows, cdiv(width, file_rows))
        spread = one_hot((color == iota((colors, lanes), 0)) & (inside < block))
        wide = mm(wt_ref[...], spread, TN).astype(bf16)
        row = iota((rows, channels), 0)
        tall = one_hot(lax.shift_right_logical(row, 3) == iota((rows, channels), 1))
        full = mm(tall, wide)
        src = iota((rows, lanes), 1)
        part = bucket(src, width, per)
        inside = src - part * width
        own = part * file_rows + lax.bitwise_and(inside, file_rows - 1)
        keep = own == lax.bitwise_and(iota((rows, lanes), 0), GROUP - 1)
        out_ref[...] = jnp.where(keep, full, 0.0).astype(bf16)

    weights(block, wk_ref)
    weights(wh_ref.shape[1] // per, wh_ref)

    taps = taps_ref[...]
    count = taps.shape[0]
    lane = iota((count, DEPTH), 1)
    copy = bucket(lane, PITCH, 8)
    at = lane - copy * PITCH - 5
    tap = at * side + copy
    valid = (at >= 0) & (at < side) & (copy < side)
    forward = jnp.where(valid & (tap == iota((count, DEPTH), 0)), 1.0, 0.0)
    backward = jnp.where(valid & (count - 1 - tap == iota((count, DEPTH), 0)), 1.0, 0.0)
    kf_ref[...] = lax.dot_general(taps, forward, TN, precision=lax.Precision.HIGHEST,
                                  preferred_element_type=f32)
    kb_ref[...] = lax.dot_general(taps, backward, TN, precision=lax.Precision.HIGHEST,
                                  preferred_element_type=f32)

    eye = iota((channels, channels), 0) == iota((channels, channels), 1)
    for n, ref in enumerate((bias_ref, gain_ref, off_ref, koff_ref)):
        row = jnp.broadcast_to(ref[...].reshape(1, channels), (channels, channels))
        column = jnp.sum(jnp.where(eye, row, 0.0), axis=1, keepdims=True)
        vec_ref[n] = jnp.broadcast_to(column, (channels, LANES))


def pack_kernel(x_ref, out_ref):
    colors, file_rows, width = x_ref.shape
    count = width // LANES
    block = colors * file_rows
    row, lane = iota((16, LANES), 0), iota((16, LANES), 1)
    pick = one_hot(((row < 3) & (lane == row + LANES - 3)) | ((row >= 11) & (row < 14) & (lane == row - 11)))
    edges = []
    for d in range(count):
        tile = x_ref[:, :, d * LANES:(d + 1) * LANES].reshape(block, LANES)
        out_ref[d, :block, :] = tile
        edges.append(mm(pick, tile, NT))
    none = jnp.zeros((8, block), f32)
    for d in range(count):
        left = edges[d - 1][:8] if d > 0 else none
        right = edges[d + 1][8:] if d < count - 1 else none
        halo = left + right
        chunks = []
        for start in range(0, 2 * LANES, LANES):
            stop = min(start + LANES, block)
            if stop <= start:
                chunks.append(jnp.zeros((8, LANES), f32))
            elif stop - start < LANES:
                chunks.append(jnp.concatenate(
                    [halo[:, start:stop], jnp.zeros((8, LANES - stop + start), f32)], axis=1))
            else:
                chunks.append(halo[:, start:stop])
        out_ref[d, block:block + 16, :] = jnp.concatenate(chunks, axis=0).astype(bf16)


def edges_kernel(cot_ref, top_ref, bot_ref, all_ref, edge_ref):
    channels, height, width = cot_ref.shape
    zeros = jnp.zeros((channels, 4, width), f32)
    top = jnp.concatenate([zeros, top_ref[...].astype(f32)], axis=1)
    bot = jnp.concatenate([bot_ref[...].astype(f32), zeros], axis=1)
    full = jnp.concatenate([top, cot_ref[...].astype(f32), bot], axis=1).astype(bf16)
    all_ref[...] = full
    row, lane = iota((8, width), 0), iota((8, width), 1)
    pick = one_hot(((row < 3) & (lane == row)) | ((row >= 3) & (row < 6) & (lane == row + width - 6)))
    edge_ref[...] = mm(pick, full.reshape(channels * PITCH, width), NT).astype(bf16)


def shifted(center, halo):
    rows, width = center.shape
    lane = iota((rows, width), 1)
    copies = []
    for move in range(-3, 4):
        if move == 0:
            copies.append(center)
        elif move > 0:
            copies.append(pltpu.roll(jnp.where(lane < move, halo, center), width - move, 1))
        else:
            copies.append(pltpu.roll(jnp.where(lane >= width + move, halo, center), -move, 1))
    copies.append(jnp.zeros((rows, width), center.dtype))
    return jnp.concatenate(copies, axis=0)


def toeplitz(base, height):
    taps = pltpu.roll(jnp.broadcast_to(base, (height, DEPTH)), 0, 1, stride=1, stride_axis=0)
    return jnp.concatenate(split2(taps), axis=0)


def back_kernel(factor, all_ref, left_ref, right_ref, kb_ref, halo_ref, grad_ref, sum_ref):
    channels, _, width = all_ref.shape
    height = grad_ref.shape[1]
    row, lane = iota((8, width), 0), iota((8, width), 1)
    from_left = one_hot((row >= 3) & (row < 6) & (lane == row + width - 6))
    from_right = one_hot((row < 3) & (lane == row))
    halo = mm(left_ref[...], from_left, TN) + mm(right_ref[...], from_right, TN)
    halo_ref[...] = halo.astype(bf16).reshape(channels, PITCH, width)

    def one(k, carry):
        plane = all_ref[k]
        stack = shifted(plane, halo_ref[k])
        both = mm(toeplitz(kb_ref[pl.ds(k, 1), :], height), stack)
        grad = (both[:height] + both[height:]) * factor
        grad_ref[k] = grad
        own = plane.astype(f32)[8:8 + height]
        sum_ref[0, k] = jnp.sum(grad.reshape(height // 8, 8, width), axis=0)
        sum_ref[1, k] = jnp.sum(own.reshape(height // 8, 8, width), axis=0) * factor
        return carry

    lax.fori_loop(0, channels, one, 0, unroll=4)


def layer_norm(patch, channels):
    values = patch.astype(bf16).astype(f32).reshape(channels, GROUP, LANES)
    center = values - jnp.mean(values, axis=0, keepdims=True)
    spread = jnp.mean(center * center, axis=0, keepdims=True)
    inverse = lax.rsqrt(spread + norm_eps)
    return center * inverse, inverse


def per_row(vec_ref, n):
    return vec_ref[n][:, None, :]


def main_kernel(colors, file_rows, factor, x_ref, wk_ref, vec_ref, grad_ref, sum_ref, all_ref, halo_ref,
                norm_ref, out_ref, norm_s, gram_s, diag_s):
    channels, height, width = grad_ref.shape
    block = colors * file_rows
    per = GROUP // file_rows
    inner = per * block
    rows = channels * GROUP
    bias, gain, offset = per_row(vec_ref, 0), per_row(vec_ref, 1), per_row(vec_ref, 2)
    scale_part = jnp.zeros((channels, GROUP, width), f32)
    ones = jnp.where(iota((16, width), 0) == 0, 1.0, 0.0).astype(bf16)
    for g in range(height // GROUP):
        pixels = jnp.concatenate([x_ref[per * g + a, :block, :] for a in range(per)], axis=0)
        patch = mm(wk_ref[...], pixels).reshape(channels, GROUP, width) + bias
        xhat, inverse = layer_norm(patch, channels)
        norm_s[:, g * GROUP:(g + 1) * GROUP, :] = xhat * gain + offset
        grad = grad_ref[:, g * GROUP:(g + 1) * GROUP, :]
        scale_part += grad * xhat
        inside = grad * gain
        mean_a = jnp.mean(inside, axis=0, keepdims=True)
        mean_b = jnp.mean(inside * xhat, axis=0, keepdims=True)
        patch_grad = (inverse * (inside - mean_a - xhat * mean_b)).astype(bf16).reshape(rows, width)
        gram = mm(jnp.concatenate([pixels, ones], axis=0), patch_grad, NT)
        if g == 0:
            gram_s[...] = gram
        else:
            gram_s[...] += gram

    def one(k, carry):
        plane = norm_s[k].astype(bf16)
        norm_ref[k] = plane
        stack = shifted(all_ref[k], halo_ref[k])
        cross = mm(plane, stack, NT)
        total = cross[:8]
        for a in range(1, height // 8):
            total += pltpu.roll(cross[8 * a:8 * a + 8], DEPTH - 8 * a, 1)
        diag_s[k] = total
        return carry

    lax.fori_loop(0, channels, one, 0, unroll=4)

    line = diag_s[:, 0, :]
    for b in range(1, 8):
        line += pltpu.roll(diag_s[:, b, :], DEPTH - b, 1)
    lane = iota((56, DEPTH), 1)
    copy = bucket(lane, PITCH, 8)
    at = lane - copy * PITCH - 5
    valid = (at >= 0) & (at < side) & (copy < side)
    taps = one_hot(valid & (side * side - 1 - at * side - copy == iota((56, DEPTH), 0)))
    line = jnp.concatenate([jnp.zeros((LANES - channels, DEPTH), f32), line], axis=0)
    result = sum(mm(taps, part, NT) for part in split2(line * factor))

    gather = one_hot(lax.shift_right_logical(iota((rows, LANES), 0), 3) == iota((rows, LANES), 1))
    src = iota((inner + 16, rows), 0)
    part = bucket(src, block, per + 1)
    own = part * file_rows + lax.bitwise_and(src - part * block, file_rows - 1)
    keep = (own == lax.bitwise_and(iota((inner + 16, rows), 1), GROUP - 1)) | (src >= inner)
    gram = jnp.where(keep, gram_s[...], 0.0)
    by_channel = sum(mm(part, gather) for part in split2(gram))
    src = iota((56, inner + 16), 1)
    part = bucket(src, block, per + 1)
    color = bucket(src - part * block, file_rows, colors)
    target = iota((56, inner + 16), 0)
    fold = one_hot(((color == target) & (src < inner)) | ((src == inner) & (target == colors)))
    result += sum(mm(fold, part) for part in split2(by_channel))
    for n, part in enumerate((scale_part, sum_ref[0], sum_ref[1])):
        pick = one_hot(iota((56, LANES), 0) == colors + 1 + n)
        line = sum(mm(pick, piece, NT) for piece in split2(part.reshape(rows, width)))
        result += sum(mm(piece, gather) for piece in split2(line))
    out_ref[...] = result


def stem_kernel(colors, file_rows, edge_ref, x_ref, top_ref, bot_ref, wk_ref, wh_ref, vec_ref, kf_ref, norm_ref,
                out_ref, all_s, halo_s):
    channels, height, width = norm_ref.shape
    block = colors * file_rows
    per = GROUP // file_rows
    half = per // 2
    chunks = wh_ref.shape[1] // (per * LANES)
    bias, gain, offset = per_row(vec_ref, 0), per_row(vec_ref, 1), per_row(vec_ref, 2)
    no_top, no_bot = edge_ref[0], edge_ref[1]
    no_left, no_right = edge_ref[2], edge_ref[3]
    shape = (channels, GROUP, width)
    lower = iota(shape, 1) < 4
    row_ok = jnp.where(lower, 1 - no_bot, 1 - no_top) > 0

    outer = [bot_ref[a] for a in range(half)] + [top_ref[a] for a in range(half)]
    pixels = jnp.concatenate([piece[:block] for piece in outer], axis=0)
    xhat, _ = layer_norm(mm(wk_ref[...], pixels).reshape(shape) + bias, channels)
    rows = jnp.where(row_ok, xhat * gain + offset, 0.0).astype(bf16)
    all_s[:, 0:8, :] = rows
    all_s[:, 8 + height:16 + height, :] = rows
    all_s[:, 8:8 + height, :] = norm_ref[...]

    groups = height // GROUP
    lines = []
    for g in range(groups + 1):
        pieces = []
        for a in range(per):
            piece = outer[a][block:block + 16] if g == groups else x_ref[per * g + a, block:block + 16, :]
            piece = piece.astype(f32)
            pieces += [piece[8 * c:8 * c + 8] for c in range(chunks)]
        lines.append(jnp.concatenate(pieces, axis=1))
    lines.append(jnp.zeros((LANES - 8 * len(lines), per * chunks * LANES), f32))
    lines = jnp.concatenate(lines, axis=0).astype(bf16)
    xhat, _ = layer_norm(mm(wh_ref[...], lines, NT).reshape(shape) + bias, channels)
    lane = iota(shape, 2)
    column = lax.bitwise_and(lane, 7)
    ok = jnp.where(column < 3, 1 - no_left, 1 - no_right) > 0
    ok = ok & (row_ok | (lane < 8 * groups))
    halo = jnp.where(ok, xhat * gain + offset, 0.0).astype(bf16).reshape(channels * GROUP, width)
    for g in range(groups + 1):
        moved = pltpu.roll(halo, width - 8 * g - 3, 1).reshape(shape)
        if g < groups:
            halo_s[:, 8 + 8 * g:16 + 8 * g, :] = moved
        else:
            halo_s[:, 0:8, :] = moved
            halo_s[:, 8 + height:16 + height, :] = moved

    def one(k, carry):
        both = mm(toeplitz(kf_ref[pl.ds(k, 1), :], height), shifted(all_s[k], halo_s[k]))
        out_ref[k] = (both[:height] + both[height:] + vec_ref[3, pl.ds(k, 1), :]).astype(bf16)
        return carry

    lax.fori_loop(0, channels, one, 0, unroll=4)


def kernel_call(body, out_shape, us, **kw):
    return pl.pallas_call(
        body,
        out_shape=out_shape,
        compiler_params=pltpu.CompilerParams(vmem_limit_bytes=VMEM),
        cost_estimate=pl.CostEstimate(flops=int(us * 1e9), bytes_accessed=int(us * 3e6), transcendentals=0),
        **kw,
    )


def shaped(shape, dtype):
    return jax.ShapeDtypeStruct(shape, dtype)


def shift(x, axis, step):
    count = lax.axis_size(axis)
    pairs = [(i, i + step) for i in range(count) if 0 <= i + step < count]
    return lax.ppermute(x, axis, pairs)


def total(x):
    for axis in ("cols", "rows"):
        count = lax.axis_size(axis)
        step = 1
        while step < count:
            x = x + lax.ppermute(x, axis, [(i, i ^ step) for i in range(count)])
            step *= 2
    return x


def per_device(
    file_pixels,
    patchify_weight,
    patchify_bias,
    norm_gain,
    norm_offset_vector,
    kernel,
    kernel_offset,
    cotangent,
):
    colors, file_rows, _ = file_pixels.shape
    channels, height, width = cotangent.shape
    n_rows, n_cols = lax.axis_size("rows"), lax.axis_size("cols")
    factor = 1.0 / math.sqrt(height * n_rows * width * n_cols)
    block = colors * file_rows
    per = GROUP // file_rows
    block_rows = block + 16
    padded = cdiv(block, LANES) * LANES
    rows = channels * GROUP
    tile = (channels, height, width)

    packed = kernel_call(pack_kernel, shaped((n_cols, block_rows, LANES), bf16), 2)(file_pixels)
    pixels = lax.all_to_all(packed, "cols", split_axis=0, concat_axis=0, tiled=True)

    top = shift(cotangent[:, height - 4:, :], "rows", 1)
    bot = shift(cotangent[:, :4, :], "rows", -1)
    cot_all, edges = kernel_call(
        edges_kernel,
        (shaped((channels, PITCH, width), bf16), shaped((8, channels * PITCH), bf16)),
        1.5,
    )(cotangent, top, bot)
    from_left = shift(edges, "cols", 1)
    from_right = shift(edges, "cols", -1)
    wk, wh, kb, kf, vec = kernel_call(
        functools.partial(params_kernel, colors, file_rows),
        (
            shaped((rows, per * block), bf16),
            shaped((rows, per * padded), bf16),
            shaped((channels, DEPTH), f32),
            shaped((channels, DEPTH), f32),
            shaped((4, channels, LANES), f32),
        ),
        1.5,
    )(patchify_weight.T, kernel.T, patchify_bias, norm_gain, norm_offset_vector, kernel_offset)
    cot_halo, grad, sums = kernel_call(
        functools.partial(back_kernel, factor),
        (
            shaped((channels, PITCH, width), bf16),
            shaped(tile, f32),
            shaped((2, channels, GROUP, width), f32),
        ),
        5,
    )(cot_all, from_left, from_right, kb)

    norm, part = kernel_call(
        functools.partial(main_kernel, colors, file_rows, factor),
        (shaped(tile, bf16), shaped((56, LANES), f32)),
        6,
        scratch_shapes=[
            pltpu.VMEM(tile, f32),
            pltpu.VMEM((per * block + 16, rows), f32),
            pltpu.VMEM((channels, 8, DEPTH), f32),
        ],
    )(pixels, wk, vec, grad, sums, cot_all, cot_halo)

    half = per // 2
    top = shift(pixels[n_cols - half:], "rows", 1)
    bot = shift(pixels[:half], "rows", -1)
    row_at, col_at = lax.axis_index("rows"), lax.axis_index("cols")
    at_edge = jnp.stack([row_at == 0, row_at == n_rows - 1, col_at == 0, col_at == n_cols - 1])
    vmem = pl.BlockSpec(memory_space=pltpu.VMEM)
    stem_output = kernel_call(
        functools.partial(stem_kernel, colors, file_rows),
        shaped(tile, bf16),
        5,
        in_specs=[pl.BlockSpec(memory_space=pltpu.SMEM)] + [vmem] * 8,
        scratch_shapes=[pltpu.VMEM((channels, PITCH, width), bf16)] * 2,
    )(at_edge.astype(jnp.int32), pixels, top, bot, wk, wh, vec, kf, norm)

    result = total(part)
    taps = side * side
    first, second = result[:, :channels], result[:, channels:2 * channels]
    return (
        stem_output,
        first[:colors].T,
        first[colors],
        first[colors + 1],
        first[colors + 2],
        second[:taps].T,
        first[colors + 3],
    )


def solution(mesh):
    return jax.shard_map(
        per_device,
        mesh=mesh,
        in_specs=(
            P(None, ("rows", "cols"), None),
            P(),
            P(),
            P(),
            P(),
            P(),
            P(),
            P(None, "rows", "cols"),
        ),
        out_specs=(P(None, "rows", "cols"), P(), P(), P(), P(), P(), P()),
        check_vma=False,
    )
```

```python
import functools
import math

import jax
import jax.numpy as jnp
import numpy as np
from jax import lax
from jax.experimental import pallas as pl
from jax.experimental.pallas import tpu as pltpu
from jax.sharding import PartitionSpec as P

norm_eps = 1e-06
side = 7
LANES = 128
GROUP = 8
PITCH = 48
DEPTH = 8 * PITCH
VMEM = 20 * 1024 * 1024
UNROLL = 16
bf16, f32 = jnp.bfloat16, jnp.float32

NN = (((1,), (0,)), ((), ()))
NT = (((1,), (1,)), ((), ()))
TN = (((0,), (0,)), ((), ()))


def mm(a, b, dims=NN):
    return lax.dot_general(a, b, dims, preferred_element_type=f32)


def iota(shape, axis):
    return lax.broadcasted_iota(jnp.int32, shape, axis)


def split2(x):
    high = x.astype(bf16)
    return high, (x - high.astype(f32)).astype(bf16)


def one_hot(cond):
    return jnp.where(cond, 1.0, 0.0).astype(bf16)


def cdiv(a, b):
    return -(-a // b)


def constants(colors, file_rows, channels):
    block = colors * file_rows
    per = GROUP // file_rows
    rows = channels * GROUP
    inner = per * block
    out = {}

    def source(width):
        at = np.arange(per * width)
        part, inside = at // width, at % width
        ok = inside < block
        return np.where(ok, inside // file_rows, -1), np.where(ok, part * file_rows + inside % file_rows, -1)

    for name, width in (("", block), ("_halo", cdiv(block, LANES) * LANES)):
        color, row = source(width)
        out["spread" + name] = color[None, :] == np.arange(colors)[:, None]
        out["keep" + name] = row[None, :] == (np.arange(rows) % GROUP)[:, None]
    out["tall"] = (np.arange(rows) // GROUP)[:, None] == np.arange(channels)[None, :]
    out["gather"] = (np.arange(rows) // GROUP)[:, None] == np.arange(LANES)[None, :]
    color, row = source(block)
    out["diagonal"] = np.concatenate([out["keep"].T, np.ones((16, rows), bool)])
    fold = np.zeros((56, inner + 16), bool)
    fold[color, np.arange(inner)] = True
    fold[colors, inner] = True
    out["fold"] = fold
    lane = np.arange(DEPTH)
    copy, at = lane // PITCH, lane % PITCH - 5
    tap = np.where((at >= 0) & (at < side) & (copy < side), at * side + copy, -1)
    count = side * side
    out["forward"] = tap[None, :] == np.arange(count)[:, None]
    out["backward"] = (tap >= 0)[None, :] & (count - 1 - tap[None, :] == np.arange(count)[:, None])
    out["taps"] = np.concatenate([out["backward"], np.zeros((56 - count, DEPTH), bool)])
    pick = np.zeros((3, 56, LANES), bool)
    for n in range(3):
        pick[n, colors + 1 + n] = True
    out["pick"] = np.concatenate(list(pick), axis=1)
    return {k: jnp.asarray(v, f32 if k in ("forward", "backward") else bf16) for k, v in out.items()}


def params_kernel(wt_ref, taps_ref, bias_ref, gain_ref, off_ref, koff_ref, spread_ref, keep_ref, spread_h_ref,
                  keep_h_ref, tall_ref, forward_ref, backward_ref, wk_ref, wh_ref, kb_ref, kf_ref, vec_ref):
    channels = wt_ref.shape[1]
    for spread, keep, out_ref in ((spread_ref, keep_ref, wk_ref), (spread_h_ref, keep_h_ref, wh_ref)):
        wide = mm(wt_ref[...], spread[...], TN).astype(bf16)
        out_ref[...] = mm(tall_ref[...], wide).astype(bf16) * keep[...]
    for place, out_ref in ((forward_ref, kf_ref), (backward_ref, kb_ref)):
        out_ref[...] = lax.dot_general(taps_ref[...], place[...], TN, precision=lax.Precision.HIGHEST,
                                       preferred_element_type=f32)
    eye = iota((channels, channels), 0) == iota((channels, channels), 1)
    for n, ref in enumerate((bias_ref, gain_ref, off_ref, koff_ref)):
        row = jnp.broadcast_to(ref[...].reshape(1, channels), (channels, channels))
        column = jnp.sum(jnp.where(eye, row, 0.0), axis=1, keepdims=True)
        vec_ref[n] = jnp.broadcast_to(column, (channels, LANES))


def pack_kernel(at_ref, x_hbm, cot_hbm, cot_ref, keep_ref, give_ref, edge_ref, edge_s, x_ref, sems):
    colors, file_rows, width = x_ref.shape
    channels, height, _ = cot_ref.shape
    chips, block_rows, _ = keep_ref.shape
    count = width // LANES
    block = colors * file_rows
    core, chip = at_ref[0], at_ref[1]
    load_x = pltpu.make_async_copy(x_hbm, x_ref, sems.at[0])
    load_cot = pltpu.make_async_copy(cot_hbm, cot_ref, sems.at[1])
    load_x.start()
    load_cot.start()
    load_cot.wait()

    row, lane = iota((8, LANES), 0), iota((8, LANES), 1)
    pick = one_hot(((row < 3) & (lane == row)) | ((row >= 3) & (row < 6) & (lane == row + LANES - 6)))
    edges = mm(pick, cot_ref[...].reshape(channels * height, LANES), NT)
    edges = jnp.concatenate(
        [edges[:, n:n + LANES] for n in range(0, channels * height, LANES)], axis=0).astype(bf16)
    edge_ref[...] = edges
    give_ref[chips * block_rows:, :] = edges
    load_x.wait()

    row, lane = iota((16, LANES), 0), iota((16, LANES), 1)
    pick = one_hot(((row < 3) & (lane == row + LANES - 3)) | ((row >= 11) & (row < 14) & (lane == row - 11)))
    zeros = jnp.zeros((16, block), f32)
    edge_s[0] = zeros
    edge_s[count + 1] = zeros
    for d in range(count):
        tile = x_ref[:, :, d * LANES:(d + 1) * LANES].reshape(block, LANES)
        edge_s[d + 1] = mm(pick, tile, NT)

    def halo(d):
        both = edge_s[d][:8] + edge_s[d + 2][8:]
        chunks = []
        for start in range(0, 2 * LANES, LANES):
            stop = min(start + LANES, block)
            if stop <= start:
                chunks.append(jnp.zeros((8, LANES), f32))
            elif stop - start < LANES:
                chunks.append(jnp.concatenate(
                    [both[:, start:stop], jnp.zeros((8, LANES - stop + start), f32)], axis=1))
            else:
                chunks.append(both[:, start:stop])
        return jnp.concatenate(chunks, axis=0).astype(bf16)

    for away in range(chips):
        there = lax.rem(chip + away, chips)
        for other in range(2):
            d = 2 * there + (core if other == 0 else 1 - core)
            tile = x_ref[:, :, pl.ds(pl.multiple_of(d * LANES, LANES), LANES)].reshape(block, LANES)
            if other == 0:
                keep_ref[away, :block, :] = tile
                keep_ref[away, block:, :] = halo(d)
            else:
                start = away * block_rows
                give_ref[start:start + block, :] = tile
                give_ref[start + block:start + block_rows, :] = halo(d)


def pair_kernel(keep_ref, got_ref, *pair_refs):
    _, block_rows, _ = keep_ref.shape
    for away, ref in enumerate(pair_refs):
        ref[0] = keep_ref[away]
        ref[1] = got_ref[away * block_rows:(away + 1) * block_rows, :]


def strips_kernel(at_ref, cot_ref, near_ref, far_ref, halo_ref, one_ref, two_ref):
    channels, height, width = cot_ref.shape
    size = far_ref.shape[0]
    core = at_ref[0]
    near = near_ref[near_ref.shape[0] - size:, :].astype(f32)
    far = far_ref[...].astype(f32)
    left = jnp.where(core == 0, far, near)
    right = jnp.where(core == 0, near, far)
    left = jnp.concatenate([left[n:n + 8] for n in range(0, size, 8)], axis=1).astype(bf16)
    right = jnp.concatenate([right[n:n + 8] for n in range(0, size, 8)], axis=1).astype(bf16)
    row, lane = iota((8, width), 0), iota((8, width), 1)
    from_left = one_hot((row >= 3) & (row < 6) & (lane == row + width - 6) & (at_ref[4] == 0))
    from_right = one_hot((row < 3) & (lane == row) & (at_ref[5] == 0))
    halo = (mm(left, from_left, TN) + mm(right, from_right, TN)).reshape(channels, height, width)
    halo_ref[...] = halo.astype(bf16)
    own = cot_ref[...].astype(f32)
    up = jnp.concatenate([own[:, :4], halo[:, :4]], axis=1)
    down = jnp.concatenate([own[:, height - 4:], halo[:, height - 4:]], axis=1)
    even = at_ref[6] == 0
    one_ref[...] = jnp.where(even, down, up).astype(bf16)
    two_ref[...] = jnp.where(even, up, down).astype(bf16)


def shifted(center, halo):
    rows, width = center.shape
    lane = iota((rows, width), 1)
    copies = []
    for move in range(-3, 4):
        if move == 0:
            copies.append(center)
        elif move > 0:
            copies.append(pltpu.roll(jnp.where(lane < move, halo, center), width - move, 1))
        else:
            copies.append(pltpu.roll(jnp.where(lane >= width + move, halo, center), -move, 1))
    copies.append(jnp.zeros((rows, width), center.dtype))
    return jnp.concatenate(copies, axis=0)


def toeplitz(base, height):
    taps = pltpu.roll(jnp.broadcast_to(base, (height, DEPTH)), 0, 1, stride=1, stride_axis=0)
    return jnp.concatenate(split2(taps), axis=0)


def back_kernel(factor, at_ref, cot_ref, beside_ref, one_ref, two_ref, kb_ref, all_ref, halo_ref, grad_ref, sum_ref):
    channels, height, width = cot_ref.shape
    even = at_ref[6] == 0
    one, two = one_ref[...].astype(f32), two_ref[...].astype(f32)
    top = jnp.where(at_ref[2] == 0, jnp.where(even, two, one), 0.0)
    bot = jnp.where(at_ref[3] == 0, jnp.where(even, one, two), 0.0)
    none = jnp.zeros((channels, 4, width), f32)
    for part, middle, ref in ((slice(0, 4), cot_ref, all_ref), (slice(4, 8), beside_ref, halo_ref)):
        ref[:, 0:8, :] = jnp.concatenate([none, top[:, part]], axis=1).astype(bf16)
        ref[:, 8:8 + height, :] = middle[...]
        ref[:, 8 + height:, :] = jnp.concatenate([bot[:, part], none], axis=1).astype(bf16)

    def one(k, carry):
        plane = all_ref[k]
        stack = shifted(plane, halo_ref[k])
        both = mm(toeplitz(kb_ref[pl.ds(k, 1), :], height), stack)
        grad = (both[:height] + both[height:]) * factor
        grad_ref[k] = grad
        own = plane.astype(f32)[8:8 + height]
        sum_ref[0, k] = jnp.sum(grad.reshape(height // 8, 8, width), axis=0)
        sum_ref[1, k] = jnp.sum(own.reshape(height // 8, 8, width), axis=0) * factor
        return carry

    lax.fori_loop(0, channels, one, 0, unroll=UNROLL)


def layer_norm(patch, channels):
    values = patch.astype(bf16).astype(f32).reshape(channels, GROUP, LANES)
    center = values - jnp.mean(values, axis=0, keepdims=True)
    spread = jnp.mean(center * center, axis=0, keepdims=True)
    inverse = lax.rsqrt(spread + norm_eps)
    return center * inverse, inverse


def per_row(vec_ref, n):
    return vec_ref[n][:, None, :]


def order_kernel(at_ref, *refs):
    pair_refs, (x_ref, one_ref, two_ref) = refs[:-3], refs[-3:]
    chips = len(pair_refs)
    core, chip = at_ref[0], at_ref[1]
    for away, ref in enumerate(pair_refs):
        there = lax.rem(chip - away + chips, chips)
        x_ref[2 * there + core] = ref[0]
        x_ref[2 * there + 1 - core] = ref[1]
    half = one_ref.shape[0]
    up = x_ref[:half]
    down = x_ref[2 * chips - half:]
    even = at_ref[6] == 0
    one_ref[...] = jnp.where(even, down, up)
    two_ref[...] = jnp.where(even, up, down)


def main_kernel(colors, file_rows, factor, x_ref, wk_ref, vec_ref, grad_ref, sum_ref, all_ref, halo_ref,
                taps_ref, gather_ref, diagonal_ref, fold_ref, pick_ref,
                norm_ref, out_ref, norm_s, gram_s, diag_s):
    channels, height, width = grad_ref.shape
    block = colors * file_rows
    per = GROUP // file_rows
    rows = channels * GROUP
    bias, gain, offset = per_row(vec_ref, 0), per_row(vec_ref, 1), per_row(vec_ref, 2)
    scale_part = jnp.zeros((channels, GROUP, width), f32)
    ones = jnp.where(iota((16, width), 0) == 0, 1.0, 0.0).astype(bf16)
    for g in range(height // GROUP):
        pixels = jnp.concatenate([x_ref[per * g + a, :block, :] for a in range(per)], axis=0)
        patch = mm(wk_ref[...], pixels).reshape(channels, GROUP, width) + bias
        xhat, inverse = layer_norm(patch, channels)
        norm_s[:, g * GROUP:(g + 1) * GROUP, :] = xhat * gain + offset
        grad = grad_ref[:, g * GROUP:(g + 1) * GROUP, :]
        scale_part += grad * xhat
        inside = grad * gain
        mean_a = jnp.mean(inside, axis=0, keepdims=True)
        mean_b = jnp.mean(inside * xhat, axis=0, keepdims=True)
        patch_grad = (inverse * (inside - mean_a - xhat * mean_b)).astype(bf16).reshape(rows, width)
        gram = mm(jnp.concatenate([pixels, ones], axis=0), patch_grad, NT)
        if g == 0:
            gram_s[...] = gram
        else:
            gram_s[...] += gram

    def one(k, carry):
        plane = norm_s[k].astype(bf16)
        norm_ref[k] = plane
        stack = shifted(all_ref[k], halo_ref[k])
        cross = mm(plane, stack, NT)
        total = cross[:8]
        for a in range(1, height // 8):
            total += pltpu.roll(cross[8 * a:8 * a + 8], DEPTH - 8 * a, 1)
        diag_s[k] = total
        return carry

    lax.fori_loop(0, channels, one, 0, unroll=UNROLL)

    line = diag_s[:, 0, :]
    for b in range(1, 8):
        line += pltpu.roll(diag_s[:, b, :], DEPTH - b, 1)
    line = jnp.concatenate([jnp.zeros((LANES - channels, DEPTH), f32), line * factor], axis=0)
    result = sum(mm(taps_ref[...], part, NT) for part in split2(line))

    gather = gather_ref[...]
    gram = gram_s[...] * diagonal_ref[...].astype(f32)
    by_channel = sum(mm(part, gather) for part in split2(gram))
    result += sum(mm(fold_ref[...], part) for part in split2(by_channel))
    parts = [part.reshape(rows, width) for part in (scale_part, sum_ref[0], sum_ref[1])]
    line = sum(mm(pick_ref[...], piece, NT) for piece in split2(jnp.concatenate(parts, axis=1)))
    result += sum(mm(piece, gather) for piece in split2(line))
    out_ref[...] = result


def stem_halo_kernel(colors, file_rows, at_ref, x_ref, one_ref, two_ref, wk_ref, wh_ref, vec_ref, norm_ref,
                     all_s, halo_s):
    channels, height, width = norm_ref.shape
    block = colors * file_rows
    per = GROUP // file_rows
    half = per // 2
    chunks = wh_ref.shape[1] // (per * LANES)
    bias, gain, offset = per_row(vec_ref, 0), per_row(vec_ref, 1), per_row(vec_ref, 2)
    no_top, no_bot = at_ref[2], at_ref[3]
    no_left, no_right = at_ref[4], at_ref[5]
    shape = (channels, GROUP, width)
    lower = iota(shape, 1) < 4
    row_ok = jnp.where(lower, 1 - no_bot, 1 - no_top) > 0

    even = at_ref[6] == 0
    one, two = one_ref[...], two_ref[...]
    top, bot = jnp.where(even, two, one), jnp.where(even, one, two)
    outer = [bot[a] for a in range(half)] + [top[a] for a in range(half)]
    pixels = jnp.concatenate([piece[:block] for piece in outer], axis=0)
    xhat, _ = layer_norm(mm(wk_ref[...], pixels).reshape(shape) + bias, channels)
    rows = jnp.where(row_ok, xhat * gain + offset, 0.0).astype(bf16)
    all_s[:, 0:8, :] = rows
    all_s[:, 8 + height:16 + height, :] = rows
    all_s[:, 8:8 + height, :] = norm_ref[...]

    groups = height // GROUP
    lines = []
    for g in range(groups + 1):
        pieces = []
        for a in range(per):
            piece = outer[a][block:block + 16] if g == groups else x_ref[per * g + a, block:block + 16, :]
            piece = piece.astype(f32)
            pieces += [piece[8 * c:8 * c + 8] for c in range(chunks)]
        lines.append(jnp.concatenate(pieces, axis=1))
    lines.append(jnp.zeros((LANES - 8 * len(lines), per * chunks * LANES), f32))
    lines = jnp.concatenate(lines, axis=0).astype(bf16)
    xhat, _ = layer_norm(mm(wh_ref[...], lines, NT).reshape(shape) + bias, channels)
    lane = iota(shape, 2)
    column = lax.bitwise_and(lane, 7)
    ok = jnp.where(column < 3, 1 - no_left, 1 - no_right) > 0
    ok = ok & (row_ok | (lane < 8 * groups))
    halo = jnp.where(ok, xhat * gain + offset, 0.0).astype(bf16).reshape(channels * GROUP, width)
    for g in range(groups + 1):
        moved = pltpu.roll(halo, width - 8 * g - 3, 1).reshape(shape)
        if g < groups:
            halo_s[:, 8 + 8 * g:16 + 8 * g, :] = moved
        else:
            halo_s[:, 0:8, :] = moved
            halo_s[:, 8 + height:16 + height, :] = moved


def stem_kernel(start, *refs):
    all_ref, halo_ref, kf_ref, vec_ref = refs[:4]
    out_ref, out_s, sem = refs[-3:]
    count, height, _ = out_s.shape

    def one(n, carry):
        k = start + n
        both = mm(toeplitz(kf_ref[pl.ds(k, 1), :], height), shifted(all_ref[k], halo_ref[k]))
        out_s[n] = (both[:height] + both[height:] + vec_ref[3, pl.ds(k, 1), :]).astype(bf16)
        return carry

    lax.fori_loop(0, count, one, 0, unroll=UNROLL)
    copy = pltpu.make_async_copy(out_s, out_ref.at[pl.ds(start, count)], sem)
    copy.start()
    copy.wait()


def last_kernel(colors, x_ref, y_ref, *outs):
    total = x_ref[...] + y_ref[...]
    channels = outs[1].shape[0]
    first = total[:, :channels]
    second = total[:, channels:2 * channels]
    outs[0][...] = first[:colors]
    for n in range(4):
        outs[1 + n][...] = first[colors + n]
    outs[5][...] = second[:outs[5].shape[0]]


def in_vmem(shape, dtype):
    return pltpu.VMEM(shape, dtype)


def kernel_call(body, out_shape, us, *args, loose=(), **kw):
    loose = tuple(loose) + tuple(kw.get("input_output_aliases", {}))
    args = [
        arg if n in loose or arg.dtype == jnp.int32 else pltpu.with_memory_space_constraint(arg, pltpu.VMEM)
        for n, arg in enumerate(args)
    ]
    return pl.pallas_call(
        body,
        out_shape=out_shape,
        compiler_params=pltpu.CompilerParams(vmem_limit_bytes=VMEM),
        cost_estimate=pl.CostEstimate(flops=int(us * 1e9), bytes_accessed=int(us * 3e6), transcendentals=0),
        **kw,
    )(*args)


def shaped(shape, dtype):
    return jax.ShapeDtypeStruct(shape, dtype)


def pairing(count, odd):
    return [(i, (i + 1 if (i + odd) % 2 == 0 else i - 1) % count) for i in range(count)]


def swap(parts, axis):
    return [lax.ppermute(part, axis, pairing(lax.axis_size(axis), n)) for n, part in enumerate(parts)]


def per_device(
    file_pixels,
    patchify_weight,
    patchify_bias,
    norm_gain,
    norm_offset_vector,
    kernel,
    kernel_offset,
    cotangent,
):
    colors, file_rows, _ = file_pixels.shape
    channels, height, width = cotangent.shape
    n_rows, n_cols = lax.axis_size("rows"), lax.axis_size("cols")
    factor = 1.0 / math.sqrt(height * n_rows * width * n_cols)
    block = colors * file_rows
    per = GROUP // file_rows
    block_rows = block + 16
    padded = cdiv(block, LANES) * LANES
    rows = channels * GROUP
    tile = (channels, height, width)
    tall = (channels, PITCH, width)
    const = constants(colors, file_rows, channels)

    row_at, col_at = lax.axis_index("rows"), lax.axis_index("cols")
    chips = n_cols // 2
    at = jnp.stack([
        col_at % 2, col_at // 2, row_at == 0, row_at == n_rows - 1, col_at == 0, col_at == n_cols - 1, row_at % 2,
    ]).astype(jnp.int32)
    smem = pl.BlockSpec(memory_space=pltpu.SMEM)
    vmem = pl.BlockSpec(memory_space=pltpu.VMEM)
    edge_rows = channels * height // 16

    beyond = pl.BlockSpec(memory_space=pl.ANY)
    cot, keep, give, edges = kernel_call(
        pack_kernel,
        (
            in_vmem(tile, bf16),
            in_vmem((chips, block_rows, LANES), bf16),
            in_vmem((chips * block_rows + edge_rows, LANES), bf16),
            in_vmem((edge_rows, LANES), bf16),
        ),
        2,
        at, *(pltpu.with_memory_space_constraint(arg, pltpu.HBM) for arg in (file_pixels, cotangent)),
        loose=(1, 2),
        in_specs=[smem] + [beyond] * 2,
        scratch_shapes=[
            pltpu.VMEM((n_cols + 2, 16, block), f32),
            pltpu.VMEM(file_pixels.shape, bf16),
            pltpu.SemaphoreType.DMA((2,)),
        ],
    )
    got = lax.ppermute(give, "cols", [(i, i ^ 1) for i in range(n_cols)])
    far = lax.ppermute(edges, "cols", pairing(n_cols, 1))
    pairs = kernel_call(pair_kernel, (in_vmem((2, block_rows, LANES), bf16),) * chips, 0.5, keep, got)
    pairs = [pairs[0]] + [
        lax.ppermute(pairs[n], "cols", [(i, (i + 2 * n) % n_cols) for i in range(n_cols)])
        for n in range(1, chips)
    ]

    kept, far = lax.optimization_barrier((pairs[0], far))
    pairs[0] = kept
    beside, *strips = kernel_call(
        strips_kernel,
        (in_vmem(tile, bf16), in_vmem((channels, 8, width), bf16), in_vmem((channels, 8, width), bf16)),
        1,
        at, cot, got, far,
        in_specs=[smem] + [vmem] * 3,
    )
    beside, taps = lax.optimization_barrier((beside, kernel))
    strips = swap(strips, "rows")
    wk, wh, kb, kf, vec = kernel_call(
        params_kernel,
        (
            in_vmem((rows, per * block), bf16),
            in_vmem((rows, per * padded), bf16),
            in_vmem((channels, DEPTH), f32),
            in_vmem((channels, DEPTH), f32),
            in_vmem((4, channels, LANES), f32),
        ),
        1.5,
        patchify_weight.T, taps.T, patchify_bias, norm_gain, norm_offset_vector, kernel_offset,
        const["spread"], const["keep"], const["spread_halo"], const["keep_halo"], const["tall"],
        const["forward"], const["backward"],
    )
    cot_all, cot_halo, grad, sums = kernel_call(
        functools.partial(back_kernel, factor),
        (in_vmem(tall, bf16), in_vmem(tall, bf16), in_vmem(tile, f32), in_vmem((2, channels, GROUP, width), f32)),
        5,
        at, cot, beside, *strips, kb,
        in_specs=[smem] + [vmem] * 5,
    )

    half = per // 2
    pixels, *ends = kernel_call(
        order_kernel,
        (in_vmem((n_cols, block_rows, LANES), bf16),) + (in_vmem((half, block_rows, LANES), bf16),) * 2,
        0.5,
        at, *pairs,
        in_specs=[smem] + [vmem] * chips,
    )
    ends = swap(ends, "rows")
    norm, result = kernel_call(
        functools.partial(main_kernel, colors, file_rows, factor),
        (in_vmem(tile, bf16), in_vmem((56, LANES), f32)),
        6,
        pixels, wk, vec, grad, sums, cot_all, cot_halo,
        const["taps"], const["gather"], const["diagonal"], const["fold"], const["pick"],
        scratch_shapes=[
            pltpu.VMEM(tile, f32),
            pltpu.VMEM((per * block + 16, rows), f32),
            pltpu.VMEM((channels, 8, DEPTH), f32),
        ],
    )

    size = n_rows * n_cols
    chunk = channels // 4
    jobs = ["halo"] + list(range(0, channels, chunk))
    stem_output = None
    rounds = (size - 1).bit_length()
    for n in range(rounds):
        step = 1 if n == 0 else (1 << n) + 1
        other = lax.ppermute(result, ("rows", "cols"), [(i, i ^ step) for i in range(size)])
        final = n == rounds - 1
        if n > 0:
            for job in jobs if final else jobs[:1]:
                if job == "halo":
                    result, norm = lax.optimization_barrier((result, norm))
                    norm_all, norm_halo = kernel_call(
                        functools.partial(stem_halo_kernel, colors, file_rows),
                        (in_vmem(tall, bf16), in_vmem(tall, bf16)),
                        2,
                        at, pixels, *ends, wk, wh, vec, norm,
                        in_specs=[smem] + [vmem] * 7,
                    )
                    result, norm_all = lax.optimization_barrier((result, norm_all))
                else:
                    result, norm_all = lax.optimization_barrier((result, norm_all))
                    before = () if stem_output is None else (stem_output,)
                    stem_output = kernel_call(
                        functools.partial(stem_kernel, job),
                        shaped(tile, bf16),
                        1.5,
                        norm_all, norm_halo, kf, vec, *before,
                        in_specs=[vmem] * 4 + [beyond] * len(before),
                        out_specs=beyond,
                        input_output_aliases={4: 0} if before else {},
                        scratch_shapes=[pltpu.VMEM((chunk, height, width), bf16), pltpu.SemaphoreType.DMA],
                    )
                    result, stem_output = lax.optimization_barrier((result, stem_output))
            jobs = [] if final else jobs[1:]
        if not final:
            result = result + other

    taps = side * side
    outs = kernel_call(
        functools.partial(last_kernel, colors),
        (shaped((colors, channels), f32),) + (shaped((channels,), f32),) * 4 + (shaped((taps, channels), f32),),
        1,
        result, other,
    )
    return (stem_output, outs[0].T, outs[1], outs[2], outs[3], outs[5].T, outs[4])


def solution(mesh):
    return jax.shard_map(
        per_device,
        mesh=mesh,
        in_specs=(
            P(None, ("rows", "cols"), None),
            P(),
            P(),
            P(),
            P(),
            P(),
            P(),
            P(None, "rows", "cols"),
        ),
        out_specs=(P(None, "rows", "cols"), P(), P(), P(), P(), P(), P()),
        check_vma=False,
    )
```

```python
import functools
import math

import jax
import jax.numpy as jnp
import numpy as np
from jax import lax
from jax.experimental import pallas as pl
from jax.experimental.pallas import tpu as pltpu
from jax.sharding import PartitionSpec as P

norm_eps = 1e-06
side = 7
LANES = 128
GROUP = 8
PITCH = 48
DEPTH = 8 * PITCH
VMEM = 20 * 1024 * 1024
UNROLL = 32
bf16, f32 = jnp.bfloat16, jnp.float32

NN = (((1,), (0,)), ((), ()))
NT = (((1,), (1,)), ((), ()))
TN = (((0,), (0,)), ((), ()))


def mm(a, b, dims=NN):
    return lax.dot_general(a, b, dims, preferred_element_type=f32)


def iota(shape, axis):
    return lax.broadcasted_iota(jnp.int32, shape, axis)


def split2(x):
    high = x.astype(bf16)
    return high, (x - high.astype(f32)).astype(bf16)


def one_hot(cond):
    return jnp.where(cond, 1.0, 0.0).astype(bf16)


def cdiv(a, b):
    return -(-a // b)


def constants(colors, file_rows, channels):
    block = colors * file_rows
    per = GROUP // file_rows
    rows = channels * GROUP
    out = {}
    for name, width in (("", block), ("_halo", cdiv(block, LANES) * LANES)):
        at = np.arange(per * width)
        part, inside = at // width, at % width
        ok = inside < block
        color = np.where(ok, inside % colors, -1)
        row = np.where(ok, part * file_rows + inside // colors, -1)
        out["spread" + name] = color[None, :] == np.arange(colors)[:, None]
        out["keep" + name] = row[None, :] == (np.arange(rows) % GROUP)[:, None]
    out["tall"] = (np.arange(rows) // GROUP)[:, None] == np.arange(channels)[None, :]
    lane = np.arange(DEPTH)
    copy, at = lane // PITCH, lane % PITCH - 5
    tap = np.where((at >= 0) & (at < side) & (copy < side), at * side + copy, -1)
    count = side * side
    out["forward"] = tap[None, :] == np.arange(count)[:, None]
    out["backward"] = (tap >= 0)[None, :] & (count - 1 - tap[None, :] == np.arange(count)[:, None])
    out["taps"] = np.concatenate([out["backward"], np.zeros((56 - count, DEPTH), bool)])
    pick = np.zeros((3, 56, LANES), bool)
    for n in range(3):
        pick[n, colors + 1 + n] = True
    out["pick"] = np.concatenate(list(pick), axis=1)
    return {k: jnp.asarray(v, f32 if k in ("forward", "backward") else bf16) for k, v in out.items()}


def params_kernel(wt_ref, taps_ref, bias_ref, gain_ref, off_ref, koff_ref, spread_ref, keep_ref, spread_h_ref,
                  keep_h_ref, tall_ref, forward_ref, backward_ref, wk_ref, wh_ref, kb_ref, kf_ref, vec_ref):
    channels = wt_ref.shape[1]
    for spread, keep, out_ref in ((spread_ref, keep_ref, wk_ref), (spread_h_ref, keep_h_ref, wh_ref)):
        wide = mm(wt_ref[...], spread[...], TN).astype(bf16)
        out_ref[...] = mm(tall_ref[...], wide).astype(bf16) * keep[...]
    for place, out_ref in ((forward_ref, kf_ref), (backward_ref, kb_ref)):
        out_ref[...] = lax.dot_general(taps_ref[...], place[...], TN, precision=lax.Precision.HIGHEST,
                                       preferred_element_type=f32)
    eye = iota((channels, channels), 0) == iota((channels, channels), 1)
    for n, ref in enumerate((bias_ref, gain_ref, off_ref, koff_ref)):
        row = jnp.broadcast_to(ref[...].reshape(1, channels), (channels, channels))
        column = jnp.sum(jnp.where(eye, row, 0.0), axis=1, keepdims=True)
        vec_ref[n] = jnp.broadcast_to(column, (channels, LANES))


def pack_kernel(at_ref, x_hbm, cot_hbm, cot_ref, keep_ref, give_ref, edge_ref, edge_s, x_ref, y_ref, sems):
    colors, file_rows, width = x_ref.shape
    channels, height, _ = cot_ref.shape
    chips, block_rows, _ = keep_ref.shape
    count = width // LANES
    block = colors * file_rows
    core, chip = at_ref[0, 0], at_ref[1, 0]
    load_x = pltpu.make_async_copy(x_hbm, x_ref, sems.at[0])
    load_cot = pltpu.make_async_copy(cot_hbm, cot_ref, sems.at[1])
    load_x.start()
    load_cot.start()
    load_cot.wait()

    row, lane = iota((8, LANES), 0), iota((8, LANES), 1)
    pick = one_hot(((row < 3) & (lane == row)) | ((row >= 3) & (row < 6) & (lane == row + LANES - 6)))
    edges = mm(pick, cot_ref[...].reshape(channels * height, LANES), NT)
    edges = jnp.concatenate(
        [edges[:, n:n + LANES] for n in range(0, channels * height, LANES)], axis=0).astype(bf16)
    edge_ref[:edges.shape[0]] = edges
    edge_ref[edges.shape[0]:] = edges[:edge_ref.shape[0] - edges.shape[0]]
    give_ref[chips * block_rows:, :] = edges

    row, src = iota((block, block), 0), iota((block, block), 1)
    part = sum((row >= colors * n).astype(jnp.int32) for n in range(1, file_rows)) if file_rows > 1 else 0
    move = one_hot(src == (row - colors * part) * file_rows + part)
    load_x.wait()
    y_ref[...] = mm(move, x_ref[...].reshape(block, width)).astype(bf16)

    row, lane = iota((16, LANES), 0), iota((16, LANES), 1)
    pick = one_hot(((row < 3) & (lane == row + LANES - 3)) | ((row >= 11) & (row < 14) & (lane == row - 11)))
    zeros = jnp.zeros((16, block), f32)
    edge_s[0] = zeros
    edge_s[count + 1] = zeros
    for d in range(count):
        tile = y_ref[:, d * LANES:(d + 1) * LANES]
        edge_s[d + 1] = mm(pick, tile, NT)

    def halo(d):
        both = edge_s[d][:8] + edge_s[d + 2][8:]
        chunks = []
        for start in range(0, 2 * LANES, LANES):
            stop = min(start + LANES, block)
            if stop <= start:
                chunks.append(jnp.zeros((8, LANES), f32))
            elif stop - start < LANES:
                chunks.append(jnp.concatenate(
                    [both[:, start:stop], jnp.zeros((8, LANES - stop + start), f32)], axis=1))
            else:
                chunks.append(both[:, start:stop])
        return jnp.concatenate(chunks, axis=0).astype(bf16)

    for away in range(chips):
        there = lax.rem(chip + away, chips)
        for other in range(2):
            d = 2 * there + (core if other == 0 else 1 - core)
            tile = y_ref[:, pl.ds(pl.multiple_of(d * LANES, LANES), LANES)]
            if other == 0:
                keep_ref[away, :block, :] = tile
                keep_ref[away, block:, :] = halo(d)
            else:
                start = away * block_rows
                give_ref[start:start + block, :] = tile
                give_ref[start + block:start + block_rows, :] = halo(d)


def pair_kernel(keep_ref, got_ref, *pair_refs):
    _, block_rows, _ = keep_ref.shape
    for away, ref in enumerate(pair_refs):
        ref[0] = keep_ref[away]
        ref[1] = got_ref[away * block_rows:(away + 1) * block_rows, :]


def strips_kernel(at_ref, cot_ref, near_ref, far_ref, halo_ref, one_ref, two_ref):
    channels, height, width = cot_ref.shape
    size = channels * height // 16
    core = at_ref[0, 0]
    near = near_ref[near_ref.shape[0] - size:, :].astype(f32)
    far = far_ref[:size, :].astype(f32)
    left = jnp.where(core == 0, far, near)
    right = jnp.where(core == 0, near, far)
    left = jnp.concatenate([left[n:n + 8] for n in range(0, size, 8)], axis=1).astype(bf16)
    right = jnp.concatenate([right[n:n + 8] for n in range(0, size, 8)], axis=1).astype(bf16)
    row, lane = iota((8, width), 0), iota((8, width), 1)
    from_left = one_hot((row >= 3) & (row < 6) & (lane == row + width - 6) & (at_ref[4, 0] == 0))
    from_right = one_hot((row < 3) & (lane == row) & (at_ref[5, 0] == 0))
    halo = (mm(left, from_left, TN) + mm(right, from_right, TN)).reshape(channels, height, width)
    halo_ref[...] = halo.astype(bf16)
    own = cot_ref[...].astype(f32)
    pick = one_hot((lane == row + width - 3) & (row < 3) | (lane == row - 3) & (row >= 3) & (row < 6))
    up, down = own[:, :4], own[:, height - 4:]
    up_halo, down_halo = halo[:, :4], halo[:, height - 4:]
    even = at_ref[6, 0] == 0
    for ref, rows, beside in (
        (one_ref, jnp.where(even, down, up), jnp.where(even, down_halo, up_halo)),
        (two_ref, jnp.where(even, up, down), jnp.where(even, up_halo, down_halo)),
    ):
        ref[:channels] = rows.astype(bf16)
        dense = mm(pick, beside.reshape(channels * 4, width).astype(bf16), NT)
        for n in range(0, channels * 4, LANES):
            for q in range(2):
                ref[channels + n // 64 + q] = dense[4 * q:4 * q + 4, n:n + LANES].astype(bf16)


def shifted(center, halo):
    rows, width = center.shape
    lane = iota((rows, width), 1)
    copies = []
    for move in range(-3, 4):
        if move == 0:
            copies.append(center)
        elif move > 0:
            copies.append(pltpu.roll(jnp.where(lane < move, halo, center), width - move, 1))
        else:
            copies.append(pltpu.roll(jnp.where(lane >= width + move, halo, center), -move, 1))
    copies.append(jnp.zeros((rows, width), center.dtype))
    return jnp.concatenate(copies, axis=0)


def toeplitz(base, height):
    taps = pltpu.roll(jnp.broadcast_to(base, (height, DEPTH)), 0, 1, stride=1, stride_axis=0)
    return jnp.concatenate(split2(taps), axis=0)


def back_kernel(factor, at_ref, cot_ref, beside_ref, one_ref, two_ref, kb_ref,
                flip_ref, grad_ref, total_ref, all_ref, halo_ref, sum_ref):
    channels, height, width = cot_ref.shape
    even = at_ref[6, 0] == 0
    one, two = one_ref[...].astype(f32), two_ref[...].astype(f32)
    top = jnp.where(at_ref[2, 0] == 0, jnp.where(even, two, one), 0.0)
    bot = jnp.where(at_ref[3, 0] == 0, jnp.where(even, one, two), 0.0)
    row, lane = iota((8, width), 0), iota((8, width), 1)
    place = one_hot((lane == row + width - 3) & (row < 3) | (lane == row - 3) & (row >= 3) & (row < 6))

    def beside(part):
        dense = jnp.concatenate(
            [
                jnp.concatenate([part[channels + n // 64 + q] for q in range(2)], axis=0)
                for n in range(0, channels * 4, LANES)
            ],
            axis=1,
        )
        return mm(dense.astype(bf16), place, TN).reshape(channels, 4, width)

    none = jnp.zeros((channels, 4, width), f32)
    for above, middle, below, ref in (
        (top[:channels], cot_ref, bot[:channels], all_ref),
        (beside(top), beside_ref, beside(bot), halo_ref),
    ):
        ref[:, 0:8, :] = jnp.concatenate([none, above], axis=1).astype(bf16)
        ref[:, 8:8 + height, :] = middle[...]
        ref[:, 8 + height:, :] = jnp.concatenate([below, none], axis=1).astype(bf16)

    eye = one_hot(iota((width, width), 0) == iota((width, width), 1))

    def one(k, carry):
        plane = all_ref[k]
        stack = shifted(plane, halo_ref[k])
        flip_ref[k] = mm(eye, stack, NT).astype(bf16)
        both = mm(toeplitz(kb_ref[pl.ds(k, 1), :], height), stack)
        grad = (both[:height] + both[height:]) * factor
        grad_ref[k] = grad
        own = plane.astype(f32)[8:8 + height]
        sum_ref[0, k] = jnp.sum(grad.reshape(height // 8, 8, width), axis=0)
        sum_ref[1, k] = jnp.sum(own.reshape(height // 8, 8, width), axis=0) * factor
        return carry

    lax.fori_loop(0, channels, one, 0, unroll=UNROLL)
    for n in range(2):
        total_ref[n] = sum(sum_ref[n, :, b, :] for b in range(8))


def layer_norm(patch, channels):
    values = patch.astype(bf16).astype(f32).reshape(channels, GROUP, LANES)
    center = values - jnp.mean(values, axis=0, keepdims=True)
    spread = jnp.mean(center * center, axis=0, keepdims=True)
    inverse = lax.rsqrt(spread + norm_eps)
    return center * inverse, inverse


def per_row(vec_ref, n):
    return vec_ref[n][:, None, :]


def order_kernel(at_ref, *refs):
    pair_refs, (x_ref, one_ref, two_ref) = refs[:-3], refs[-3:]
    chips = len(pair_refs)
    core, chip = at_ref[0, 0], at_ref[1, 0]
    for away, ref in enumerate(pair_refs):
        there = lax.rem(chip - away + chips, chips)
        x_ref[2 * there + core] = ref[0]
        x_ref[2 * there + 1 - core] = ref[1]
    half = one_ref.shape[0]
    up = x_ref[:half]
    down = x_ref[2 * chips - half:]
    even = at_ref[6, 0] == 0
    one_ref[...] = jnp.where(even, down, up)
    two_ref[...] = jnp.where(even, up, down)


def main_kernel(colors, file_rows, factor, x_ref, wk_ref, vec_ref, grad_ref, total_ref, flip_ref, taps_ref, pick_ref,
                norm_ref, out_ref, norm_s, grad_s, diag_s):
    channels, height, width = grad_ref.shape
    block = colors * file_rows
    per = GROUP // file_rows
    rows = channels * GROUP
    bias, gain, offset = per_row(vec_ref, 0), per_row(vec_ref, 1), per_row(vec_ref, 2)
    scale_part = jnp.zeros((channels, GROUP, width), f32)
    ones = jnp.where(iota((16, width), 0) == 0, 1.0, 0.0).astype(bf16)
    by_color = jnp.zeros((colors + 16, channels), f32)
    for g in range(height // GROUP):
        blocks = [x_ref[per * g + a, :block, :] for a in range(per)]
        patch = mm(wk_ref[...], jnp.concatenate(blocks, axis=0)).reshape(channels, GROUP, width) + bias
        xhat, inverse = layer_norm(patch, channels)
        norm_s[:, g * GROUP:(g + 1) * GROUP, :] = xhat * gain + offset
        grad = grad_ref[:, g * GROUP:(g + 1) * GROUP, :]
        scale_part += grad * xhat
        inside = grad * gain
        mean_a = jnp.mean(inside, axis=0, keepdims=True)
        mean_b = jnp.mean(inside * xhat, axis=0, keepdims=True)
        grad_s[g] = (inverse * (inside - mean_a - xhat * mean_b)).reshape(rows, width)
        left, right = [], []
        for h in range(GROUP):
            start = h % file_rows * colors
            left.append(jnp.concatenate([blocks[h // file_rows][start:start + colors], ones], axis=0))
            right.append(grad_s[g, pl.ds(h, channels, stride=GROUP), :].astype(bf16))
        by_color += mm(jnp.concatenate(left, axis=1), jnp.concatenate(right, axis=1), NT)

    def one(k, carry):
        plane = norm_s[k].astype(bf16)
        norm_ref[k] = plane
        cross = mm(plane, flip_ref[k])
        total = cross[:8]
        for a in range(1, height // 8):
            total += pltpu.roll(cross[8 * a:8 * a + 8], DEPTH - 8 * a, 1)
        diag_s[k] = total
        return carry

    lax.fori_loop(0, channels, one, 0, unroll=UNROLL)

    line = diag_s[:, 0, :]
    for b in range(1, 8):
        line += pltpu.roll(diag_s[:, b, :], DEPTH - b, 1)
    line = jnp.concatenate([jnp.zeros((LANES - channels, DEPTH), f32), line * factor], axis=0)
    out_ref[...] = sum(mm(taps_ref[...], part, NT) for part in split2(line))
    parts = jnp.concatenate([jnp.sum(scale_part, axis=1), total_ref[0], total_ref[1]], axis=1)
    first = sum(mm(pick_ref[...], part, NT) for part in split2(parts))
    out_ref[:, :channels] = first + by_color[:56]


def stem_halo_kernel(colors, file_rows, at_ref, x_ref, one_ref, two_ref, wk_ref, wh_ref, vec_ref, norm_ref,
                     all_s, halo_s):
    channels, height, width = norm_ref.shape
    block = colors * file_rows
    per = GROUP // file_rows
    half = per // 2
    chunks = wh_ref.shape[1] // (per * LANES)
    bias, gain, offset = per_row(vec_ref, 0), per_row(vec_ref, 1), per_row(vec_ref, 2)
    no_top, no_bot = at_ref[2, 0], at_ref[3, 0]
    no_left, no_right = at_ref[4, 0], at_ref[5, 0]
    shape = (channels, GROUP, width)
    lower = iota(shape, 1) < 4
    row_ok = jnp.where(lower, 1 - no_bot, 1 - no_top) > 0

    even = at_ref[6, 0] == 0
    one, two = one_ref[...], two_ref[...]
    top, bot = jnp.where(even, two, one), jnp.where(even, one, two)
    outer = [bot[a] for a in range(half)] + [top[a] for a in range(half)]
    pixels = jnp.concatenate([piece[:block] for piece in outer], axis=0)
    xhat, _ = layer_norm(mm(wk_ref[...], pixels).reshape(shape) + bias, channels)
    rows = jnp.where(row_ok, xhat * gain + offset, 0.0).astype(bf16)
    all_s[:, 0:8, :] = rows
    all_s[:, 8 + height:16 + height, :] = rows
    all_s[:, 8:8 + height, :] = norm_ref[...]

    groups = height // GROUP
    lines = []
    for g in range(groups + 1):
        pieces = []
        for a in range(per):
            piece = outer[a][block:block + 16] if g == groups else x_ref[per * g + a, block:block + 16, :]
            piece = piece.astype(f32)
            pieces += [piece[8 * c:8 * c + 8] for c in range(chunks)]
        lines.append(jnp.concatenate(pieces, axis=1))
    lines.append(jnp.zeros((LANES - 8 * len(lines), per * chunks * LANES), f32))
    lines = jnp.concatenate(lines, axis=0).astype(bf16)
    xhat, _ = layer_norm(mm(wh_ref[...], lines, NT).reshape(shape) + bias, channels)
    lane = iota(shape, 2)
    column = lax.bitwise_and(lane, 7)
    ok = jnp.where(column < 3, 1 - no_left, 1 - no_right) > 0
    ok = ok & (row_ok | (lane < 8 * groups))
    halo = jnp.where(ok, xhat * gain + offset, 0.0).astype(bf16).reshape(channels * GROUP, width)
    for g in range(groups + 1):
        moved = pltpu.roll(halo, width - 8 * g - 3, 1).reshape(shape)
        if g < groups:
            halo_s[:, 8 + 8 * g:16 + 8 * g, :] = moved
        else:
            halo_s[:, 0:8, :] = moved
            halo_s[:, 8 + height:16 + height, :] = moved


def stem_kernel(start, *refs):
    all_ref, halo_ref, kf_ref, vec_ref = refs[:4]
    out_ref, out_s, sem = refs[-3:]
    count, height, _ = out_s.shape

    def one(n, carry):
        k = start + n
        both = mm(toeplitz(kf_ref[pl.ds(k, 1), :], height), shifted(all_ref[k], halo_ref[k]))
        out_s[n] = (both[:height] + both[height:] + vec_ref[3, pl.ds(k, 1), :]).astype(bf16)
        return carry

    lax.fori_loop(0, count, one, 0, unroll=UNROLL)
    copy = pltpu.make_async_copy(out_s, out_ref.at[pl.ds(start, count)], sem)
    copy.start()
    copy.wait()


def last_kernel(colors, x_ref, y_ref, *outs):
    total = x_ref[...] + y_ref[...]
    channels = outs[1].shape[0]
    first = total[:, :channels]
    second = total[:, channels:2 * channels]
    outs[0][...] = first[:colors]
    for n in range(4):
        outs[1 + n][...] = first[colors + n]
    outs[5][...] = second[:outs[5].shape[0]]


def in_vmem(shape, dtype):
    return pltpu.VMEM(shape, dtype)


def kernel_call(body, out_shape, us, *args, loose=(), **kw):
    loose = tuple(loose) + tuple(kw.get("input_output_aliases", {}))
    args = [
        arg if n in loose else pltpu.with_memory_space_constraint(arg, pltpu.VMEM)
        for n, arg in enumerate(args)
    ]
    return pl.pallas_call(
        body,
        out_shape=out_shape,
        compiler_params=pltpu.CompilerParams(vmem_limit_bytes=VMEM),
        cost_estimate=pl.CostEstimate(flops=int(us * 1e9), bytes_accessed=int(us * 3e6), transcendentals=0),
        **kw,
    )(*args)


def shaped(shape, dtype):
    return jax.ShapeDtypeStruct(shape, dtype)


def pairing(count, odd):
    return [(i, (i + 1 if (i + odd) % 2 == 0 else i - 1) % count) for i in range(count)]


def swap(parts, axis):
    return [lax.ppermute(part, axis, pairing(lax.axis_size(axis), n)) for n, part in enumerate(parts)]


def per_device(
    file_pixels,
    patchify_weight,
    patchify_bias,
    norm_gain,
    norm_offset_vector,
    kernel,
    kernel_offset,
    cotangent,
):
    colors, file_rows, _ = file_pixels.shape
    channels, height, width = cotangent.shape
    n_rows, n_cols = lax.axis_size("rows"), lax.axis_size("cols")
    factor = 1.0 / math.sqrt(height * n_rows * width * n_cols)
    block = colors * file_rows
    per = GROUP // file_rows
    block_rows = block + 16
    padded = cdiv(block, LANES) * LANES
    rows = channels * GROUP
    tile = (channels, height, width)
    tall = (channels, PITCH, width)
    const = constants(colors, file_rows, channels)

    row_at, col_at = lax.axis_index("rows"), lax.axis_index("cols")
    chips = n_cols // 2
    at = jnp.stack([
        col_at % 2, col_at // 2, row_at == 0, row_at == n_rows - 1, col_at == 0, col_at == n_cols - 1, row_at % 2, 0,
    ]).astype(jnp.int32)
    at = jnp.broadcast_to(at[:, None], (8, LANES))
    vmem = pl.BlockSpec(memory_space=pltpu.VMEM)
    edge_rows = channels * height // 16

    beyond = pl.BlockSpec(memory_space=pl.ANY)
    cot, keep, give, edges = kernel_call(
        pack_kernel,
        (
            in_vmem(tile, bf16),
            in_vmem((chips, block_rows, LANES), bf16),
            in_vmem((chips * block_rows + edge_rows, LANES), bf16),
            in_vmem((edge_rows + 48, LANES), bf16),
        ),
        2,
        at, *(pltpu.with_memory_space_constraint(arg, pltpu.HBM) for arg in (file_pixels, cotangent)),
        loose=(1, 2),
        in_specs=[vmem] + [beyond] * 2,
        scratch_shapes=[
            pltpu.VMEM((n_cols + 2, 16, block), f32),
            pltpu.VMEM(file_pixels.shape, bf16),
            pltpu.VMEM((block, n_cols * LANES), bf16),
            pltpu.SemaphoreType.DMA((2,)),
        ],
    )
    got = lax.ppermute(give, "cols", [(i, i ^ 1) for i in range(n_cols)])
    far = lax.ppermute(edges, "cols", pairing(n_cols, 1))
    pairs = kernel_call(pair_kernel, (in_vmem((2, block_rows, LANES), bf16),) * chips, 0.5, keep, got)
    pairs = [pairs[0]] + [
        lax.ppermute(pairs[n], "cols", [(i, (i + 2 * n) % n_cols) for i in range(n_cols)])
        for n in range(1, chips)
    ]

    kept, far = lax.optimization_barrier((pairs[0], far))
    pairs[0] = kept
    beside, *strips = kernel_call(
        strips_kernel,
        (in_vmem(tile, bf16), in_vmem((channels + channels // 16, 4, width), bf16), in_vmem((channels + channels // 16, 4, width), bf16)),
        0.01,
        at, cot, got, far,
        in_specs=[vmem] + [vmem] * 3,
    )
    beside, taps = lax.optimization_barrier((beside, kernel))
    strips = swap(strips, "rows")
    wk, wh, kb, kf, vec = kernel_call(
        params_kernel,
        (
            in_vmem((rows, per * block), bf16),
            in_vmem((rows, per * padded), bf16),
            in_vmem((channels, DEPTH), f32),
            in_vmem((channels, DEPTH), f32),
            in_vmem((4, channels, LANES), f32),
        ),
        0.01,
        patchify_weight.T, taps.T, patchify_bias, norm_gain, norm_offset_vector, kernel_offset,
        const["spread"], const["keep"], const["spread_halo"], const["keep_halo"], const["tall"],
        const["forward"], const["backward"],
    )
    flipped, grad, totals = kernel_call(
        functools.partial(back_kernel, factor),
        (in_vmem((channels, width, DEPTH), bf16), in_vmem(tile, f32), in_vmem((2, channels, width), f32)),
        0.01,
        at, cot, beside, *strips, kb,
        scratch_shapes=[
            pltpu.VMEM(tall, bf16),
            pltpu.VMEM(tall, bf16),
            pltpu.VMEM((2, channels, GROUP, width), f32),
        ],
    )

    half = per // 2
    grad, *pairs = lax.optimization_barrier((grad, *pairs))
    pixels, *ends = kernel_call(
        order_kernel,
        (in_vmem((n_cols, block_rows, LANES), bf16),) + (in_vmem((half, block_rows, LANES), bf16),) * 2,
        0.01,
        at, *pairs,
        in_specs=[vmem] + [vmem] * chips,
    )
    norm, result = kernel_call(
        functools.partial(main_kernel, colors, file_rows, factor),
        (in_vmem(tile, bf16), in_vmem((56, LANES), f32)),
        6,
        pixels, wk, vec, grad, totals, flipped, const["taps"], const["pick"],
        scratch_shapes=[
            pltpu.VMEM(tile, f32),
            pltpu.VMEM((height // GROUP, rows, width), f32),
            pltpu.VMEM((channels, 8, DEPTH), f32),
        ],
    )

    size = n_rows * n_cols
    chunk = channels // 2
    rounds = (size - 1).bit_length()
    jobs = {0: ["one"], 1: ["two"], 2: ["halo"], 3: [0], rounds - 1: [chunk]}
    stem_output = None
    for n in range(rounds):
        step = 1 if n == 0 else (1 << n) + 1
        other = lax.ppermute(result, ("rows", "cols"), [(i, i ^ step) for i in range(size)])
        for job in jobs.get(n, []):
            if job in ("one", "two"):
                which = ("one", "two").index(job)
                result, end = lax.optimization_barrier((result, ends[which]))
                ends[which] = lax.ppermute(end, "rows", pairing(n_rows, which))
            elif job == "halo":
                result, norm = lax.optimization_barrier((result, norm))
                norm_all, norm_halo = kernel_call(
                    functools.partial(stem_halo_kernel, colors, file_rows),
                    (in_vmem(tall, bf16), in_vmem(tall, bf16)),
                    2,
                    at, pixels, *ends, wk, wh, vec, norm,
                )
            else:
                result, norm_all = lax.optimization_barrier((result, norm_all))
                before = () if stem_output is None else (stem_output,)
                stem_output = kernel_call(
                    functools.partial(stem_kernel, job),
                    shaped(tile, bf16),
                    1.5,
                    norm_all, norm_halo, kf, vec, *before,
                    in_specs=[vmem] * 4 + [beyond] * len(before),
                    out_specs=beyond,
                    input_output_aliases={4: 0} if before else {},
                    scratch_shapes=[pltpu.VMEM((chunk, height, width), bf16), pltpu.SemaphoreType.DMA],
                )
                result, stem_output = lax.optimization_barrier((result, stem_output))
        if n < rounds - 1:
            result = result + other

    taps = side * side
    outs = kernel_call(
        functools.partial(last_kernel, colors),
        (shaped((colors, channels), f32),) + (shaped((channels,), f32),) * 4 + (shaped((taps, channels), f32),),
        1,
        result, other,
    )
    return (stem_output, outs[0].T, outs[1], outs[2], outs[3], outs[5].T, outs[4])


def solution(mesh):
    return jax.shard_map(
        per_device,
        mesh=mesh,
        in_specs=(
            P(None, ("rows", "cols"), None),
            P(),
            P(),
            P(),
            P(),
            P(),
            P(),
            P(None, "rows", "cols"),
        ),
        out_specs=(P(None, "rows", "cols"), P(), P(), P(), P(), P(), P()),
        check_vma=False,
    )
```

```python
import functools
import math

import jax
import jax.numpy as jnp
import numpy as np
from jax import lax
from jax.experimental import pallas as pl
from jax.experimental.pallas import tpu as pltpu
from jax.sharding import PartitionSpec as P

norm_eps = 1e-06
side = 7
LANES = 128
GROUP = 8
OUTER = 8 * 16
VMEM = 20 * 1024 * 1024
UNROLL = 64
bf16, f32 = jnp.bfloat16, jnp.float32

NN = (((1,), (0,)), ((), ()))
NT = (((1,), (1,)), ((), ()))
TN = (((0,), (0,)), ((), ()))


def mm(a, b, dims=NN):
    return lax.dot_general(a, b, dims, preferred_element_type=f32)


def iota(shape, axis):
    return lax.broadcasted_iota(jnp.int32, shape, axis)


def split2(x):
    high = x.astype(bf16)
    return high, (x - high.astype(f32)).astype(bf16)


def one_hot(cond):
    return jnp.where(cond, 1.0, 0.0).astype(bf16)


def cdiv(a, b):
    return -(-a // b)


def constants(colors, file_rows, channels, height):
    block = colors * file_rows
    per = GROUP // file_rows
    rows = channels * GROUP
    out = {}
    for name, width in (("", block), ("_halo", cdiv(block, LANES) * LANES)):
        at = np.arange(per * width)
        part, inside = at // width, at % width
        ok = inside < block
        color = np.where(ok, inside % colors, -1)
        row = np.where(ok, part * file_rows + inside // colors, -1)
        out["spread" + name] = color[None, :] == np.arange(colors)[:, None]
        out["keep" + name] = row[None, :] == (np.arange(rows) % GROUP)[:, None]
    out["tall"] = (np.arange(rows) // GROUP)[:, None] == np.arange(channels)[None, :]
    inner = 8 * height
    count = side * side
    forward = np.zeros((count, inner + 2 * OUTER), bool)
    taps = np.zeros((56, inner + OUTER), bool)
    for tap in range(count):
        down, copy = divmod(tap, side)
        own, above, below = height * copy + down - 3, 16 * copy + down + 5, 16 * copy + down - 3
        forward[tap, own % inner] = True
        forward[tap, inner + above] = True
        forward[tap, inner + OUTER + below % OUTER] = True
        taps[count - 1 - tap, own % inner] = True
        taps[count - 1 - tap, inner + above] = True
    out["forward"], out["backward"], out["taps"] = forward, forward[::-1], taps
    lane, row = np.arange(inner)[None, :], np.arange(height)[:, None]
    out["band"] = (abs(lane % height - row) <= 3) & (lane < height * side)
    lane, row = np.arange(OUTER)[None, :], np.arange(8)[:, None]
    at = lane % 16
    out["fringe"] = np.concatenate([(at < 8) & (at >= row + 5), (at >= 8) & (at <= row + 3)]) & (lane < 16 * side)
    pick = np.zeros((3, 56, LANES), bool)
    for n in range(3):
        pick[n, colors + 1 + n] = True
    out["pick"] = np.concatenate(list(pick), axis=1)
    return {k: jnp.asarray(v, f32 if k in ("forward", "backward", "band", "fringe") else bf16) for k, v in out.items()}


def params_kernel(wt_ref, taps_ref, bias_ref, gain_ref, off_ref, koff_ref, spread_ref, keep_ref, spread_h_ref,
                  keep_h_ref, tall_ref, forward_ref, backward_ref, wk_ref, wh_ref, kb_ref, kf_ref, vec_ref):
    channels = wt_ref.shape[1]
    for spread, keep, out_ref in ((spread_ref, keep_ref, wk_ref), (spread_h_ref, keep_h_ref, wh_ref)):
        wide = mm(wt_ref[...], spread[...], TN).astype(bf16)
        out_ref[...] = mm(tall_ref[...], wide).astype(bf16) * keep[...]
    for place, out_ref in ((forward_ref, kf_ref), (backward_ref, kb_ref)):
        out_ref[...] = lax.dot_general(taps_ref[...], place[...], TN, precision=lax.Precision.HIGHEST,
                                       preferred_element_type=f32)
    eye = iota((channels, channels), 0) == iota((channels, channels), 1)
    for n, ref in enumerate((bias_ref, gain_ref, off_ref, koff_ref)):
        row = jnp.broadcast_to(ref[...].reshape(1, channels), (channels, channels))
        column = jnp.sum(jnp.where(eye, row, 0.0), axis=1, keepdims=True)
        vec_ref[n] = jnp.broadcast_to(column, (channels, LANES))


def pack_kernel(at_ref, x_hbm, cot_hbm, cot_ref, keep_ref, give_ref, edge_ref, edge_s, x_ref, y_ref, sems):
    colors, file_rows, width = x_ref.shape
    channels, height, _ = cot_ref.shape
    chips, block_rows, _ = keep_ref.shape
    count = width // LANES
    block = colors * file_rows
    core, chip = at_ref[0, 0], at_ref[1, 0]
    load_x = pltpu.make_async_copy(x_hbm, x_ref, sems.at[0])
    load_cot = pltpu.make_async_copy(cot_hbm, cot_ref, sems.at[1])
    load_x.start()
    load_cot.start()
    load_cot.wait()

    row, lane = iota((8, LANES), 0), iota((8, LANES), 1)
    pick = one_hot(((row < 3) & (lane == row)) | ((row >= 3) & (row < 6) & (lane == row + LANES - 6)))
    edges = mm(pick, cot_ref[...].reshape(channels * height, LANES), NT)
    edges = jnp.concatenate(
        [edges[:, n:n + LANES] for n in range(0, channels * height, LANES)], axis=0).astype(bf16)
    edge_ref[:edges.shape[0]] = edges
    edge_ref[edges.shape[0]:] = edges[:edge_ref.shape[0] - edges.shape[0]]
    give_ref[chips * block_rows:, :] = edges

    row, src = iota((block, block), 0), iota((block, block), 1)
    part = sum((row >= colors * n).astype(jnp.int32) for n in range(1, file_rows)) if file_rows > 1 else 0
    move = one_hot(src == (row - colors * part) * file_rows + part)
    load_x.wait()
    y_ref[...] = mm(move, x_ref[...].reshape(block, width)).astype(bf16)

    row, lane = iota((16, LANES), 0), iota((16, LANES), 1)
    pick = one_hot(((row < 3) & (lane == row + LANES - 3)) | ((row >= 11) & (row < 14) & (lane == row - 11)))
    zeros = jnp.zeros((16, block), f32)
    edge_s[0] = zeros
    edge_s[count + 1] = zeros
    for d in range(count):
        tile = y_ref[:, d * LANES:(d + 1) * LANES]
        edge_s[d + 1] = mm(pick, tile, NT)

    def halo(d):
        both = edge_s[d][:8] + edge_s[d + 2][8:]
        chunks = []
        for start in range(0, 2 * LANES, LANES):
            stop = min(start + LANES, block)
            if stop <= start:
                chunks.append(jnp.zeros((8, LANES), f32))
            elif stop - start < LANES:
                chunks.append(jnp.concatenate(
                    [both[:, start:stop], jnp.zeros((8, LANES - stop + start), f32)], axis=1))
            else:
                chunks.append(both[:, start:stop])
        return jnp.concatenate(chunks, axis=0).astype(bf16)

    for away in range(chips):
        there = lax.bitwise_xor(chip, away)
        for other in range(2):
            d = 2 * there + (core if (other == 0) == (away == 0) else 1 - core)
            tile = y_ref[:, pl.ds(pl.multiple_of(d * LANES, LANES), LANES)]
            if other == 0:
                keep_ref[away, :block, :] = tile
                keep_ref[away, block:, :] = halo(d)
            else:
                start = away * block_rows
                give_ref[start:start + block, :] = tile
                give_ref[start + block:start + block_rows, :] = halo(d)


def pair_kernel(keep_ref, got_ref, *pair_refs):
    _, block_rows, _ = keep_ref.shape
    for away, ref in enumerate(pair_refs):
        ref[0] = keep_ref[away]
        ref[1] = got_ref[away * block_rows:(away + 1) * block_rows, :]


def strips_kernel(at_ref, cot_ref, near_ref, far_ref, halo_ref, one_ref, two_ref):
    channels, height, width = cot_ref.shape
    size = channels * height // 16
    core = at_ref[0, 0]
    near = near_ref[near_ref.shape[0] - size:, :].astype(f32)
    far = far_ref[:size, :].astype(f32)
    left = jnp.where(core == 0, far, near)
    right = jnp.where(core == 0, near, far)
    left = jnp.concatenate([left[n:n + 8] for n in range(0, size, 8)], axis=1).astype(bf16)
    right = jnp.concatenate([right[n:n + 8] for n in range(0, size, 8)], axis=1).astype(bf16)
    row, lane = iota((8, width), 0), iota((8, width), 1)
    from_left = one_hot((row >= 3) & (row < 6) & (lane == row + width - 6) & (at_ref[4, 0] == 0))
    from_right = one_hot((row < 3) & (lane == row) & (at_ref[5, 0] == 0))
    halo = (mm(left, from_left, TN) + mm(right, from_right, TN)).reshape(channels, height, width)
    halo_ref[...] = halo.astype(bf16)
    own = cot_ref[...].astype(f32)
    pick = one_hot((lane == row + width - 3) & (row < 3) | (lane == row - 3) & (row >= 3) & (row < 6))
    up, down = own[:, :4], own[:, height - 4:]
    up_halo, down_halo = halo[:, :4], halo[:, height - 4:]
    even = at_ref[6, 0] == 0
    for ref, rows, beside in (
        (one_ref, jnp.where(even, down, up), jnp.where(even, down_halo, up_halo)),
        (two_ref, jnp.where(even, up, down), jnp.where(even, up_halo, down_halo)),
    ):
        ref[:channels] = rows.astype(bf16)
        dense = mm(pick, beside.reshape(channels * 4, width).astype(bf16), NT)
        for n in range(0, channels * 4, LANES):
            for q in range(2):
                ref[channels + n // 64 + q] = dense[4 * q:4 * q + 4, n:n + LANES].astype(bf16)


def shifted(center, halo):
    rows, width = center.shape
    lane = iota((rows, width), 1)
    copies = []
    for move in range(-3, 4):
        if move == 0:
            copies.append(center)
        elif move > 0:
            copies.append(pltpu.roll(jnp.where(lane < move, halo, center), width - move, 1))
        else:
            copies.append(pltpu.roll(jnp.where(lane >= width + move, halo, center), -move, 1))
    copies.append(jnp.zeros((rows, width), center.dtype))
    return jnp.concatenate(copies, axis=0)


def toeplitz(base, mask):
    return pltpu.roll(jnp.broadcast_to(base, mask.shape), 0, 1, stride=1, stride_axis=0) * mask


def inner_taps(base_ref, k, band_ref):
    inner = band_ref.shape[1]
    base = base_ref[pl.ds(k, 1), :]
    return jnp.concatenate(split2(toeplitz(base[:, :inner], band_ref[...])), axis=0)


def outer_taps(base_ref, k, inner, fringe_ref):
    base = base_ref[pl.ds(k, 1), :]
    above = toeplitz(base[:, inner:inner + OUTER], fringe_ref[:8])
    below = toeplitz(base[:, inner + OUTER:], fringe_ref[8:])
    return jnp.concatenate(split2(jnp.concatenate([above, below], axis=0)), axis=0)


def back_inner_kernel(factor, cot_ref, beside_ref, kb_ref, band_ref, stack_ref, grad_ref, total_ref, sum_ref):
    channels, height, width = cot_ref.shape

    def one(k, carry):
        plane = cot_ref[k]
        stack = shifted(plane, beside_ref[k])
        stack_ref[k] = stack
        both = mm(inner_taps(kb_ref, k, band_ref), stack)
        grad_ref[k] = (both[:height] + both[height:]) * factor
        sum_ref[k] = jnp.sum(plane.astype(f32).reshape(height // 8, 8, width), axis=0)
        return carry

    lax.fori_loop(0, channels, one, 0, unroll=UNROLL)
    total_ref[...] = sum(sum_ref[:, b, :] for b in range(8)) * factor


def back_outer_kernel(factor, at_ref, one_ref, two_ref, grad_ref, kb_ref, fringe_ref,
                      stack_ref, edge_ref, plane_ref, halo_ref):
    channels, height, width = grad_ref.shape
    even = at_ref[6, 0] == 0
    one, two = one_ref[...].astype(f32), two_ref[...].astype(f32)
    top = jnp.where(at_ref[2, 0] == 0, jnp.where(even, two, one), 0.0)
    bot = jnp.where(at_ref[3, 0] == 0, jnp.where(even, one, two), 0.0)
    row, lane = iota((8, width), 0), iota((8, width), 1)
    place = one_hot((lane == row + width - 3) & (row < 3) | (lane == row - 3) & (row >= 3) & (row < 6))

    def beside(part):
        dense = jnp.concatenate(
            [
                jnp.concatenate([part[channels + n // 64 + q] for q in range(2)], axis=0)
                for n in range(0, channels * 4, LANES)
            ],
            axis=1,
        )
        return mm(dense.astype(bf16), place, TN).reshape(channels, 4, width)

    none = jnp.zeros((channels, 4, width), f32)
    plane_ref[...] = jnp.concatenate([none, top[:channels], bot[:channels], none], axis=1).astype(bf16)
    halo_ref[...] = jnp.concatenate([none, beside(top), beside(bot), none], axis=1).astype(bf16)

    def one(k, carry):
        stack = shifted(plane_ref[k], halo_ref[k])
        stack_ref[k] = stack
        both = mm(outer_taps(kb_ref, k, 8 * height, fringe_ref), stack)
        edge = (both[:16] + both[16:]) * factor
        edge_ref[k] = edge + jnp.concatenate([grad_ref[k, :8, :], grad_ref[k, height - 8:, :]], axis=0)
        return carry

    lax.fori_loop(0, channels, one, 0, unroll=UNROLL)


def layer_norm(patch, channels):
    values = patch.astype(bf16).astype(f32).reshape(channels, GROUP, LANES)
    center = values - jnp.mean(values, axis=0, keepdims=True)
    spread = jnp.mean(center * center, axis=0, keepdims=True)
    inverse = lax.rsqrt(spread + norm_eps)
    return center * inverse, inverse


def per_row(vec_ref, n):
    return vec_ref[n][:, None, :]


def order_kernel(at_ref, *refs):
    pair_refs, (x_ref, one_ref, two_ref) = refs[:-3], refs[-3:]
    chips = len(pair_refs)
    core, chip = at_ref[0, 0], at_ref[1, 0]
    for away, ref in enumerate(pair_refs):
        there = lax.bitwise_xor(chip, away)
        x_ref[2 * there + core] = ref[0 if away == 0 else 1]
        x_ref[2 * there + 1 - core] = ref[1 if away == 0 else 0]
    half = one_ref.shape[0]
    up = x_ref[:half]
    down = x_ref[2 * chips - half:]
    even = at_ref[6, 0] == 0
    one_ref[...] = jnp.where(even, down, up)
    two_ref[...] = jnp.where(even, up, down)


def main_kernel(colors, file_rows, factor, x_ref, wk_ref, vec_ref, grad_ref, edge_ref, total_ref, stack_ref, rim_ref,
                taps_ref, pick_ref, band_ref, fringe_ref, norm_ref, out_ref, norm_s, grad_s, diag_s):
    channels, height, width = grad_ref.shape
    block = colors * file_rows
    per = GROUP // file_rows
    rows = channels * GROUP
    bias, gain, offset = per_row(vec_ref, 0), per_row(vec_ref, 1), per_row(vec_ref, 2)
    scale_part = jnp.zeros((channels, GROUP, width), f32)
    shift_part = jnp.zeros((channels, GROUP, width), f32)
    inner = 8 * height
    ones = jnp.where(iota((16, width), 0) == 0, 1.0, 0.0).astype(bf16)
    by_color = jnp.zeros((colors + 16, channels), f32)
    for g in range(height // GROUP):
        blocks = [x_ref[per * g + a, :block, :] for a in range(per)]
        patch = mm(wk_ref[...], jnp.concatenate(blocks, axis=0)).reshape(channels, GROUP, width) + bias
        xhat, inverse = layer_norm(patch, channels)
        norm_s[:, g * GROUP:(g + 1) * GROUP, :] = xhat * gain + offset
        if g == 0:
            grad = edge_ref[:, :8, :]
        elif g == height // GROUP - 1:
            grad = edge_ref[:, 8:, :]
        else:
            grad = grad_ref[:, g * GROUP:(g + 1) * GROUP, :]
        scale_part += grad * xhat
        shift_part += grad
        inside = grad * gain
        mean_a = jnp.mean(inside, axis=0, keepdims=True)
        mean_b = jnp.mean(inside * xhat, axis=0, keepdims=True)
        grad_s[g] = (inverse * (inside - mean_a - xhat * mean_b)).reshape(rows, width)
        left, right = [], []
        for h in range(GROUP):
            start = h % file_rows * colors
            left.append(jnp.concatenate([blocks[h // file_rows][start:start + colors], ones], axis=0))
            right.append(grad_s[g, pl.ds(h, channels, stride=GROUP), :].astype(bf16))
        by_color += mm(jnp.concatenate(left, axis=1), jnp.concatenate(right, axis=1), NT)

    def one(k, carry):
        plane = norm_s[k].astype(bf16)
        norm_ref[k] = plane
        both = mm(plane, jnp.concatenate([stack_ref[k], rim_ref[k]], axis=0), NT)
        cross = both[:, :inner]
        total = cross[:8] * band_ref[:8]
        for a in range(1, height // 8):
            rows = cross[8 * a:8 * a + 8]
            if a == height // 8 - 1:
                rows = rows * band_ref[8 * a:]
            total += pltpu.roll(rows, inner - 8 * a, 1)
        cross = both[:, inner:]
        rim = cross[:8] * fringe_ref[:8] + pltpu.roll(cross[height - 8:] * fringe_ref[8:], 8, 1)
        diag_s[k] = jnp.concatenate([total, rim], axis=1)
        return carry

    lax.fori_loop(0, channels, one, 0, unroll=UNROLL)

    line, rim = diag_s[:, 0, :inner], diag_s[:, 0, inner:]
    for b in range(1, 8):
        line += pltpu.roll(diag_s[:, b, :inner], inner - b, 1)
        rim += pltpu.roll(diag_s[:, b, inner:], OUTER - b, 1)
    line = jnp.concatenate([line, rim], axis=1) * factor
    line = jnp.concatenate([jnp.zeros((LANES - channels, line.shape[1]), f32), line], axis=0)
    out_ref[...] = sum(mm(taps_ref[...], part, NT) for part in split2(line))
    parts = jnp.concatenate([jnp.sum(scale_part, axis=1), jnp.sum(shift_part, axis=1), total_ref[...]], axis=1)
    first = sum(mm(pick_ref[...], part, NT) for part in split2(parts))
    out_ref[:, :channels] = first + by_color[:56]


def side_columns(at_ref, wh_ref, vec_ref, lines, row_ok):
    channels = vec_ref.shape[1]
    shape = (channels, GROUP, LANES)
    bias, gain, offset = per_row(vec_ref, 0), per_row(vec_ref, 1), per_row(vec_ref, 2)
    lines.append(jnp.zeros((LANES - 8 * len(lines), wh_ref.shape[1]), f32))
    lines = jnp.concatenate(lines, axis=0).astype(bf16)
    xhat, _ = layer_norm(mm(wh_ref[...], lines, NT).reshape(shape) + bias, channels)
    column = lax.bitwise_and(iota(shape, 2), 7)
    ok = jnp.where(column < 3, 1 - at_ref[4, 0], 1 - at_ref[5, 0]) > 0
    if row_ok is not None:
        ok = ok & row_ok
    return jnp.where(ok, xhat * gain + offset, 0.0).astype(bf16).reshape(channels * GROUP, LANES)


def side_line(pieces, chunks):
    pieces = [piece.astype(f32) for piece in pieces]
    return jnp.concatenate([piece[8 * c:8 * c + 8] for piece in pieces for c in range(chunks)], axis=1)


def stem_side_kernel(colors, file_rows, at_ref, x_ref, wh_ref, vec_ref, halo_ref):
    channels, height, width = halo_ref.shape
    block = colors * file_rows
    per = GROUP // file_rows
    chunks = wh_ref.shape[1] // (per * LANES)
    groups = height // GROUP
    lines = [
        side_line([x_ref[per * g + a, block:block + 16, :] for a in range(per)], chunks) for g in range(groups)
    ]
    halo = side_columns(at_ref, wh_ref, vec_ref, lines, None)
    for g in range(groups):
        moved = pltpu.roll(halo, width - 8 * g - 3, 1).reshape(channels, GROUP, width)
        halo_ref[:, 8 * g:8 * g + 8, :] = moved


def stem_inner_kernel(start, norm_ref, side_ref, kf_ref, vec_ref, band_ref, out_ref):
    count, height, _ = out_ref.shape

    def one(n, carry):
        k = start + n
        both = mm(inner_taps(kf_ref, k, band_ref), shifted(norm_ref[k], side_ref[k]))
        out_ref[n] = both[:height] + both[height:] + vec_ref[3, pl.ds(k, 1), :]
        return carry

    lax.fori_loop(0, count, one, 0, unroll=UNROLL)


def stem_outer_kernel(colors, file_rows, parts, at_ref, one_ref, two_ref, wk_ref, wh_ref, vec_ref, kf_ref, fringe_ref,
                      *refs):
    inner_refs, (out_ref, plane_s, halo_s, out_s, sems) = refs[:parts], refs[parts:]
    channels, height, width = out_s.shape
    block = colors * file_rows
    per = GROUP // file_rows
    half = per // 2
    chunks = wh_ref.shape[1] // (per * LANES)
    shape = (channels, GROUP, width)
    bias, gain, offset = per_row(vec_ref, 0), per_row(vec_ref, 1), per_row(vec_ref, 2)
    row_ok = jnp.where(iota(shape, 1) < 4, 1 - at_ref[3, 0], 1 - at_ref[2, 0]) > 0

    even = at_ref[6, 0] == 0
    one, two = one_ref[...], two_ref[...]
    top, bot = jnp.where(even, two, one), jnp.where(even, one, two)
    blocks = [bot[a] for a in range(half)] + [top[a] for a in range(half)]
    pixels = jnp.concatenate([piece[:block] for piece in blocks], axis=0)
    xhat, _ = layer_norm(mm(wk_ref[...], pixels).reshape(shape) + bias, channels)
    rows = jnp.where(row_ok, xhat * gain + offset, 0.0).astype(bf16)
    line = side_line([piece[block:block + 16] for piece in blocks], chunks)
    side = side_columns(at_ref, wh_ref, vec_ref, [line], row_ok)
    side = pltpu.roll(side, width - 3, 1).reshape(shape)
    for start in (0, 8):
        plane_s[:, start:start + 8, :] = rows
        halo_s[:, start:start + 8, :] = side

    count = channels // parts
    copies = []
    for part, inner_ref in enumerate(inner_refs):
        def one(n, carry, part=part, inner_ref=inner_ref):
            k = part * count + n
            both = mm(outer_taps(kf_ref, k, 8 * height, fringe_ref), shifted(plane_s[k], halo_s[k]))
            edge = both[:16] + both[16:]
            own = inner_ref[n]
            out_s[k] = jnp.concatenate(
                [own[:8] + edge[:8], own[8:height - 8], own[height - 8:] + edge[8:]], axis=0).astype(bf16)
            return carry

        lax.fori_loop(0, count, one, 0, unroll=UNROLL)
        here = pl.ds(part * count, count)
        copies.append(pltpu.make_async_copy(out_s.at[here], out_ref.at[here], sems.at[part]))
        copies[-1].start()
    for copy in copies:
        copy.wait()


def last_kernel(colors, x_ref, y_ref, *outs):
    total = x_ref[...] + y_ref[...]
    channels = outs[1].shape[0]
    first = total[:, :channels]
    second = total[:, channels:2 * channels]
    outs[0][...] = first[:colors]
    for n in range(4):
        outs[1 + n][...] = first[colors + n]
    outs[5][...] = second[:outs[5].shape[0]]


def in_vmem(shape, dtype):
    return pltpu.VMEM(shape, dtype)


def kernel_call(body, out_shape, us, *args, loose=(), **kw):
    loose = tuple(loose) + tuple(kw.get("input_output_aliases", {}))
    args = [
        arg if n in loose else pltpu.with_memory_space_constraint(arg, pltpu.VMEM)
        for n, arg in enumerate(args)
    ]
    return pl.pallas_call(
        body,
        out_shape=out_shape,
        compiler_params=pltpu.CompilerParams(vmem_limit_bytes=VMEM),
        cost_estimate=pl.CostEstimate(flops=int(us * 1e9), bytes_accessed=int(us * 3e6), transcendentals=0),
        **kw,
    )(*args)


def shaped(shape, dtype):
    return jax.ShapeDtypeStruct(shape, dtype)


def pairing(count, odd):
    return [(i, (i + 1 if (i + odd) % 2 == 0 else i - 1) % count) for i in range(count)]


def swap(parts, axis):
    return [lax.ppermute(part, axis, pairing(lax.axis_size(axis), n)) for n, part in enumerate(parts)]


def per_device(
    file_pixels,
    patchify_weight,
    patchify_bias,
    norm_gain,
    norm_offset_vector,
    kernel,
    kernel_offset,
    cotangent,
):
    colors, file_rows, _ = file_pixels.shape
    channels, height, width = cotangent.shape
    n_rows, n_cols = lax.axis_size("rows"), lax.axis_size("cols")
    factor = 1.0 / math.sqrt(height * n_rows * width * n_cols)
    block = colors * file_rows
    per = GROUP // file_rows
    block_rows = block + 16
    padded = cdiv(block, LANES) * LANES
    rows = channels * GROUP
    tile = (channels, height, width)
    inner = 8 * height
    const = constants(colors, file_rows, channels, height)

    row_at, col_at = lax.axis_index("rows"), lax.axis_index("cols")
    chips = n_cols // 2
    at = jnp.stack([
        col_at % 2, col_at // 2, row_at == 0, row_at == n_rows - 1, col_at == 0, col_at == n_cols - 1, row_at % 2, 0,
    ]).astype(jnp.int32)
    at = jnp.broadcast_to(at[:, None], (8, LANES))
    vmem = pl.BlockSpec(memory_space=pltpu.VMEM)
    edge_rows = channels * height // 16

    beyond = pl.BlockSpec(memory_space=pl.ANY)
    cot, keep, give, edges = kernel_call(
        pack_kernel,
        (
            in_vmem(tile, bf16),
            in_vmem((chips, block_rows, LANES), bf16),
            in_vmem((chips * block_rows + edge_rows, LANES), bf16),
            in_vmem((edge_rows + 48, LANES), bf16),
        ),
        2,
        at, *(pltpu.with_memory_space_constraint(arg, pltpu.HBM) for arg in (file_pixels, cotangent)),
        loose=(1, 2),
        in_specs=[vmem] + [beyond] * 2,
        scratch_shapes=[
            pltpu.VMEM((n_cols + 2, 16, block), f32),
            pltpu.VMEM(file_pixels.shape, bf16),
            pltpu.VMEM((block, n_cols * LANES), bf16),
            pltpu.SemaphoreType.DMA((2,)),
        ],
    )
    got = lax.ppermute(give, "cols", [(i, i ^ 1) for i in range(n_cols)])
    far = lax.ppermute(edges, "cols", pairing(n_cols, 1))
    pairs = kernel_call(pair_kernel, (in_vmem((2, block_rows, LANES), bf16),) * chips, 0.5, keep, got)
    pairs = [pairs[0]] + [
        lax.ppermute(pairs[n], "cols", [(i, i ^ (2 * n + 1)) for i in range(n_cols)])
        for n in range(1, chips)
    ]

    kept, far = lax.optimization_barrier((pairs[0], far))
    pairs[0] = kept
    beside, *strips = kernel_call(
        strips_kernel,
        (in_vmem(tile, bf16), in_vmem((channels + channels // 16, 4, width), bf16), in_vmem((channels + channels // 16, 4, width), bf16)),
        0.01,
        at, cot, got, far,
        in_specs=[vmem] + [vmem] * 3,
    )
    beside, taps = lax.optimization_barrier((beside, kernel))
    strips = swap(strips, "rows")
    wk, wh, kb, kf, vec = kernel_call(
        params_kernel,
        (
            in_vmem((rows, per * block), bf16),
            in_vmem((rows, per * padded), bf16),
            in_vmem((channels, inner + 2 * OUTER), f32),
            in_vmem((channels, inner + 2 * OUTER), f32),
            in_vmem((4, channels, LANES), f32),
        ),
        0.01,
        patchify_weight.T, taps.T, patchify_bias, norm_gain, norm_offset_vector, kernel_offset,
        const["spread"], const["keep"], const["spread_halo"], const["keep_halo"], const["tall"],
        const["forward"], const["backward"],
    )
    stack, grad, total = kernel_call(
        functools.partial(back_inner_kernel, factor),
        (in_vmem((channels, inner, width), bf16), in_vmem(tile, f32), in_vmem((channels, width), f32)),
        0.01,
        cot, beside, kb, const["band"],
        scratch_shapes=[pltpu.VMEM((channels, 8, width), f32)],
    )
    rim, edge = kernel_call(
        functools.partial(back_outer_kernel, factor),
        (in_vmem((channels, OUTER, width), bf16), in_vmem((channels, 16, width), f32)),
        0.01,
        at, *strips, grad, kb, const["fringe"],
        scratch_shapes=[pltpu.VMEM((channels, 16, width), bf16)] * 2,
    )

    half = per // 2
    edge, *pairs = lax.optimization_barrier((edge, *pairs))
    pixels, *ends = kernel_call(
        order_kernel,
        (in_vmem((n_cols, block_rows, LANES), bf16),) + (in_vmem((half, block_rows, LANES), bf16),) * 2,
        0.01,
        at, *pairs,
        in_specs=[vmem] + [vmem] * chips,
    )
    norm, result = kernel_call(
        functools.partial(main_kernel, colors, file_rows, factor),
        (in_vmem(tile, bf16), in_vmem((56, LANES), f32)),
        6,
        pixels, wk, vec, grad, edge, total, stack, rim, const["taps"], const["pick"], const["band"], const["fringe"],
        scratch_shapes=[
            pltpu.VMEM(tile, f32),
            pltpu.VMEM((height // GROUP, rows, width), f32),
            pltpu.VMEM((channels, 8, inner + OUTER), f32),
        ],
    )

    size = n_rows * n_cols
    chunk = channels
    rounds = (size - 1).bit_length()
    jobs = {0: ["side"], 1: ["one"], 2: ["two"], 3: [0], rounds - 1: ["outer"]}
    parts = []
    for n in range(rounds):
        step = 1 if n == 0 else (1 << n) + 1
        other = lax.ppermute(result, ("rows", "cols"), [(i, i ^ step) for i in range(size)])
        for job in jobs.get(n, []):
            if job in ("one", "two"):
                which = ("one", "two").index(job)
                result, end = lax.optimization_barrier((result, ends[which]))
                ends[which] = lax.ppermute(end, "rows", pairing(n_rows, which))
            elif job == "side":
                result, pixels = lax.optimization_barrier((result, pixels))
                beside = kernel_call(
                    functools.partial(stem_side_kernel, colors, file_rows),
                    in_vmem(tile, bf16),
                    1,
                    at, pixels, wh, vec,
                )
                result, beside = lax.optimization_barrier((result, beside))
            elif job == "outer":
                result, *parts = lax.optimization_barrier((result, *parts))
                stem_output = kernel_call(
                    functools.partial(stem_outer_kernel, colors, file_rows, len(parts)),
                    shaped(tile, bf16),
                    3,
                    at, *ends, wk, wh, vec, kf, const["fringe"], *parts,
                    in_specs=[vmem] * (8 + len(parts)),
                    out_specs=beyond,
                    scratch_shapes=[
                        pltpu.VMEM((channels, 16, width), bf16),
                        pltpu.VMEM((channels, 16, width), bf16),
                        pltpu.VMEM(tile, bf16),
                        pltpu.SemaphoreType.DMA((len(parts),)),
                    ],
                )
                result, stem_output = lax.optimization_barrier((result, stem_output))
            else:
                result, norm = lax.optimization_barrier((result, norm))
                part = kernel_call(
                    functools.partial(stem_inner_kernel, job * chunk),
                    in_vmem((chunk, height, width), f32),
                    2,
                    norm, beside, kf, vec, const["band"],
                )
                result, part = lax.optimization_barrier((result, part))
                parts.append(part)
        if n < rounds - 1:
            result = result + other

    taps = side * side
    outs = kernel_call(
        functools.partial(last_kernel, colors),
        (shaped((colors, channels), f32),) + (shaped((channels,), f32),) * 4 + (shaped((taps, channels), f32),),
        1,
        result, other,
    )
    return (stem_output, outs[0].T, outs[1], outs[2], outs[3], outs[5].T, outs[4])


def solution(mesh):
    return jax.shard_map(
        per_device,
        mesh=mesh,
        in_specs=(
            P(None, ("rows", "cols"), None),
            P(),
            P(),
            P(),
            P(),
            P(),
            P(),
            P(None, "rows", "cols"),
        ),
        out_specs=(P(None, "rows", "cols"), P(), P(), P(), P(), P(), P()),
        check_vma=False,
    )
```

```python
import functools
import math

import jax
import jax.numpy as jnp
import numpy as np
from jax import lax
from jax.experimental import pallas as pl
from jax.experimental.pallas import tpu as pltpu
from jax.sharding import PartitionSpec as P

norm_eps = 1e-06
side = 7
LANES = 128
GROUP = 8
OUTER = 8 * 16
VMEM = 20 * 1024 * 1024
UNROLL = 64
bf16, f32 = jnp.bfloat16, jnp.float32

NN = (((1,), (0,)), ((), ()))
NT = (((1,), (1,)), ((), ()))
TN = (((0,), (0,)), ((), ()))


def mm(a, b, dims=NN):
    return lax.dot_general(a, b, dims, preferred_element_type=f32)


def iota(shape, axis):
    return lax.broadcasted_iota(jnp.int32, shape, axis)


def split2(x):
    high = x.astype(bf16)
    return high, (x - high.astype(f32)).astype(bf16)


def one_hot(cond):
    return jnp.where(cond, 1.0, 0.0).astype(bf16)


def cdiv(a, b):
    return -(-a // b)


def constants(colors, file_rows, channels, height):
    block = colors * file_rows
    per = GROUP // file_rows
    rows = channels * GROUP
    out = {}
    at = np.arange(per * block)
    out["spread"] = (at % colors)[None, :] == np.arange(colors)[:, None]
    out["keep"] = (at // colors)[None, :] == (np.arange(rows) % GROUP)[:, None]
    out["tall"] = (np.arange(rows) // GROUP)[:, None] == np.arange(channels)[None, :]
    inner = 8 * height
    count = side * side
    forward = np.zeros((count, inner + 2 * OUTER), bool)
    taps = np.zeros((56, inner + OUTER), bool)
    for tap in range(count):
        down, copy = divmod(tap, side)
        own, above, below = height * copy + down - 3, 16 * copy + down + 5, 16 * copy + down - 3
        forward[tap, own % inner] = True
        forward[tap, inner + above] = True
        forward[tap, inner + OUTER + below % OUTER] = True
        taps[count - 1 - tap, own % inner] = True
        taps[count - 1 - tap, inner + above] = True
    out["forward"], out["backward"], out["taps"] = forward, forward[::-1], taps
    lane, row = np.arange(inner)[None, :], np.arange(height)[:, None]
    out["band"] = (abs(lane % height - row) <= 3) & (lane < height * side)
    lane, row = np.arange(OUTER)[None, :], np.arange(8)[:, None]
    at = lane % 16
    out["fringe"] = np.concatenate([(at < 8) & (at >= row + 5), (at >= 8) & (at <= row + 3)]) & (lane < 16 * side)
    pick = np.zeros((3, 56, LANES), bool)
    for n in range(3):
        pick[n, colors + 1 + n] = True
    out["pick"] = np.concatenate(list(pick), axis=1)
    return {k: jnp.asarray(v, f32 if k in ("band", "fringe") else bf16) for k, v in out.items()}


def params_kernel(wt_ref, taps_ref, bias_ref, gain_ref, off_ref, koff_ref, spread_ref, keep_ref, tall_ref, forward_ref,
                  backward_ref, wk_ref, kb_ref, kf_ref, vec_ref):
    channels = wt_ref.shape[1]
    wide = mm(wt_ref[...], spread_ref[...], TN).astype(bf16)
    wk_ref[...] = mm(tall_ref[...], wide).astype(bf16) * keep_ref[...]
    parts = split2(taps_ref[...])
    for place, out_ref in ((forward_ref, kf_ref), (backward_ref, kb_ref)):
        out_ref[...] = sum(mm(part, place[...], TN) for part in parts)
    eye = iota((channels, channels), 0) == iota((channels, channels), 1)
    for n, ref in enumerate((bias_ref, gain_ref, off_ref, koff_ref)):
        row = jnp.broadcast_to(ref[...].reshape(1, channels), (channels, channels))
        column = jnp.sum(jnp.where(eye, row, 0.0), axis=1, keepdims=True)
        vec_ref[n] = jnp.broadcast_to(column, (channels, LANES))


def pack_kernel(at_ref, x_hbm, cot_hbm, cot_ref, keep_ref, give_ref, edge_ref, edge_s, x_ref, y_ref, sems):
    colors, file_rows, width = x_ref.shape
    channels, height, _ = cot_ref.shape
    chips, block_rows, _ = keep_ref.shape
    count = width // LANES
    block = colors * file_rows
    core, chip = at_ref[0, 0], at_ref[1, 0]
    load_x = pltpu.make_async_copy(x_hbm, x_ref, sems.at[0])
    load_cot = pltpu.make_async_copy(cot_hbm, cot_ref, sems.at[1])
    load_x.start()
    load_cot.start()
    row, src = iota((block, block), 0), iota((block, block), 1)
    part = sum((row >= colors * n).astype(jnp.int32) for n in range(1, file_rows)) if file_rows > 1 else 0
    move = one_hot(src == (row - colors * part) * file_rows + part)
    load_x.wait()
    y_ref[...] = mm(move, x_ref[...].reshape(block, width)).astype(bf16)

    row, lane = iota((16, LANES), 0), iota((16, LANES), 1)
    pick = one_hot(((row < 3) & (lane == row + LANES - 3)) | ((row >= 11) & (row < 14) & (lane == row - 11)))
    zeros = jnp.zeros((16, block), f32)
    edge_s[0] = zeros
    edge_s[count + 1] = zeros
    for d in range(count):
        tile = y_ref[:, d * LANES:(d + 1) * LANES]
        edge_s[d + 1] = mm(pick, tile, NT)

    def halo(d):
        both = edge_s[d][:8] + edge_s[d + 2][8:]
        chunks = []
        for start in range(0, 2 * LANES, LANES):
            stop = min(start + LANES, block)
            if stop <= start:
                chunks.append(jnp.zeros((8, LANES), f32))
            elif stop - start < LANES:
                chunks.append(jnp.concatenate(
                    [both[:, start:stop], jnp.zeros((8, LANES - stop + start), f32)], axis=1))
            else:
                chunks.append(both[:, start:stop])
        return jnp.concatenate(chunks, axis=0).astype(bf16)

    for away in range(chips):
        there = lax.bitwise_xor(chip, away)
        for other in range(2):
            d = 2 * there + (core if (other == 0) == (away == 0) else 1 - core)
            tile = y_ref[:, pl.ds(pl.multiple_of(d * LANES, LANES), LANES)]
            if other == 0:
                keep_ref[away, :block, :] = tile
                keep_ref[away, block:, :] = halo(d)
            else:
                start = away * block_rows
                give_ref[start:start + block, :] = tile
                give_ref[start + block:start + block_rows, :] = halo(d)

    load_cot.wait()

    row, lane = iota((8, LANES), 0), iota((8, LANES), 1)
    pick = one_hot(((row < 3) & (lane == row)) | ((row >= 3) & (row < 6) & (lane == row + LANES - 6)))
    edges = mm(pick, cot_ref[...].reshape(channels * height, LANES), NT)
    edges = jnp.concatenate(
        [edges[:, n:n + LANES] for n in range(0, channels * height, LANES)], axis=0).astype(bf16)
    edge_ref[:edges.shape[0]] = edges
    edge_ref[edges.shape[0]:] = edges[:edge_ref.shape[0] - edges.shape[0]]
    give_ref[chips * block_rows:, :] = edges


def pair_kernel(keep_ref, got_ref, *pair_refs):
    _, block_rows, _ = keep_ref.shape
    for away, ref in enumerate(pair_refs):
        ref[0] = keep_ref[away]
        ref[1] = got_ref[away * block_rows:(away + 1) * block_rows, :]


def strips_kernel(at_ref, cot_ref, near_ref, far_ref, halo_ref, one_ref, two_ref):
    channels, height, width = cot_ref.shape
    size = channels * height // 16
    core = at_ref[0, 0]
    near = near_ref[near_ref.shape[0] - size:, :].astype(f32)
    far = far_ref[:size, :].astype(f32)
    left = jnp.where(core == 0, far, near)
    right = jnp.where(core == 0, near, far)
    sides = jnp.concatenate(
        [jnp.concatenate([side[n:n + 8] for n in range(0, size, 8)], axis=1) for side in (left, right)], axis=0)
    row, lane = iota((16, width), 0), iota((16, width), 1)
    from_left = (row >= 3) & (row < 6) & (lane == row + width - 6) & (at_ref[4, 0] == 0)
    from_right = (row >= 8) & (row < 11) & (lane == row - 8) & (at_ref[5, 0] == 0)
    halo = mm(sides.astype(bf16), one_hot(from_left | from_right), TN).reshape(channels, height, width)
    halo_ref[...] = halo.astype(bf16)
    write_strips(at_ref, cot_ref[...].astype(f32), halo, one_ref, two_ref)


def write_strips(at_ref, own, halo, one_ref, two_ref):
    channels, height, width = own.shape
    row, lane = iota((8, width), 0), iota((8, width), 1)
    pick = one_hot((lane == row + width - 3) & (row < 3) | (lane == row - 3) & (row >= 3) & (row < 6))
    up, down = own[:, :4], own[:, height - 4:]
    up_halo, down_halo = halo[:, :4], halo[:, height - 4:]
    even = at_ref[6, 0] == 0
    for ref, rows, beside in (
        (one_ref, jnp.where(even, down, up), jnp.where(even, down_halo, up_halo)),
        (two_ref, jnp.where(even, up, down), jnp.where(even, up_halo, down_halo)),
    ):
        ref[:channels] = rows.astype(bf16)
        dense = mm(pick, beside.reshape(channels * 4, width).astype(bf16), NT)
        for n in range(0, channels * 4, LANES):
            for q in range(2):
                ref[channels + n // 64 + q] = dense[4 * q:4 * q + 4, n:n + LANES].astype(bf16)


def read_strips(at_ref, one_ref, two_ref, plane_ref, halo_ref):
    channels, _, width = plane_ref.shape
    even = at_ref[6, 0] == 0
    one, two = one_ref[...].astype(f32), two_ref[...].astype(f32)
    top = jnp.where(at_ref[2, 0] == 0, jnp.where(even, two, one), 0.0)
    bot = jnp.where(at_ref[3, 0] == 0, jnp.where(even, one, two), 0.0)
    row, lane = iota((8, width), 0), iota((8, width), 1)
    place = one_hot((lane == row + width - 3) & (row < 3) | (lane == row - 3) & (row >= 3) & (row < 6))

    def beside(part):
        dense = jnp.concatenate(
            [
                jnp.concatenate([part[channels + n // 64 + q] for q in range(2)], axis=0)
                for n in range(0, channels * 4, LANES)
            ],
            axis=1,
        )
        return mm(dense.astype(bf16), place, TN).reshape(channels, 4, width)

    none = jnp.zeros((channels, 4, width), f32)
    plane_ref[...] = jnp.concatenate([none, top[:channels], bot[:channels], none], axis=1).astype(bf16)
    halo_ref[...] = jnp.concatenate([none, beside(top), beside(bot), none], axis=1).astype(bf16)


def shifted(center, halo):
    rows, width = center.shape
    lane = iota((rows, width), 1)
    copies = []
    for move in range(-3, 4):
        if move == 0:
            copies.append(center)
        elif move > 0:
            copies.append(pltpu.roll(jnp.where(lane < move, halo, center), width - move, 1))
        else:
            copies.append(pltpu.roll(jnp.where(lane >= width + move, halo, center), -move, 1))
    copies.append(jnp.zeros((rows, width), center.dtype))
    return jnp.concatenate(copies, axis=0)


def toeplitz(base, mask):
    return pltpu.roll(jnp.broadcast_to(base, mask.shape), 0, 1, stride=1, stride_axis=0) * mask


def inner_taps(base_ref, k, band_ref):
    inner = band_ref.shape[1]
    base = base_ref[pl.ds(k, 1), :]
    return jnp.concatenate(split2(toeplitz(base[:, :inner], band_ref[...])), axis=0)


def outer_taps(base_ref, k, inner, fringe_ref):
    base = base_ref[pl.ds(k, 1), :]
    above = toeplitz(base[:, inner:inner + OUTER], fringe_ref[:8])
    below = toeplitz(base[:, inner + OUTER:], fringe_ref[8:])
    return jnp.concatenate(split2(jnp.concatenate([above, below], axis=0)), axis=0)


def back_inner_kernel(factor, cot_ref, beside_ref, kb_ref, band_ref, stack_ref, grad_ref, total_ref, sum_ref):
    channels, height, width = cot_ref.shape

    def one(k, carry):
        plane = cot_ref[k]
        stack = shifted(plane, beside_ref[k])
        stack_ref[k] = stack
        both = mm(inner_taps(kb_ref, k, band_ref), stack)
        grad_ref[k] = (both[:height] + both[height:]) * factor
        sum_ref[k] = jnp.sum(plane.astype(f32).reshape(height // 8, 8, width), axis=0)
        return carry

    lax.fori_loop(0, channels, one, 0, unroll=UNROLL)
    total_ref[...] = sum(sum_ref[:, b, :] for b in range(8)) * factor


def back_outer_kernel(factor, at_ref, one_ref, two_ref, grad_ref, kb_ref, fringe_ref,
                      stack_ref, edge_ref, plane_ref, halo_ref):
    channels, height, width = grad_ref.shape
    read_strips(at_ref, one_ref, two_ref, plane_ref, halo_ref)

    def one(k, carry):
        stack = shifted(plane_ref[k], halo_ref[k])
        stack_ref[k] = stack
        both = mm(outer_taps(kb_ref, k, 8 * height, fringe_ref), stack)
        edge = (both[:16] + both[16:]) * factor
        edge_ref[k] = edge + jnp.concatenate([grad_ref[k, :8, :], grad_ref[k, height - 8:, :]], axis=0)
        return carry

    lax.fori_loop(0, channels, one, 0, unroll=UNROLL)


def layer_norm(patch, channels):
    values = patch.astype(bf16).astype(f32).reshape(channels, GROUP, LANES)
    center = values - jnp.mean(values, axis=0, keepdims=True)
    spread = jnp.mean(center * center, axis=0, keepdims=True)
    inverse = lax.rsqrt(spread + norm_eps)
    return center * inverse, inverse


def per_row(vec_ref, n):
    return vec_ref[n][:, None, :]


def order_kernel(at_ref, *refs):
    pair_refs, x_ref = refs[:-1], refs[-1]
    chips = len(pair_refs)
    core, chip = at_ref[0, 0], at_ref[1, 0]
    for away, ref in enumerate(pair_refs):
        there = lax.bitwise_xor(chip, away)
        x_ref[2 * there + core] = ref[0 if away == 0 else 1]
        x_ref[2 * there + 1 - core] = ref[1 if away == 0 else 0]


def main_kernel(colors, file_rows, factor, x_ref, wk_ref, vec_ref, grad_ref, edge_ref, total_ref, stack_ref, rim_ref,
                taps_ref, pick_ref, band_ref, fringe_ref, norm_ref, out_ref, norm_s, grad_s, diag_s):
    channels, height, width = grad_ref.shape
    block = colors * file_rows
    per = GROUP // file_rows
    rows = channels * GROUP
    bias, gain, offset = per_row(vec_ref, 0), per_row(vec_ref, 1), per_row(vec_ref, 2)
    scale_part = jnp.zeros((channels, GROUP, width), f32)
    shift_part = jnp.zeros((channels, GROUP, width), f32)
    inner = 8 * height
    ones = jnp.where(iota((16, width), 0) == 0, 1.0, 0.0).astype(bf16)
    by_color = jnp.zeros((channels, colors + 16), f32)
    for g in range(height // GROUP):
        blocks = [x_ref[per * g + a, :block, :] for a in range(per)]
        patch = mm(wk_ref[...], jnp.concatenate(blocks, axis=0)).reshape(channels, GROUP, width) + bias
        xhat, inverse = layer_norm(patch, channels)
        norm_s[:, g * GROUP:(g + 1) * GROUP, :] = xhat * gain + offset
        if g == 0:
            grad = edge_ref[:, :8, :]
        elif g == height // GROUP - 1:
            grad = edge_ref[:, 8:, :]
        else:
            grad = grad_ref[:, g * GROUP:(g + 1) * GROUP, :]
        scale_part += grad * xhat
        shift_part += grad
        inside = grad * gain
        mean_a = jnp.mean(inside, axis=0, keepdims=True)
        mean_b = jnp.mean(inside * xhat, axis=0, keepdims=True)
        grad_s[g] = (inverse * (inside - mean_a - xhat * mean_b)).reshape(rows, width)
        left, right = [], []
        for h in range(GROUP):
            start = h % file_rows * colors
            left.append(jnp.concatenate([blocks[h // file_rows][start:start + colors], ones], axis=0))
            right.append(grad_s[g, pl.ds(h, channels, stride=GROUP), :].astype(bf16))
        by_color += mm(jnp.concatenate(right, axis=1), jnp.concatenate(left, axis=1), NT)

    band, fringe = band_ref[...], fringe_ref[...]
    none = jnp.zeros((height, width), bf16)

    def one(n, carry):
        planes, stacks = [], []
        for m in range(2):
            k = 2 * n + m
            plane = norm_s[k].astype(bf16)
            norm_ref[k] = plane
            planes.append(jnp.concatenate([plane, none] if m == 0 else [none, plane], axis=1))
            stacks.append(jnp.concatenate([stack_ref[k], rim_ref[k]], axis=0))
        both = mm(jnp.concatenate(planes, axis=0), jnp.concatenate(stacks, axis=1), NT)
        for m in range(2):
            cross = both[m * height:(m + 1) * height, :inner]
            total = cross[:8] * band[:8]
            for a in range(1, height // 8):
                rows = cross[8 * a:8 * a + 8]
                if a == height // 8 - 1:
                    rows = rows * band[8 * a:]
                total += pltpu.roll(rows, inner - 8 * a, 1)
            cross = both[m * height:(m + 1) * height, inner:]
            rim = cross[:8] * fringe[:8] + pltpu.roll(cross[height - 8:] * fringe[8:], 8, 1)
            diag_s[2 * n + m] = jnp.concatenate([total, rim], axis=1)
        return carry

    lax.fori_loop(0, channels // 2, one, 0, unroll=UNROLL // 2)

    line, rim = diag_s[:, 0, :inner], diag_s[:, 0, inner:]
    for b in range(1, 8):
        line += pltpu.roll(diag_s[:, b, :inner], inner - b, 1)
        rim += pltpu.roll(diag_s[:, b, inner:], OUTER - b, 1)
    line = jnp.concatenate([line, rim], axis=1) * factor
    line = jnp.concatenate([jnp.zeros((LANES - channels, line.shape[1]), f32), line], axis=0)
    out_ref[...] = sum(mm(taps_ref[...], part, NT) for part in split2(line))
    parts = jnp.concatenate([jnp.sum(scale_part, axis=1), jnp.sum(shift_part, axis=1), total_ref[...]], axis=1)
    first = sum(mm(pick_ref[...], part, NT) for part in split2(parts))
    out_ref[:, :channels] = first + by_color.T[:56]


def side_line(pieces, block):
    parts = []
    for piece in pieces:
        piece = piece.astype(f32)
        for start in range(0, block, LANES):
            at = start // LANES * 8
            parts.append(piece[at:at + 8, :min(LANES, block - start)])
    return jnp.concatenate(parts, axis=1)


def stem_side_kernel(colors, file_rows, at_ref, x_ref, norm_ref, wk_ref, vec_ref, halo_ref, one_ref, two_ref):
    channels, height, width = halo_ref.shape
    block = colors * file_rows
    per = GROUP // file_rows
    groups = height // GROUP
    shape = (channels, GROUP, LANES)
    bias, gain, offset = per_row(vec_ref, 0), per_row(vec_ref, 1), per_row(vec_ref, 2)
    lines = [side_line([x_ref[per * g + a, block:block + 16, :] for a in range(per)], block) for g in range(groups)]
    lines.append(jnp.zeros((LANES - 8 * groups, wk_ref.shape[1]), f32))
    lines = jnp.concatenate(lines, axis=0).astype(bf16)
    xhat, _ = layer_norm(mm(wk_ref[...], lines, NT).reshape(shape) + bias, channels)
    column = lax.bitwise_and(iota(shape, 2), 7)
    ok = jnp.where(column < 3, 1 - at_ref[4, 0], 1 - at_ref[5, 0]) > 0
    halo = jnp.where(ok, xhat * gain + offset, 0.0).astype(bf16).reshape(channels * GROUP, LANES)
    for g in range(groups):
        moved = pltpu.roll(halo, width - 8 * g - 3, 1).reshape(channels, GROUP, width)
        halo_ref[:, 8 * g:8 * g + 8, :] = moved
    write_strips(at_ref, norm_ref[...].astype(f32), halo_ref[...].astype(f32), one_ref, two_ref)


def stem_inner_kernel(start, norm_ref, side_ref, kf_ref, vec_ref, band_ref, out_ref):
    count, height, _ = out_ref.shape

    def one(n, carry):
        k = start + n
        both = mm(inner_taps(kf_ref, k, band_ref), shifted(norm_ref[k], side_ref[k]))
        out_ref[n] = both[:height] + both[height:] + vec_ref[3, pl.ds(k, 1), :]
        return carry

    lax.fori_loop(0, count, one, 0, unroll=min(UNROLL, count))


def stem_outer_kernel(parts, at_ref, one_ref, two_ref, kf_ref, fringe_ref, *refs):
    inner_refs, (out_ref, plane_s, halo_s, out_s, sems) = refs[:parts], refs[parts:]
    channels, height, _ = out_s.shape
    read_strips(at_ref, one_ref, two_ref, plane_s, halo_s)
    count = channels // parts
    copies = []
    for part, inner_ref in enumerate(inner_refs):
        def one(n, carry, part=part, inner_ref=inner_ref):
            k = part * count + n
            both = mm(outer_taps(kf_ref, k, 8 * height, fringe_ref), shifted(plane_s[k], halo_s[k]))
            edge = both[:16] + both[16:]
            own = inner_ref[n]
            out_s[k] = jnp.concatenate(
                [own[:8] + edge[:8], own[8:height - 8], own[height - 8:] + edge[8:]], axis=0).astype(bf16)
            return carry

        lax.fori_loop(0, count, one, 0, unroll=min(UNROLL, count))
        here = pl.ds(part * count, count)
        copies.append(pltpu.make_async_copy(out_s.at[here], out_ref.at[here], sems.at[part]))
        copies[-1].start()
    for copy in copies:
        copy.wait()


def last_kernel(colors, *refs):
    parts, outs = refs[:-6], refs[-6:]
    total = sum(part[...] for part in parts)
    channels = outs[1].shape[0]
    first = total[:, :channels]
    second = total[:, channels:2 * channels]
    outs[0][...] = first[:colors]
    for n in range(4):
        outs[1 + n][...] = first[colors + n]
    outs[5][...] = second[:outs[5].shape[0]]


def in_vmem(shape, dtype):
    return pltpu.VMEM(shape, dtype)


def kernel_call(body, out_shape, us, *args, loose=(), **kw):
    loose = tuple(loose) + tuple(kw.get("input_output_aliases", {}))
    args = [
        arg if n in loose else pltpu.with_memory_space_constraint(arg, pltpu.VMEM)
        for n, arg in enumerate(args)
    ]
    return pl.pallas_call(
        body,
        out_shape=out_shape,
        compiler_params=pltpu.CompilerParams(vmem_limit_bytes=VMEM),
        cost_estimate=pl.CostEstimate(flops=int(us * 1e9), bytes_accessed=int(us * 3e6), transcendentals=0),
        **kw,
    )(*args)


def shaped(shape, dtype):
    return jax.ShapeDtypeStruct(shape, dtype)


def pairing(count, odd):
    return [(i, (i + 1 if (i + odd) % 2 == 0 else i - 1) % count) for i in range(count)]


def swap(parts, axis):
    return [lax.ppermute(part, axis, pairing(lax.axis_size(axis), n)) for n, part in enumerate(parts)]


def per_device(
    file_pixels,
    patchify_weight,
    patchify_bias,
    norm_gain,
    norm_offset_vector,
    kernel,
    kernel_offset,
    cotangent,
):
    colors, file_rows, _ = file_pixels.shape
    channels, height, width = cotangent.shape
    n_rows, n_cols = lax.axis_size("rows"), lax.axis_size("cols")
    factor = 1.0 / math.sqrt(height * n_rows * width * n_cols)
    block = colors * file_rows
    per = GROUP // file_rows
    block_rows = block + 16
    rows = channels * GROUP
    tile = (channels, height, width)
    inner = 8 * height
    const = constants(colors, file_rows, channels, height)

    row_at, col_at = lax.axis_index("rows"), lax.axis_index("cols")
    chips = n_cols // 2
    at = (col_at % 2, col_at // 2, row_at == 0, row_at == n_rows - 1, col_at == 0, col_at == n_cols - 1, row_at % 2)
    at = sum(jnp.where(iota((8, LANES), 0) == n, x.astype(jnp.int32), 0) for n, x in enumerate(at))
    vmem = pl.BlockSpec(memory_space=pltpu.VMEM)
    edge_rows = channels * height // 16

    beyond = pl.BlockSpec(memory_space=pl.ANY)
    cot, keep, give, edges = kernel_call(
        pack_kernel,
        (
            in_vmem(tile, bf16),
            in_vmem((chips, block_rows, LANES), bf16),
            in_vmem((chips * block_rows + edge_rows, LANES), bf16),
            in_vmem((edge_rows + 48, LANES), bf16),
        ),
        2,
        at, *(pltpu.with_memory_space_constraint(arg, pltpu.HBM) for arg in (file_pixels, cotangent)),
        loose=(1, 2),
        in_specs=[vmem] + [beyond] * 2,
        scratch_shapes=[
            pltpu.VMEM((n_cols + 2, 16, block), f32),
            pltpu.VMEM(file_pixels.shape, bf16),
            pltpu.VMEM((block, n_cols * LANES), bf16),
            pltpu.SemaphoreType.DMA((2,)),
        ],
    )
    got = lax.ppermute(give, "cols", [(i, i ^ 1) for i in range(n_cols)])
    far = lax.ppermute(edges, "cols", pairing(n_cols, 1))
    pairs = kernel_call(pair_kernel, (in_vmem((2, block_rows, LANES), bf16),) * chips, 0.5, keep, got)
    pairs = [pairs[0]] + [
        lax.ppermute(pairs[n], "cols", [(i, i ^ (2 * n + 1)) for i in range(n_cols)])
        for n in range(1, chips)
    ]

    kept, far = lax.optimization_barrier((pairs[0], far))
    pairs[0] = kept
    beside, *strips = kernel_call(
        strips_kernel,
        (in_vmem(tile, bf16), in_vmem((channels + channels // 16, 4, width), bf16), in_vmem((channels + channels // 16, 4, width), bf16)),
        0.01,
        at, cot, got, far,
        in_specs=[vmem] + [vmem] * 3,
    )
    beside, taps = lax.optimization_barrier((beside, kernel))
    strips = swap(strips, "rows")
    wk, kb, kf, vec = kernel_call(
        params_kernel,
        (
            in_vmem((rows, per * block), bf16),
            in_vmem((channels, inner + 2 * OUTER), f32),
            in_vmem((channels, inner + 2 * OUTER), f32),
            in_vmem((4, channels, LANES), f32),
        ),
        0.01,
        patchify_weight.T, taps.T, patchify_bias, norm_gain, norm_offset_vector, kernel_offset,
        const["spread"], const["keep"], const["tall"], const["forward"], const["backward"],
    )
    stack, grad, total = kernel_call(
        functools.partial(back_inner_kernel, factor),
        (in_vmem((channels, inner, width), bf16), in_vmem(tile, f32), in_vmem((channels, width), f32)),
        0.01,
        cot, beside, kb, const["band"],
        scratch_shapes=[pltpu.VMEM((channels, 8, width), f32)],
    )
    rim, edge = kernel_call(
        functools.partial(back_outer_kernel, factor),
        (in_vmem((channels, OUTER, width), bf16), in_vmem((channels, 16, width), f32)),
        0.01,
        at, *strips, grad, kb, const["fringe"],
        scratch_shapes=[pltpu.VMEM((channels, 16, width), bf16)] * 2,
    )

    edge, *pairs = lax.optimization_barrier((edge, *pairs))
    pixels = kernel_call(order_kernel, in_vmem((n_cols, block_rows, LANES), bf16), 0.01, at, *pairs)
    norm, result = kernel_call(
        functools.partial(main_kernel, colors, file_rows, factor),
        (in_vmem(tile, bf16), in_vmem((56, LANES), f32)),
        6,
        pixels, wk, vec, grad, edge, total, stack, rim, const["taps"], const["pick"], const["band"], const["fringe"],
        scratch_shapes=[
            pltpu.VMEM(tile, f32),
            pltpu.VMEM((height // GROUP, rows, width), f32),
            pltpu.VMEM((channels, 8, inner + OUTER), f32),
        ],
    )

    size = n_rows * n_cols
    chunk = channels // 2
    stages = [[1], [3, 5, 7], [9, 17, 25]]
    jobs = {0: ["side"], 1: ["one", "two", 0], 2: [1, "outer"]}
    parts = []
    for n, steps in enumerate(stages):
        others = [lax.ppermute(result, ("rows", "cols"), [(i, i ^ step) for i in range(size)]) for step in steps]
        for job in jobs.get(n, []):
            if job in ("one", "two"):
                which = ("one", "two").index(job)
                result, end = lax.optimization_barrier((result, ends[which]))
                ends[which] = lax.ppermute(end, "rows", pairing(n_rows, which))
            elif job == "side":
                result, norm = lax.optimization_barrier((result, norm))
                beside, *ends = kernel_call(
                    functools.partial(stem_side_kernel, colors, file_rows),
                    (in_vmem(tile, bf16),) + (in_vmem((channels + channels // 16, 4, width), bf16),) * 2,
                    1,
                    at, pixels, norm, wk, vec,
                )
                result, beside = lax.optimization_barrier((result, beside))
            elif job == "outer":
                result, *parts = lax.optimization_barrier((result, *parts))
                stem_output = kernel_call(
                    functools.partial(stem_outer_kernel, len(parts)),
                    shaped(tile, bf16),
                    3,
                    at, *ends, kf, const["fringe"], *parts,
                    in_specs=[vmem] * (5 + len(parts)),
                    out_specs=beyond,
                    scratch_shapes=[
                        pltpu.VMEM((channels, 16, width), bf16),
                        pltpu.VMEM((channels, 16, width), bf16),
                        pltpu.VMEM(tile, bf16),
                        pltpu.SemaphoreType.DMA((len(parts),)),
                    ],
                )
                result, stem_output = lax.optimization_barrier((result, stem_output))
            else:
                result, norm = lax.optimization_barrier((result, norm))
                part = kernel_call(
                    functools.partial(stem_inner_kernel, job * chunk),
                    in_vmem((chunk, height, width), f32),
                    2,
                    norm, beside, kf, vec, const["band"],
                )
                result, part = lax.optimization_barrier((result, part))
                parts.append(part)
        if n < len(stages) - 1:
            result = sum(others, result)

    taps = side * side
    outs = kernel_call(
        functools.partial(last_kernel, colors),
        (shaped((colors, channels), f32),) + (shaped((channels,), f32),) * 4 + (shaped((taps, channels), f32),),
        1,
        result, *others,
    )
    return (stem_output, outs[0].T, outs[1], outs[2], outs[3], outs[5].T, outs[4])


def solution(mesh):
    return jax.shard_map(
        per_device,
        mesh=mesh,
        in_specs=(
            P(None, ("rows", "cols"), None),
            P(),
            P(),
            P(),
            P(),
            P(),
            P(),
            P(None, "rows", "cols"),
        ),
        out_specs=(P(None, "rows", "cols"), P(), P(), P(), P(), P(), P()),
        check_vma=False,
    )
```

```python
import functools
import math

import jax
import jax.numpy as jnp
import numpy as np
from jax import lax
from jax.experimental import pallas as pl
from jax.experimental.pallas import tpu as pltpu
from jax.sharding import PartitionSpec as P

norm_eps = 1e-06
side = 7
LANES = 128
GROUP = 8
OUTER = 8 * 16
VMEM = 20 * 1024 * 1024
UNROLL = 64
bf16, f32 = jnp.bfloat16, jnp.float32

NN = (((1,), (0,)), ((), ()))
NT = (((1,), (1,)), ((), ()))
TN = (((0,), (0,)), ((), ()))


def mm(a, b, dims=NN):
    return lax.dot_general(a, b, dims, preferred_element_type=f32)


def iota(shape, axis):
    return lax.broadcasted_iota(jnp.int32, shape, axis)


def split2(x):
    high = x.astype(bf16)
    return high, (x - high.astype(f32)).astype(bf16)


def one_hot(cond):
    return jnp.where(cond, 1.0, 0.0).astype(bf16)


def cdiv(a, b):
    return -(-a // b)


def constants(colors, file_rows, channels, height):
    block = colors * file_rows
    per = GROUP // file_rows
    rows = channels * GROUP
    out = {}
    at = np.arange(per * block)
    out["spread"] = (at % colors)[None, :] == np.arange(colors)[:, None]
    out["keep"] = (at // colors)[None, :] == (np.arange(rows) % GROUP)[:, None]
    out["tall"] = (np.arange(rows) // GROUP)[:, None] == np.arange(channels)[None, :]
    inner = 8 * height
    count = side * side
    forward = np.zeros((count, inner + 2 * OUTER), bool)
    taps = np.zeros((56, inner + OUTER), bool)
    for tap in range(count):
        down, copy = divmod(tap, side)
        own, above, below = height * copy + down - 3, 16 * copy + down + 5, 16 * copy + down - 3
        forward[tap, own % inner] = True
        forward[tap, inner + above] = True
        forward[tap, inner + OUTER + below % OUTER] = True
        taps[count - 1 - tap, own % inner] = True
        taps[count - 1 - tap, inner + above] = True
    out["forward"], out["backward"], out["taps"] = forward, forward[::-1], taps
    lane, row = np.arange(inner)[None, :], np.arange(height)[:, None]
    out["band"] = (abs(lane % height - row) <= 3) & (lane < height * side)
    lane, row = np.arange(OUTER)[None, :], np.arange(8)[:, None]
    at = lane % 16
    out["fringe"] = np.concatenate([(at < 8) & (at >= row + 5), (at >= 8) & (at <= row + 3)]) & (lane < 16 * side)
    pick = np.zeros((3, 56, LANES), bool)
    for n in range(3):
        pick[n, colors + 1 + n] = True
    out["pick"] = np.concatenate(list(pick), axis=1)
    return {k: jnp.asarray(v, f32 if k in ("band", "fringe") else bf16) for k, v in out.items()}


def params_kernel(wt_ref, taps_ref, bias_ref, gain_ref, off_ref, koff_ref, spread_ref, keep_ref, tall_ref, forward_ref,
                  backward_ref, wk_ref, kb_ref, kf_ref, vec_ref):
    channels = wt_ref.shape[1]
    wide = mm(wt_ref[...], spread_ref[...], TN).astype(bf16)
    wk_ref[...] = mm(tall_ref[...], wide).astype(bf16) * keep_ref[...]
    parts = split2(taps_ref[...])
    for place, out_ref in ((forward_ref, kf_ref), (backward_ref, kb_ref)):
        out_ref[...] = sum(mm(part, place[...], TN) for part in parts)
    eye = iota((channels, channels), 0) == iota((channels, channels), 1)
    for n, ref in enumerate((bias_ref, gain_ref, off_ref, koff_ref)):
        row = jnp.broadcast_to(ref[...].reshape(1, channels), (channels, channels))
        column = jnp.sum(jnp.where(eye, row, 0.0), axis=1, keepdims=True)
        vec_ref[n] = jnp.broadcast_to(column, (channels, LANES))


def pack_kernel(at_ref, x_hbm, cot_hbm, cot_ref, keep_ref, give_ref, edge_ref, edge_s, x_ref, y_ref, sems):
    colors, file_rows, width = x_ref.shape
    channels, height, _ = cot_ref.shape
    chips, block_rows, _ = keep_ref.shape
    count = width // LANES
    block = colors * file_rows
    core, chip = at_ref[0, 0], at_ref[1, 0]
    load_x = pltpu.make_async_copy(x_hbm, x_ref, sems.at[0])
    load_cot = pltpu.make_async_copy(cot_hbm, cot_ref, sems.at[1])
    load_x.start()
    load_cot.start()
    row, src = iota((block, block), 0), iota((block, block), 1)
    part = sum((row >= colors * n).astype(jnp.int32) for n in range(1, file_rows)) if file_rows > 1 else 0
    move = one_hot(src == (row - colors * part) * file_rows + part)
    load_x.wait()
    y_ref[...] = mm(move, x_ref[...].reshape(block, width)).astype(bf16)

    row, lane = iota((16, LANES), 0), iota((16, LANES), 1)
    pick = one_hot(((row < 3) & (lane == row + LANES - 3)) | ((row >= 11) & (row < 14) & (lane == row - 11)))
    zeros = jnp.zeros((16, block), f32)
    edge_s[0] = zeros
    edge_s[count + 1] = zeros
    for d in range(count):
        tile = y_ref[:, d * LANES:(d + 1) * LANES]
        edge_s[d + 1] = mm(pick, tile, NT)

    def halo(d):
        both = edge_s[d][:8] + edge_s[d + 2][8:]
        chunks = []
        for start in range(0, 2 * LANES, LANES):
            stop = min(start + LANES, block)
            if stop <= start:
                chunks.append(jnp.zeros((8, LANES), f32))
            elif stop - start < LANES:
                chunks.append(jnp.concatenate(
                    [both[:, start:stop], jnp.zeros((8, LANES - stop + start), f32)], axis=1))
            else:
                chunks.append(both[:, start:stop])
        return jnp.concatenate(chunks, axis=0).astype(bf16)

    for away in range(chips):
        there = lax.bitwise_xor(chip, away)
        for other in range(2):
            d = 2 * there + (core if (other == 0) == (away == 0) else 1 - core)
            tile = y_ref[:, pl.ds(pl.multiple_of(d * LANES, LANES), LANES)]
            if other == 0:
                keep_ref[away, :block, :] = tile
                keep_ref[away, block:, :] = halo(d)
            else:
                start = away * block_rows
                give_ref[start:start + block, :] = tile
                give_ref[start + block:start + block_rows, :] = halo(d)

    load_cot.wait()

    row, lane = iota((8, LANES), 0), iota((8, LANES), 1)
    pick = one_hot(((row < 3) & (lane == row)) | ((row >= 3) & (row < 6) & (lane == row + LANES - 6)))
    edges = mm(pick, cot_ref[...].reshape(channels * height, LANES), NT)
    edges = jnp.concatenate(
        [edges[:, n:n + LANES] for n in range(0, channels * height, LANES)], axis=0).astype(bf16)
    edge_ref[:edges.shape[0]] = edges
    edge_ref[edges.shape[0]:] = edges[:edge_ref.shape[0] - edges.shape[0]]
    give_ref[chips * block_rows:, :] = edges


def pair_kernel(keep_ref, got_ref, *pair_refs):
    _, block_rows, _ = keep_ref.shape
    for away, ref in enumerate(pair_refs):
        ref[0] = keep_ref[away]
        ref[1] = got_ref[away * block_rows:(away + 1) * block_rows, :]


def strips_kernel(at_ref, cot_ref, near_ref, far_ref, halo_ref, one_ref, two_ref):
    channels, height, width = cot_ref.shape
    size = channels * height // 16
    core = at_ref[0, 0]
    near = near_ref[near_ref.shape[0] - size:, :].astype(f32)
    far = far_ref[:size, :].astype(f32)
    left = jnp.where(core == 0, far, near)
    right = jnp.where(core == 0, near, far)
    sides = jnp.concatenate(
        [jnp.concatenate([side[n:n + 8] for n in range(0, size, 8)], axis=1) for side in (left, right)], axis=0)
    row, lane = iota((16, width), 0), iota((16, width), 1)
    from_left = (row >= 3) & (row < 6) & (lane == row + width - 6) & (at_ref[4, 0] == 0)
    from_right = (row >= 8) & (row < 11) & (lane == row - 8) & (at_ref[5, 0] == 0)
    halo = mm(sides.astype(bf16), one_hot(from_left | from_right), TN).reshape(channels, height, width)
    halo_ref[...] = halo.astype(bf16)
    write_strips(at_ref, cot_ref[...].astype(f32), halo, one_ref, two_ref)


def write_strips(at_ref, own, halo, one_ref, two_ref):
    channels, height, width = own.shape
    row, lane = iota((8, width), 0), iota((8, width), 1)
    pick = one_hot((lane == row + width - 3) & (row < 3) | (lane == row - 3) & (row >= 3) & (row < 6))
    up, down = own[:, :4], own[:, height - 4:]
    up_halo, down_halo = halo[:, :4], halo[:, height - 4:]
    even = at_ref[6, 0] == 0
    for ref, rows, beside in (
        (one_ref, jnp.where(even, down, up), jnp.where(even, down_halo, up_halo)),
        (two_ref, jnp.where(even, up, down), jnp.where(even, up_halo, down_halo)),
    ):
        ref[:channels] = rows.astype(bf16)
        dense = mm(pick, beside.reshape(channels * 4, width).astype(bf16), NT)
        for n in range(0, channels * 4, LANES):
            for q in range(2):
                ref[channels + n // 64 + q] = dense[4 * q:4 * q + 4, n:n + LANES].astype(bf16)


def read_strips(at_ref, one_ref, two_ref, plane_ref, halo_ref):
    channels, _, width = plane_ref.shape
    even = at_ref[6, 0] == 0
    one, two = one_ref[...].astype(f32), two_ref[...].astype(f32)
    top = jnp.where(at_ref[2, 0] == 0, jnp.where(even, two, one), 0.0)
    bot = jnp.where(at_ref[3, 0] == 0, jnp.where(even, one, two), 0.0)
    row, lane = iota((8, width), 0), iota((8, width), 1)
    place = one_hot((lane == row + width - 3) & (row < 3) | (lane == row - 3) & (row >= 3) & (row < 6))

    def beside(part):
        dense = jnp.concatenate(
            [
                jnp.concatenate([part[channels + n // 64 + q] for q in range(2)], axis=0)
                for n in range(0, channels * 4, LANES)
            ],
            axis=1,
        )
        return mm(dense.astype(bf16), place, TN).reshape(channels, 4, width)

    none = jnp.zeros((channels, 4, width), f32)
    plane_ref[...] = jnp.concatenate([none, top[:channels], bot[:channels], none], axis=1).astype(bf16)
    halo_ref[...] = jnp.concatenate([none, beside(top), beside(bot), none], axis=1).astype(bf16)


def shifted(center, halo):
    rows, width = center.shape
    lane = iota((rows, width), 1)
    copies = []
    for move in range(-3, 4):
        if move == 0:
            copies.append(center)
        elif move > 0:
            copies.append(pltpu.roll(jnp.where(lane < move, halo, center), width - move, 1))
        else:
            copies.append(pltpu.roll(jnp.where(lane >= width + move, halo, center), -move, 1))
    copies.append(jnp.zeros((rows, width), center.dtype))
    return jnp.concatenate(copies, axis=0)


def toeplitz(base, mask):
    return pltpu.roll(jnp.broadcast_to(base, mask.shape), 0, 1, stride=1, stride_axis=0) * mask


def inner_taps(base_ref, k, band_ref):
    inner = band_ref.shape[1]
    base = base_ref[pl.ds(k, 1), :]
    return jnp.concatenate(split2(toeplitz(base[:, :inner], band_ref[...])), axis=0)


def outer_taps(base_ref, k, inner, fringe_ref):
    base = base_ref[pl.ds(k, 1), :]
    above = toeplitz(base[:, inner:inner + OUTER], fringe_ref[:8])
    below = toeplitz(base[:, inner + OUTER:], fringe_ref[8:])
    return jnp.concatenate(split2(jnp.concatenate([above, below], axis=0)), axis=0)


def back_inner_kernel(factor, cot_ref, beside_ref, kb_ref, band_ref, stack_ref, grad_ref, total_ref, sum_ref):
    channels, height, width = cot_ref.shape

    def one(k, carry):
        plane = cot_ref[k]
        stack = shifted(plane, beside_ref[k])
        stack_ref[k] = stack
        both = mm(inner_taps(kb_ref, k, band_ref), stack)
        grad_ref[k] = (both[:height] + both[height:]) * factor
        sum_ref[k] = jnp.sum(plane.astype(f32).reshape(height // 8, 8, width), axis=0)
        return carry

    lax.fori_loop(0, channels, one, 0, unroll=UNROLL)
    total_ref[...] = sum(sum_ref[:, b, :] for b in range(8)) * factor


def back_outer_kernel(factor, at_ref, one_ref, two_ref, grad_ref, kb_ref, fringe_ref,
                      stack_ref, edge_ref, plane_ref, halo_ref):
    channels, height, width = grad_ref.shape
    read_strips(at_ref, one_ref, two_ref, plane_ref, halo_ref)

    def one(k, carry):
        stack = shifted(plane_ref[k], halo_ref[k])
        stack_ref[k] = stack
        both = mm(outer_taps(kb_ref, k, 8 * height, fringe_ref), stack)
        edge = (both[:16] + both[16:]) * factor
        edge_ref[k] = edge + jnp.concatenate([grad_ref[k, :8, :], grad_ref[k, height - 8:, :]], axis=0)
        return carry

    lax.fori_loop(0, channels, one, 0, unroll=UNROLL)


def layer_norm(patch, channels):
    values = patch.astype(bf16).astype(f32).reshape(channels, GROUP, LANES)
    center = values - jnp.mean(values, axis=0, keepdims=True)
    spread = jnp.mean(center * center, axis=0, keepdims=True)
    inverse = lax.rsqrt(spread + norm_eps)
    return center * inverse, inverse


def per_row(vec_ref, n):
    return vec_ref[n][:, None, :]


def order_kernel(at_ref, *refs):
    pair_refs, x_ref = refs[:-1], refs[-1]
    chips = len(pair_refs)
    core, chip = at_ref[0, 0], at_ref[1, 0]
    for away, ref in enumerate(pair_refs):
        there = lax.bitwise_xor(chip, away)
        x_ref[2 * there + core] = ref[0 if away == 0 else 1]
        x_ref[2 * there + 1 - core] = ref[1 if away == 0 else 0]


def main_kernel(colors, file_rows, factor, x_ref, wk_ref, vec_ref, grad_ref, edge_ref, total_ref, stack_ref, rim_ref,
                taps_ref, pick_ref, band_ref, fringe_ref, norm_ref, out_ref, norm_s, grad_s, diag_s):
    channels, height, width = grad_ref.shape
    block = colors * file_rows
    per = GROUP // file_rows
    rows = channels * GROUP
    bias, gain, offset = per_row(vec_ref, 0), per_row(vec_ref, 1), per_row(vec_ref, 2)
    scale_part = jnp.zeros((channels, GROUP, width), f32)
    shift_part = jnp.zeros((channels, GROUP, width), f32)
    inner = 8 * height
    ones = jnp.where(iota((16, width), 0) == 0, 1.0, 0.0).astype(bf16)
    by_color = jnp.zeros((colors + 16, channels), f32)
    for g in range(height // GROUP):
        if g == 0:
            pixels = [[x_ref[per * n + a, :block, :] for a in range(per)] for n in range(height // GROUP)]
            patches = mm(wk_ref[...], jnp.concatenate([jnp.concatenate(x, axis=0) for x in pixels], axis=1))
        blocks = pixels[g]
        patch = patches[:, g * width:(g + 1) * width].reshape(channels, GROUP, width) + bias
        xhat, inverse = layer_norm(patch, channels)
        norm_s[:, g * GROUP:(g + 1) * GROUP, :] = xhat * gain + offset
        if g == 0:
            grad = edge_ref[:, :8, :]
        elif g == height // GROUP - 1:
            grad = edge_ref[:, 8:, :]
        else:
            grad = grad_ref[:, g * GROUP:(g + 1) * GROUP, :]
        scale_part += grad * xhat
        shift_part += grad
        inside = grad * gain
        mean_a = jnp.mean(inside, axis=0, keepdims=True)
        mean_b = jnp.mean(inside * xhat, axis=0, keepdims=True)
        grad_s[g] = (inverse * (inside - mean_a - xhat * mean_b)).reshape(rows, width)
        left, right = [], []
        for h in range(GROUP):
            start = h % file_rows * colors
            left.append(jnp.concatenate([blocks[h // file_rows][start:start + colors], ones], axis=0))
            right.append(grad_s[g, pl.ds(h, channels, stride=GROUP), :].astype(bf16))
        by_color += mm(jnp.concatenate(left, axis=1), jnp.concatenate(right, axis=1), NT)

    band, fringe = band_ref[...], fringe_ref[...]
    none = jnp.zeros((height, width), bf16)

    def one(n, carry):
        planes, stacks = [], []
        for m in range(2):
            k = 2 * n + m
            plane = norm_s[k].astype(bf16)
            norm_ref[k] = plane
            planes.append(jnp.concatenate([plane, none] if m == 0 else [none, plane], axis=1))
            stacks.append(jnp.concatenate([stack_ref[k], rim_ref[k]], axis=0))
        both = mm(jnp.concatenate(planes, axis=0), jnp.concatenate(stacks, axis=1), NT)
        for m in range(2):
            cross = both[m * height:(m + 1) * height, :inner]
            total = cross[:8] * band[:8]
            for a in range(1, height // 8):
                rows = cross[8 * a:8 * a + 8]
                if a == height // 8 - 1:
                    rows = rows * band[8 * a:]
                total += pltpu.roll(rows, inner - 8 * a, 1)
            cross = both[m * height:(m + 1) * height, inner:]
            rim = cross[:8] * fringe[:8] + pltpu.roll(cross[height - 8:] * fringe[8:], 8, 1)
            diag_s[2 * n + m] = jnp.concatenate([total, rim], axis=1)
        return carry

    lax.fori_loop(0, channels // 2, one, 0, unroll=UNROLL // 2)

    line, rim = diag_s[:, 0, :inner], diag_s[:, 0, inner:]
    for b in range(1, 8):
        line += pltpu.roll(diag_s[:, b, :inner], inner - b, 1)
        rim += pltpu.roll(diag_s[:, b, inner:], OUTER - b, 1)
    line = jnp.concatenate([line, rim], axis=1) * factor
    line = jnp.concatenate([jnp.zeros((LANES - channels, line.shape[1]), f32), line], axis=0)
    out_ref[...] = sum(mm(taps_ref[...], part, NT) for part in split2(line))
    parts = jnp.concatenate([jnp.sum(scale_part, axis=1), jnp.sum(shift_part, axis=1), total_ref[...]], axis=1)
    first = sum(mm(pick_ref[...], part, NT) for part in split2(parts))
    out_ref[:, :channels] = first + by_color[:56]


def side_line(pieces, block):
    parts = []
    for piece in pieces:
        piece = piece.astype(f32)
        for start in range(0, block, LANES):
            at = start // LANES * 8
            parts.append(piece[at:at + 8, :min(LANES, block - start)])
    return jnp.concatenate(parts, axis=1)


def stem_side_kernel(colors, file_rows, at_ref, x_ref, norm_ref, wk_ref, vec_ref, halo_ref, one_ref, two_ref):
    channels, height, width = halo_ref.shape
    block = colors * file_rows
    per = GROUP // file_rows
    groups = height // GROUP
    shape = (channels, GROUP, LANES)
    bias, gain, offset = per_row(vec_ref, 0), per_row(vec_ref, 1), per_row(vec_ref, 2)
    lines = [side_line([x_ref[per * g + a, block:block + 16, :] for a in range(per)], block) for g in range(groups)]
    lines.append(jnp.zeros((LANES - 8 * groups, wk_ref.shape[1]), f32))
    lines = jnp.concatenate(lines, axis=0).astype(bf16)
    xhat, _ = layer_norm(mm(wk_ref[...], lines, NT).reshape(shape) + bias, channels)
    column = lax.bitwise_and(iota(shape, 2), 7)
    ok = jnp.where(column < 3, 1 - at_ref[4, 0], 1 - at_ref[5, 0]) > 0
    halo = jnp.where(ok, xhat * gain + offset, 0.0).astype(bf16).reshape(channels * GROUP, LANES)
    for g in range(groups):
        moved = pltpu.roll(halo, width - 8 * g - 3, 1).reshape(channels, GROUP, width)
        halo_ref[:, 8 * g:8 * g + 8, :] = moved
    write_strips(at_ref, norm_ref[...].astype(f32), halo_ref[...].astype(f32), one_ref, two_ref)


def stem_inner_kernel(start, norm_ref, side_ref, kf_ref, vec_ref, band_ref, out_ref):
    count, height, _ = out_ref.shape

    def one(n, carry):
        k = start + n
        both = mm(inner_taps(kf_ref, k, band_ref), shifted(norm_ref[k], side_ref[k]))
        out_ref[n] = both[:height] + both[height:] + vec_ref[3, pl.ds(k, 1), :]
        return carry

    lax.fori_loop(0, count, one, 0, unroll=min(UNROLL, count))


def stem_outer_kernel(parts, at_ref, one_ref, two_ref, kf_ref, fringe_ref, *refs):
    inner_refs, (out_ref, plane_s, halo_s, out_s, sems) = refs[:parts], refs[parts:]
    channels, height, _ = out_s.shape
    read_strips(at_ref, one_ref, two_ref, plane_s, halo_s)
    count = channels // parts
    copies = []
    for part, inner_ref in enumerate(inner_refs):
        def one(n, carry, part=part, inner_ref=inner_ref):
            k = part * count + n
            both = mm(outer_taps(kf_ref, k, 8 * height, fringe_ref), shifted(plane_s[k], halo_s[k]))
            edge = both[:16] + both[16:]
            own = inner_ref[n]
            out_s[k] = jnp.concatenate(
                [own[:8] + edge[:8], own[8:height - 8], own[height - 8:] + edge[8:]], axis=0).astype(bf16)
            return carry

        lax.fori_loop(0, count, one, 0, unroll=min(UNROLL, count))
        here = pl.ds(part * count, count)
        copies.append(pltpu.make_async_copy(out_s.at[here], out_ref.at[here], sems.at[part]))
        copies[-1].start()
    for copy in copies:
        copy.wait()


def last_kernel(colors, *refs):
    parts, outs = refs[:-6], refs[-6:]
    total = sum(part[...] for part in parts)
    channels = outs[1].shape[0]
    first = total[:, :channels]
    second = total[:, channels:2 * channels]
    outs[0][...] = first[:colors]
    for n in range(4):
        outs[1 + n][...] = first[colors + n]
    outs[5][...] = second[:outs[5].shape[0]]


def in_vmem(shape, dtype):
    return pltpu.VMEM(shape, dtype)


def kernel_call(body, out_shape, us, *args, loose=(), **kw):
    loose = tuple(loose) + tuple(kw.get("input_output_aliases", {}))
    args = [
        arg if n in loose else pltpu.with_memory_space_constraint(arg, pltpu.VMEM)
        for n, arg in enumerate(args)
    ]
    return pl.pallas_call(
        body,
        out_shape=out_shape,
        compiler_params=pltpu.CompilerParams(vmem_limit_bytes=VMEM),
        cost_estimate=pl.CostEstimate(flops=int(us * 1e9), bytes_accessed=int(us * 3e6), transcendentals=0),
        **kw,
    )(*args)


def shaped(shape, dtype):
    return jax.ShapeDtypeStruct(shape, dtype)


def pairing(count, odd):
    return [(i, (i + 1 if (i + odd) % 2 == 0 else i - 1) % count) for i in range(count)]


def swap(parts, axis):
    return [lax.ppermute(part, axis, pairing(lax.axis_size(axis), n)) for n, part in enumerate(parts)]


def per_device(
    file_pixels,
    patchify_weight,
    patchify_bias,
    norm_gain,
    norm_offset_vector,
    kernel,
    kernel_offset,
    cotangent,
):
    colors, file_rows, _ = file_pixels.shape
    channels, height, width = cotangent.shape
    n_rows, n_cols = lax.axis_size("rows"), lax.axis_size("cols")
    factor = 1.0 / math.sqrt(height * n_rows * width * n_cols)
    block = colors * file_rows
    per = GROUP // file_rows
    block_rows = block + 16
    rows = channels * GROUP
    tile = (channels, height, width)
    inner = 8 * height
    const = constants(colors, file_rows, channels, height)

    row_at, col_at = lax.axis_index("rows"), lax.axis_index("cols")
    chips = n_cols // 2
    at = (col_at % 2, col_at // 2, row_at == 0, row_at == n_rows - 1, col_at == 0, col_at == n_cols - 1, row_at % 2)
    at = sum(jnp.where(iota((8, LANES), 0) == n, x.astype(jnp.int32), 0) for n, x in enumerate(at))
    vmem = pl.BlockSpec(memory_space=pltpu.VMEM)
    edge_rows = channels * height // 16

    beyond = pl.BlockSpec(memory_space=pl.ANY)
    cot, keep, give, edges = kernel_call(
        pack_kernel,
        (
            in_vmem(tile, bf16),
            in_vmem((chips, block_rows, LANES), bf16),
            in_vmem((chips * block_rows + edge_rows, LANES), bf16),
            in_vmem((edge_rows + 48, LANES), bf16),
        ),
        2,
        at, *(pltpu.with_memory_space_constraint(arg, pltpu.HBM) for arg in (file_pixels, cotangent)),
        loose=(1, 2),
        in_specs=[vmem] + [beyond] * 2,
        scratch_shapes=[
            pltpu.VMEM((n_cols + 2, 16, block), f32),
            pltpu.VMEM(file_pixels.shape, bf16),
            pltpu.VMEM((block, n_cols * LANES), bf16),
            pltpu.SemaphoreType.DMA((2,)),
        ],
    )
    got = lax.ppermute(give, "cols", [(i, i ^ 1) for i in range(n_cols)])
    far = lax.ppermute(edges, "cols", pairing(n_cols, 1))
    pairs = kernel_call(pair_kernel, (in_vmem((2, block_rows, LANES), bf16),) * chips, 0.5, keep, got)
    pairs = [pairs[0]] + [
        lax.ppermute(pairs[n], "cols", [(i, i ^ (2 * n + 1)) for i in range(n_cols)])
        for n in range(1, chips)
    ]

    kept, far = lax.optimization_barrier((pairs[0], far))
    pairs[0] = kept
    beside, *strips = kernel_call(
        strips_kernel,
        (in_vmem(tile, bf16), in_vmem((channels + channels // 16, 4, width), bf16), in_vmem((channels + channels // 16, 4, width), bf16)),
        0.01,
        at, cot, got, far,
        in_specs=[vmem] + [vmem] * 3,
    )
    beside, taps = lax.optimization_barrier((beside, kernel))
    strips = swap(strips, "rows")
    wk, kb, kf, vec = kernel_call(
        params_kernel,
        (
            in_vmem((rows, per * block), bf16),
            in_vmem((channels, inner + 2 * OUTER), f32),
            in_vmem((channels, inner + 2 * OUTER), f32),
            in_vmem((4, channels, LANES), f32),
        ),
        0.01,
        patchify_weight.T, taps.T, patchify_bias, norm_gain, norm_offset_vector, kernel_offset,
        const["spread"], const["keep"], const["tall"], const["forward"], const["backward"],
    )
    stack, grad, total = kernel_call(
        functools.partial(back_inner_kernel, factor),
        (in_vmem((channels, inner, width), bf16), in_vmem(tile, f32), in_vmem((channels, width), f32)),
        0.01,
        cot, beside, kb, const["band"],
        scratch_shapes=[pltpu.VMEM((channels, 8, width), f32)],
    )
    rim, edge = kernel_call(
        functools.partial(back_outer_kernel, factor),
        (in_vmem((channels, OUTER, width), bf16), in_vmem((channels, 16, width), f32)),
        0.01,
        at, *strips, grad, kb, const["fringe"],
        scratch_shapes=[pltpu.VMEM((channels, 16, width), bf16)] * 2,
    )

    edge, *pairs = lax.optimization_barrier((edge, *pairs))
    pixels = kernel_call(order_kernel, in_vmem((n_cols, block_rows, LANES), bf16), 0.01, at, *pairs)
    norm, result = kernel_call(
        functools.partial(main_kernel, colors, file_rows, factor),
        (in_vmem(tile, bf16), in_vmem((56, LANES), f32)),
        6,
        pixels, wk, vec, grad, edge, total, stack, rim, const["taps"], const["pick"], const["band"], const["fringe"],
        scratch_shapes=[
            pltpu.VMEM(tile, f32),
            pltpu.VMEM((height // GROUP, rows, width), f32),
            pltpu.VMEM((channels, 8, inner + OUTER), f32),
        ],
    )

    size = n_rows * n_cols
    chunk = channels // 2
    stages = [[1], [3, 5, 7], [9, 17, 25]]
    jobs = {0: ["side"], 1: ["one", "two", 0], 2: [1, "outer"]}
    parts = []
    for n, steps in enumerate(stages):
        others = [lax.ppermute(result, ("rows", "cols"), [(i, i ^ step) for i in range(size)]) for step in steps]
        for job in jobs.get(n, []):
            if job in ("one", "two"):
                which = ("one", "two").index(job)
                result, end = lax.optimization_barrier((result, ends[which]))
                ends[which] = lax.ppermute(end, "rows", pairing(n_rows, which))
            elif job == "side":
                result, norm = lax.optimization_barrier((result, norm))
                beside, *ends = kernel_call(
                    functools.partial(stem_side_kernel, colors, file_rows),
                    (in_vmem(tile, bf16),) + (in_vmem((channels + channels // 16, 4, width), bf16),) * 2,
                    1,
                    at, pixels, norm, wk, vec,
                )
                result, beside = lax.optimization_barrier((result, beside))
            elif job == "outer":
                result, *parts = lax.optimization_barrier((result, *parts))
                stem_output = kernel_call(
                    functools.partial(stem_outer_kernel, len(parts)),
                    shaped(tile, bf16),
                    3,
                    at, *ends, kf, const["fringe"], *parts,
                    in_specs=[vmem] * (5 + len(parts)),
                    out_specs=beyond,
                    scratch_shapes=[
                        pltpu.VMEM((channels, 16, width), bf16),
                        pltpu.VMEM((channels, 16, width), bf16),
                        pltpu.VMEM(tile, bf16),
                        pltpu.SemaphoreType.DMA((len(parts),)),
                    ],
                )
                result, stem_output = lax.optimization_barrier((result, stem_output))
            else:
                result, norm = lax.optimization_barrier((result, norm))
                part = kernel_call(
                    functools.partial(stem_inner_kernel, job * chunk),
                    in_vmem((chunk, height, width), f32),
                    2,
                    norm, beside, kf, vec, const["band"],
                )
                result, part = lax.optimization_barrier((result, part))
                parts.append(part)
        if n < len(stages) - 1:
            result = sum(others, result)

    taps = side * side
    outs = kernel_call(
        functools.partial(last_kernel, colors),
        (shaped((colors, channels), f32),) + (shaped((channels,), f32),) * 4 + (shaped((taps, channels), f32),),
        1,
        result, *others,
    )
    return (stem_output, outs[0].T, outs[1], outs[2], outs[3], outs[5].T, outs[4])


def solution(mesh):
    return jax.shard_map(
        per_device,
        mesh=mesh,
        in_specs=(
            P(None, ("rows", "cols"), None),
            P(),
            P(),
            P(),
            P(),
            P(),
            P(),
            P(None, "rows", "cols"),
        ),
        out_specs=(P(None, "rows", "cols"), P(), P(), P(), P(), P(), P()),
        check_vma=False,
    )
```

```python
import functools
import math

import jax
import jax.numpy as jnp
import numpy as np
from jax import lax
from jax.experimental import pallas as pl
from jax.experimental.pallas import tpu as pltpu
from jax.sharding import PartitionSpec as P

norm_eps = 1e-06
side = 7
LANES = 128
GROUP = 8
OUTER = 8 * 16
VMEM = 20 * 1024 * 1024
UNROLL = 64
bf16, f32 = jnp.bfloat16, jnp.float32

NN = (((1,), (0,)), ((), ()))
NT = (((1,), (1,)), ((), ()))
TN = (((0,), (0,)), ((), ()))


def mm(a, b, dims=NN):
    return lax.dot_general(a, b, dims, preferred_element_type=f32)


def iota(shape, axis):
    return lax.broadcasted_iota(jnp.int32, shape, axis)


def split2(x):
    high = x.astype(bf16)
    return high, (x - high.astype(f32)).astype(bf16)


def one_hot(cond):
    return jnp.where(cond, 1.0, 0.0).astype(bf16)


def cdiv(a, b):
    return -(-a // b)


def constants(colors, file_rows, channels, height):
    block = colors * file_rows
    per = GROUP // file_rows
    rows = channels * GROUP
    out = {}
    at = np.arange(per * block)
    out["spread"] = (at % colors)[None, :] == np.arange(colors)[:, None]
    out["keep"] = (at // colors)[None, :] == (np.arange(rows) % GROUP)[:, None]
    out["tall"] = (np.arange(rows) // GROUP)[:, None] == np.arange(channels)[None, :]
    inner = 8 * height
    count = side * side
    forward = np.zeros((count, inner + 2 * OUTER), bool)
    taps = np.zeros((56, inner + OUTER), bool)
    for tap in range(count):
        down, copy = divmod(tap, side)
        own, above, below = height * copy + down - 3, 16 * copy + down + 5, 16 * copy + down - 3
        forward[tap, own % inner] = True
        forward[tap, inner + above] = True
        forward[tap, inner + OUTER + below % OUTER] = True
        taps[count - 1 - tap, own % inner] = True
        taps[count - 1 - tap, inner + above] = True
    out["forward"], out["backward"], out["taps"] = forward, forward[::-1], taps
    lane, row = np.arange(inner)[None, :], np.arange(height)[:, None]
    out["band"] = (abs(lane % height - row) <= 3) & (lane < height * side)
    lane, row = np.arange(OUTER)[None, :], np.arange(8)[:, None]
    at = lane % 16
    out["fringe"] = np.concatenate([(at < 8) & (at >= row + 5), (at >= 8) & (at <= row + 3)]) & (lane < 16 * side)
    pick = np.zeros((3, 56, LANES), bool)
    for n in range(3):
        pick[n, colors + 1 + n] = True
    out["pick"] = np.concatenate(list(pick), axis=1)
    return {k: jnp.asarray(v, f32 if k in ("band", "fringe") else bf16) for k, v in out.items()}


def params_kernel(wt_ref, taps_ref, bias_ref, gain_ref, off_ref, koff_ref, spread_ref, keep_ref, tall_ref, forward_ref,
                  backward_ref, wk_ref, kb_ref, kf_ref, vec_ref):
    channels = wt_ref.shape[1]
    wide = mm(wt_ref[...], spread_ref[...], TN).astype(bf16)
    wk_ref[...] = mm(tall_ref[...], wide).astype(bf16) * keep_ref[...]
    parts = split2(taps_ref[...])
    for place, out_ref in ((forward_ref, kf_ref), (backward_ref, kb_ref)):
        out_ref[...] = sum(mm(part, place[...], TN) for part in parts)
    eye = iota((channels, channels), 0) == iota((channels, channels), 1)
    for n, ref in enumerate((bias_ref, gain_ref, off_ref, koff_ref)):
        row = jnp.broadcast_to(ref[...].reshape(1, channels), (channels, channels))
        column = jnp.sum(jnp.where(eye, row, 0.0), axis=1, keepdims=True)
        vec_ref[n] = jnp.broadcast_to(column, (channels, LANES))


def pack_kernel(at_ref, x_hbm, cot_hbm, cot_ref, keep_ref, give_ref, edge_ref, edge_s, x_ref, y_ref, sems):
    colors, file_rows, width = x_ref.shape
    channels, height, _ = cot_ref.shape
    chips, block_rows, _ = keep_ref.shape
    count = width // LANES
    block = colors * file_rows
    core, chip = at_ref[0, 0], at_ref[1, 0]
    load_x = pltpu.make_async_copy(x_hbm, x_ref, sems.at[0])
    load_cot = pltpu.make_async_copy(cot_hbm, cot_ref, sems.at[1])
    load_x.start()
    load_cot.start()
    row, src = iota((block, block), 0), iota((block, block), 1)
    part = sum((row >= colors * n).astype(jnp.int32) for n in range(1, file_rows)) if file_rows > 1 else 0
    move = one_hot(src == (row - colors * part) * file_rows + part)
    load_x.wait()
    y_ref[...] = mm(move, x_ref[...].reshape(block, width)).astype(bf16)

    row, lane = iota((16, LANES), 0), iota((16, LANES), 1)
    pick = one_hot(((row < 3) & (lane == row + LANES - 3)) | ((row >= 11) & (row < 14) & (lane == row - 11)))
    zeros = jnp.zeros((16, block), f32)
    edge_s[0] = zeros
    edge_s[count + 1] = zeros
    for d in range(count):
        tile = y_ref[:, d * LANES:(d + 1) * LANES]
        edge_s[d + 1] = mm(pick, tile, NT)

    def halo(d):
        both = edge_s[d][:8] + edge_s[d + 2][8:]
        chunks = []
        for start in range(0, 2 * LANES, LANES):
            stop = min(start + LANES, block)
            if stop <= start:
                chunks.append(jnp.zeros((8, LANES), f32))
            elif stop - start < LANES:
                chunks.append(jnp.concatenate(
                    [both[:, start:stop], jnp.zeros((8, LANES - stop + start), f32)], axis=1))
            else:
                chunks.append(both[:, start:stop])
        return jnp.concatenate(chunks, axis=0).astype(bf16)

    for away in range(chips):
        there = lax.bitwise_xor(chip, away)
        for other in range(2):
            d = 2 * there + (core if (other == 0) == (away == 0) else 1 - core)
            tile = y_ref[:, pl.ds(pl.multiple_of(d * LANES, LANES), LANES)]
            if other == 0:
                keep_ref[away, :block, :] = tile
                keep_ref[away, block:, :] = halo(d)
            else:
                start = away * block_rows
                give_ref[start:start + block, :] = tile
                give_ref[start + block:start + block_rows, :] = halo(d)

    load_cot.wait()

    row, lane = iota((8, LANES), 0), iota((8, LANES), 1)
    pick = one_hot(((row < 3) & (lane == row)) | ((row >= 3) & (row < 6) & (lane == row + LANES - 6)))
    edges = mm(pick, cot_ref[...].reshape(channels * height, LANES), NT)
    edges = jnp.concatenate(
        [edges[:, n:n + LANES] for n in range(0, channels * height, LANES)], axis=0).astype(bf16)
    edge_ref[:edges.shape[0]] = edges
    edge_ref[edges.shape[0]:] = edges[:edge_ref.shape[0] - edges.shape[0]]
    give_ref[chips * block_rows:, :] = edges


def pair_kernel(keep_ref, got_ref, *pair_refs):
    _, block_rows, _ = keep_ref.shape
    for away, ref in enumerate(pair_refs):
        ref[0] = keep_ref[away]
        ref[1] = got_ref[away * block_rows:(away + 1) * block_rows, :]


def strips_kernel(at_ref, cot_ref, near_ref, far_ref, halo_ref, one_ref, two_ref):
    channels, height, width = cot_ref.shape
    size = channels * height // 16
    core = at_ref[0, 0]
    near = near_ref[near_ref.shape[0] - size:, :].astype(f32)
    far = far_ref[:size, :].astype(f32)
    left = jnp.where(core == 0, far, near)
    right = jnp.where(core == 0, near, far)
    sides = jnp.concatenate(
        [jnp.concatenate([side[n:n + 8] for n in range(0, size, 8)], axis=1) for side in (left, right)], axis=0)
    row, lane = iota((16, width), 0), iota((16, width), 1)
    from_left = (row >= 3) & (row < 6) & (lane == row + width - 6) & (at_ref[4, 0] == 0)
    from_right = (row >= 8) & (row < 11) & (lane == row - 8) & (at_ref[5, 0] == 0)
    halo = mm(sides.astype(bf16), one_hot(from_left | from_right), TN).reshape(channels, height, width)
    halo_ref[...] = halo.astype(bf16)
    write_strips(at_ref, cot_ref[...].astype(f32), halo, one_ref, two_ref)


def write_strips(at_ref, own, halo, one_ref, two_ref):
    channels, height, width = own.shape
    row, lane = iota((8, width), 0), iota((8, width), 1)
    pick = one_hot((lane == row + width - 3) & (row < 3) | (lane == row - 3) & (row >= 3) & (row < 6))
    up, down = own[:, :4], own[:, height - 4:]
    up_halo, down_halo = halo[:, :4], halo[:, height - 4:]
    even = at_ref[6, 0] == 0
    for ref, rows, beside in (
        (one_ref, jnp.where(even, down, up), jnp.where(even, down_halo, up_halo)),
        (two_ref, jnp.where(even, up, down), jnp.where(even, up_halo, down_halo)),
    ):
        ref[:channels] = rows.astype(bf16)
        dense = mm(pick, beside.reshape(channels * 4, width).astype(bf16), NT)
        for n in range(0, channels * 4, LANES):
            for q in range(2):
                ref[channels + n // 64 + q] = dense[4 * q:4 * q + 4, n:n + LANES].astype(bf16)


def read_strips(at_ref, one_ref, two_ref, plane_ref, halo_ref):
    channels, _, width = plane_ref.shape
    even = at_ref[6, 0] == 0
    one, two = one_ref[...].astype(f32), two_ref[...].astype(f32)
    top = jnp.where(at_ref[2, 0] == 0, jnp.where(even, two, one), 0.0)
    bot = jnp.where(at_ref[3, 0] == 0, jnp.where(even, one, two), 0.0)
    row, lane = iota((8, width), 0), iota((8, width), 1)
    place = one_hot((lane == row + width - 3) & (row < 3) | (lane == row - 3) & (row >= 3) & (row < 6))

    def beside(part):
        dense = jnp.concatenate(
            [
                jnp.concatenate([part[channels + n // 64 + q] for q in range(2)], axis=0)
                for n in range(0, channels * 4, LANES)
            ],
            axis=1,
        )
        return mm(dense.astype(bf16), place, TN).reshape(channels, 4, width)

    none = jnp.zeros((channels, 4, width), f32)
    plane_ref[...] = jnp.concatenate([none, top[:channels], bot[:channels], none], axis=1).astype(bf16)
    halo_ref[...] = jnp.concatenate([none, beside(top), beside(bot), none], axis=1).astype(bf16)


def shifted(center, halo):
    rows, width = center.shape
    lane = iota((rows, width), 1)
    copies = []
    for move in range(-3, 4):
        if move == 0:
            copies.append(center)
        elif move > 0:
            copies.append(pltpu.roll(jnp.where(lane < move, halo, center), width - move, 1))
        else:
            copies.append(pltpu.roll(jnp.where(lane >= width + move, halo, center), -move, 1))
    copies.append(jnp.zeros((rows, width), center.dtype))
    return jnp.concatenate(copies, axis=0)


def toeplitz(base, mask):
    return pltpu.roll(jnp.broadcast_to(base, mask.shape), 0, 1, stride=1, stride_axis=0) * mask


def inner_taps(base_ref, k, band_ref):
    inner = band_ref.shape[1]
    base = base_ref[pl.ds(k, 1), :]
    return jnp.concatenate(split2(toeplitz(base[:, :inner], band_ref[...])), axis=0)


def outer_taps(base_ref, k, inner, fringe_ref):
    base = base_ref[pl.ds(k, 1), :]
    above = toeplitz(base[:, inner:inner + OUTER], fringe_ref[:8])
    below = toeplitz(base[:, inner + OUTER:], fringe_ref[8:])
    return jnp.concatenate(split2(jnp.concatenate([above, below], axis=0)), axis=0)


def back_inner_kernel(factor, cot_ref, beside_ref, kb_ref, band_ref, stack_ref, grad_ref, total_ref, sum_ref):
    channels, height, width = cot_ref.shape

    def one(k, carry):
        plane = cot_ref[k]
        stack = shifted(plane, beside_ref[k])
        stack_ref[k] = stack
        both = mm(inner_taps(kb_ref, k, band_ref), stack)
        grad_ref[k] = (both[:height] + both[height:]) * factor
        sum_ref[k] = jnp.sum(plane.astype(f32).reshape(height // 8, 8, width), axis=0)
        return carry

    lax.fori_loop(0, channels, one, 0, unroll=UNROLL)
    total_ref[...] = sum(sum_ref[:, b, :] for b in range(8)) * factor


def back_outer_kernel(factor, at_ref, one_ref, two_ref, grad_ref, kb_ref, fringe_ref,
                      stack_ref, edge_ref, plane_ref, halo_ref):
    channels, height, width = grad_ref.shape
    read_strips(at_ref, one_ref, two_ref, plane_ref, halo_ref)

    def one(k, carry):
        stack = shifted(plane_ref[k], halo_ref[k])
        stack_ref[k] = stack
        both = mm(outer_taps(kb_ref, k, 8 * height, fringe_ref), stack)
        edge = (both[:16] + both[16:]) * factor
        edge_ref[k] = edge + jnp.concatenate([grad_ref[k, :8, :], grad_ref[k, height - 8:, :]], axis=0)
        return carry

    lax.fori_loop(0, channels, one, 0, unroll=UNROLL)


def layer_norm(patch, channels):
    values = patch.astype(bf16).astype(f32).reshape(channels, GROUP, LANES)
    center = values - jnp.mean(values, axis=0, keepdims=True)
    spread = jnp.mean(center * center, axis=0, keepdims=True)
    inverse = lax.rsqrt(spread + norm_eps)
    return center * inverse, inverse


def per_row(vec_ref, n):
    return vec_ref[n][:, None, :]


def order_kernel(at_ref, *refs):
    pair_refs, x_ref = refs[:-1], refs[-1]
    chips = len(pair_refs)
    core, chip = at_ref[0, 0], at_ref[1, 0]
    for away, ref in enumerate(pair_refs):
        there = lax.bitwise_xor(chip, away)
        x_ref[2 * there + core] = ref[0 if away == 0 else 1]
        x_ref[2 * there + 1 - core] = ref[1 if away == 0 else 0]


def main_kernel(colors, file_rows, factor, x_ref, wk_ref, vec_ref, grad_ref, edge_ref, total_ref, stack_ref, rim_ref,
                taps_ref, pick_ref, band_ref, fringe_ref, norm_ref, out_ref, norm_s, grad_s, diag_s):
    channels, height, width = grad_ref.shape
    block = colors * file_rows
    per = GROUP // file_rows
    rows = channels * GROUP
    bias, gain, offset = per_row(vec_ref, 0), per_row(vec_ref, 1), per_row(vec_ref, 2)
    scale_part = jnp.zeros((channels, GROUP, width), f32)
    shift_part = jnp.zeros((channels, GROUP, width), f32)
    inner = 8 * height
    ones = jnp.where(iota((16, width), 0) == 0, 1.0, 0.0).astype(bf16)
    by_color = jnp.zeros((colors + 16, channels), f32)
    for g in range(height // GROUP):
        if g == 0:
            pixels = [[x_ref[per * n + a, :block, :] for a in range(per)] for n in range(height // GROUP)]
            patches = mm(wk_ref[...], jnp.concatenate([jnp.concatenate(x, axis=0) for x in pixels], axis=1))
        blocks = pixels[g]
        patch = patches[:, g * width:(g + 1) * width].reshape(channels, GROUP, width) + bias
        xhat, inverse = layer_norm(patch, channels)
        norm_s[:, g * GROUP:(g + 1) * GROUP, :] = xhat * gain + offset
        if g == 0:
            grad = edge_ref[:, :8, :]
        elif g == height // GROUP - 1:
            grad = edge_ref[:, 8:, :]
        else:
            grad = grad_ref[:, g * GROUP:(g + 1) * GROUP, :]
        scale_part += grad * xhat
        shift_part += grad
        inside = grad * gain
        mean_a = jnp.mean(inside, axis=0, keepdims=True)
        mean_b = jnp.mean(inside * xhat, axis=0, keepdims=True)
        grad_s[g] = (inverse * (inside - mean_a - xhat * mean_b)).reshape(rows, width)
        left, right = [], []
        for h in range(GROUP):
            start = h % file_rows * colors
            left.append(jnp.concatenate([blocks[h // file_rows][start:start + colors], ones], axis=0))
            right.append(grad_s[g, pl.ds(h, channels, stride=GROUP), :].astype(bf16))
        by_color += mm(jnp.concatenate(left, axis=1), jnp.concatenate(right, axis=1), NT)

    band, fringe = band_ref[...], fringe_ref[...]
    none = jnp.zeros((height, width), bf16)

    def one(n, carry):
        planes, stacks = [], []
        for m in range(2):
            k = 2 * n + m
            plane = norm_s[k].astype(bf16)
            norm_ref[k] = plane
            planes.append(jnp.concatenate([plane, none] if m == 0 else [none, plane], axis=1))
            stacks.append(jnp.concatenate([stack_ref[k], rim_ref[k]], axis=0))
        both = mm(jnp.concatenate(planes, axis=0), jnp.concatenate(stacks, axis=1), NT)
        for m in range(2):
            cross = both[m * height:(m + 1) * height, :inner]
            total = cross[:8] * band[:8]
            for a in range(1, height // 8):
                rows = cross[8 * a:8 * a + 8]
                if a == height // 8 - 1:
                    rows = rows * band[8 * a:]
                total += pltpu.roll(rows, inner - 8 * a, 1)
            cross = both[m * height:(m + 1) * height, inner:]
            rim = cross[:8] * fringe[:8] + pltpu.roll(cross[height - 8:] * fringe[8:], 8, 1)
            diag_s[2 * n + m] = jnp.concatenate([total, rim], axis=1)
        return carry

    lax.fori_loop(0, channels // 2, one, 0, unroll=UNROLL // 2)

    line, rim = diag_s[:, 0, :inner], diag_s[:, 0, inner:]
    for b in range(1, 8):
        line += pltpu.roll(diag_s[:, b, :inner], inner - b, 1)
        rim += pltpu.roll(diag_s[:, b, inner:], OUTER - b, 1)
    line = jnp.concatenate([line, rim], axis=1) * factor
    line = jnp.concatenate([jnp.zeros((LANES - channels, line.shape[1]), f32), line], axis=0)
    out_ref[...] = sum(mm(taps_ref[...], part, NT) for part in split2(line))
    parts = jnp.concatenate([jnp.sum(scale_part, axis=1), jnp.sum(shift_part, axis=1), total_ref[...]], axis=1)
    first = sum(mm(pick_ref[...], part, NT) for part in split2(parts))
    out_ref[:, :channels] = first + by_color[:56]


def side_line(pieces, block):
    parts = []
    for piece in pieces:
        piece = piece.astype(f32)
        for start in range(0, block, LANES):
            at = start // LANES * 8
            parts.append(piece[at:at + 8, :min(LANES, block - start)])
    return jnp.concatenate(parts, axis=1)


def stem_side_kernel(colors, file_rows, at_ref, x_ref, norm_ref, wk_ref, vec_ref, halo_ref, one_ref, two_ref):
    channels, height, width = halo_ref.shape
    block = colors * file_rows
    per = GROUP // file_rows
    groups = height // GROUP
    shape = (channels, GROUP, LANES)
    bias, gain, offset = per_row(vec_ref, 0), per_row(vec_ref, 1), per_row(vec_ref, 2)
    lines = [side_line([x_ref[per * g + a, block:block + 16, :] for a in range(per)], block) for g in range(groups)]
    lines.append(jnp.zeros((LANES - 8 * groups, wk_ref.shape[1]), f32))
    lines = jnp.concatenate(lines, axis=0).astype(bf16)
    xhat, _ = layer_norm(mm(wk_ref[...], lines, NT).reshape(shape) + bias, channels)
    column = lax.bitwise_and(iota(shape, 2), 7)
    ok = jnp.where(column < 3, 1 - at_ref[4, 0], 1 - at_ref[5, 0]) > 0
    halo = jnp.where(ok, xhat * gain + offset, 0.0).astype(bf16).reshape(channels * GROUP, LANES)
    for g in range(groups):
        moved = pltpu.roll(halo, width - 8 * g - 3, 1).reshape(channels, GROUP, width)
        halo_ref[:, 8 * g:8 * g + 8, :] = moved
    write_strips(at_ref, norm_ref[...].astype(f32), halo_ref[...].astype(f32), one_ref, two_ref)


def stem_inner_kernel(start, norm_ref, side_ref, kf_ref, vec_ref, band_ref, out_ref):
    count, height, _ = out_ref.shape

    def one(n, carry):
        k = start + n
        both = mm(inner_taps(kf_ref, k, band_ref), shifted(norm_ref[k], side_ref[k]))
        out_ref[n] = both[:height] + both[height:] + vec_ref[3, pl.ds(k, 1), :]
        return carry

    lax.fori_loop(0, count, one, 0, unroll=min(UNROLL, count))


def stem_outer_kernel(at_ref, one_ref, two_ref, norm_ref, side_ref, kf_ref, vec_ref, band_ref, fringe_ref, inner_ref,
                      out_ref, plane_s, halo_s, out_s, sems):
    channels, height, _ = out_s.shape
    done = inner_ref.shape[0]
    read_strips(at_ref, one_ref, two_ref, plane_s, halo_s)

    def one(k, own):
        both = mm(outer_taps(kf_ref, k, 8 * height, fringe_ref), shifted(plane_s[k], halo_s[k]))
        edge = both[:16] + both[16:]
        out_s[k] = jnp.concatenate(
            [own[:8] + edge[:8], own[8:height - 8], own[height - 8:] + edge[8:]], axis=0).astype(bf16)

    def first(k, carry):
        one(k, inner_ref[k])
        return carry

    def second(n, carry):
        k = done + n
        both = mm(inner_taps(kf_ref, k, band_ref), shifted(norm_ref[k], side_ref[k]))
        one(k, both[:height] + both[height:] + vec_ref[3, pl.ds(k, 1), :])
        return carry

    copies = []
    for start, count, body in ((0, done, first), (done, channels - done, second)):
        lax.fori_loop(0, count, body, 0, unroll=min(UNROLL, count))
        here = pl.ds(start, count)
        copies.append(pltpu.make_async_copy(out_s.at[here], out_ref.at[here], sems.at[len(copies)]))
        copies[-1].start()
    for copy in copies:
        copy.wait()


def last_kernel(colors, *refs):
    parts, outs = refs[:-6], refs[-6:]
    total = sum(part[...] for part in parts)
    channels = outs[1].shape[0]
    first = total[:, :channels]
    second = total[:, channels:2 * channels]
    outs[0][...] = first[:colors]
    for n in range(4):
        outs[1 + n][...] = first[colors + n]
    outs[5][...] = second[:outs[5].shape[0]]


def in_vmem(shape, dtype):
    return pltpu.VMEM(shape, dtype)


def kernel_call(body, out_shape, us, *args, loose=(), **kw):
    loose = tuple(loose) + tuple(kw.get("input_output_aliases", {}))
    args = [
        arg if n in loose else pltpu.with_memory_space_constraint(arg, pltpu.VMEM)
        for n, arg in enumerate(args)
    ]
    return pl.pallas_call(
        body,
        out_shape=out_shape,
        compiler_params=pltpu.CompilerParams(vmem_limit_bytes=VMEM),
        cost_estimate=pl.CostEstimate(flops=int(us * 1e9), bytes_accessed=int(us * 3e6), transcendentals=0),
        **kw,
    )(*args)


def shaped(shape, dtype):
    return jax.ShapeDtypeStruct(shape, dtype)


def pairing(count, odd):
    return [(i, (i + 1 if (i + odd) % 2 == 0 else i - 1) % count) for i in range(count)]


def swap(parts, axis):
    return [lax.ppermute(part, axis, pairing(lax.axis_size(axis), n)) for n, part in enumerate(parts)]


def per_device(
    file_pixels,
    patchify_weight,
    patchify_bias,
    norm_gain,
    norm_offset_vector,
    kernel,
    kernel_offset,
    cotangent,
):
    colors, file_rows, _ = file_pixels.shape
    channels, height, width = cotangent.shape
    n_rows, n_cols = lax.axis_size("rows"), lax.axis_size("cols")
    factor = 1.0 / math.sqrt(height * n_rows * width * n_cols)
    block = colors * file_rows
    per = GROUP // file_rows
    block_rows = block + 16
    rows = channels * GROUP
    tile = (channels, height, width)
    inner = 8 * height
    const = constants(colors, file_rows, channels, height)

    row_at, col_at = lax.axis_index("rows"), lax.axis_index("cols")
    chips = n_cols // 2
    at = (col_at % 2, col_at // 2, row_at == 0, row_at == n_rows - 1, col_at == 0, col_at == n_cols - 1, row_at % 2)
    at = sum(jnp.where(iota((8, LANES), 0) == n, x.astype(jnp.int32), 0) for n, x in enumerate(at))
    vmem = pl.BlockSpec(memory_space=pltpu.VMEM)
    edge_rows = channels * height // 16

    beyond = pl.BlockSpec(memory_space=pl.ANY)
    cot, keep, give, edges = kernel_call(
        pack_kernel,
        (
            in_vmem(tile, bf16),
            in_vmem((chips, block_rows, LANES), bf16),
            in_vmem((chips * block_rows + edge_rows, LANES), bf16),
            in_vmem((edge_rows + 48, LANES), bf16),
        ),
        2,
        at, *(pltpu.with_memory_space_constraint(arg, pltpu.HBM) for arg in (file_pixels, cotangent)),
        loose=(1, 2),
        in_specs=[vmem] + [beyond] * 2,
        scratch_shapes=[
            pltpu.VMEM((n_cols + 2, 16, block), f32),
            pltpu.VMEM(file_pixels.shape, bf16),
            pltpu.VMEM((block, n_cols * LANES), bf16),
            pltpu.SemaphoreType.DMA((2,)),
        ],
    )
    got = lax.ppermute(give, "cols", [(i, i ^ 1) for i in range(n_cols)])
    far = lax.ppermute(edges, "cols", pairing(n_cols, 1))
    pairs = kernel_call(pair_kernel, (in_vmem((2, block_rows, LANES), bf16),) * chips, 0.5, keep, got)
    pairs = [pairs[0]] + [
        lax.ppermute(pairs[n], "cols", [(i, i ^ (2 * n + 1)) for i in range(n_cols)])
        for n in range(1, chips)
    ]

    kept, far = lax.optimization_barrier((pairs[0], far))
    pairs[0] = kept
    beside, *strips = kernel_call(
        strips_kernel,
        (in_vmem(tile, bf16), in_vmem((channels + channels // 16, 4, width), bf16), in_vmem((channels + channels // 16, 4, width), bf16)),
        0.01,
        at, cot, got, far,
        in_specs=[vmem] + [vmem] * 3,
    )
    beside, taps = lax.optimization_barrier((beside, kernel))
    strips = swap(strips, "rows")
    wk, kb, kf, vec = kernel_call(
        params_kernel,
        (
            in_vmem((rows, per * block), bf16),
            in_vmem((channels, inner + 2 * OUTER), f32),
            in_vmem((channels, inner + 2 * OUTER), f32),
            in_vmem((4, channels, LANES), f32),
        ),
        0.01,
        patchify_weight.T, taps.T, patchify_bias, norm_gain, norm_offset_vector, kernel_offset,
        const["spread"], const["keep"], const["tall"], const["forward"], const["backward"],
    )
    stack, grad, total = kernel_call(
        functools.partial(back_inner_kernel, factor),
        (in_vmem((channels, inner, width), bf16), in_vmem(tile, f32), in_vmem((channels, width), f32)),
        0.01,
        cot, beside, kb, const["band"],
        scratch_shapes=[pltpu.VMEM((channels, 8, width), f32)],
    )
    rim, edge = kernel_call(
        functools.partial(back_outer_kernel, factor),
        (in_vmem((channels, OUTER, width), bf16), in_vmem((channels, 16, width), f32)),
        0.01,
        at, *strips, grad, kb, const["fringe"],
        scratch_shapes=[pltpu.VMEM((channels, 16, width), bf16)] * 2,
    )

    edge, *pairs = lax.optimization_barrier((edge, *pairs))
    pixels = kernel_call(order_kernel, in_vmem((n_cols, block_rows, LANES), bf16), 0.01, at, *pairs)
    norm, result = kernel_call(
        functools.partial(main_kernel, colors, file_rows, factor),
        (in_vmem(tile, bf16), in_vmem((56, LANES), f32)),
        6,
        pixels, wk, vec, grad, edge, total, stack, rim, const["taps"], const["pick"], const["band"], const["fringe"],
        scratch_shapes=[
            pltpu.VMEM(tile, f32),
            pltpu.VMEM((height // GROUP, rows, width), f32),
            pltpu.VMEM((channels, 8, inner + OUTER), f32),
        ],
    )

    size = n_rows * n_cols
    chunk = channels // 4
    stages = [[1], [3, 5, 7], [9, 17, 25]]
    jobs = {0: ["side"], 1: ["one", "two", 0], 2: ["outer"]}
    parts = []
    for n, steps in enumerate(stages):
        others = [lax.ppermute(result, ("rows", "cols"), [(i, i ^ step) for i in range(size)]) for step in steps]
        for job in jobs.get(n, []):
            if job in ("one", "two"):
                which = ("one", "two").index(job)
                result, end = lax.optimization_barrier((result, ends[which]))
                ends[which] = lax.ppermute(end, "rows", pairing(n_rows, which))
            elif job == "side":
                result, norm = lax.optimization_barrier((result, norm))
                beside, *ends = kernel_call(
                    functools.partial(stem_side_kernel, colors, file_rows),
                    (in_vmem(tile, bf16),) + (in_vmem((channels + channels // 16, 4, width), bf16),) * 2,
                    1,
                    at, pixels, norm, wk, vec,
                )
                result, beside = lax.optimization_barrier((result, beside))
            elif job == "outer":
                result, *parts = lax.optimization_barrier((result, *parts))
                stem_output = kernel_call(
                    stem_outer_kernel,
                    shaped(tile, bf16),
                    3,
                    at, *ends, norm, beside, kf, vec, const["band"], const["fringe"], *parts,
                    in_specs=[vmem] * 10,
                    out_specs=beyond,
                    scratch_shapes=[
                        pltpu.VMEM((channels, 16, width), bf16),
                        pltpu.VMEM((channels, 16, width), bf16),
                        pltpu.VMEM(tile, bf16),
                        pltpu.SemaphoreType.DMA((2,)),
                    ],
                )
                result, stem_output = lax.optimization_barrier((result, stem_output))
            else:
                result, norm = lax.optimization_barrier((result, norm))
                part = kernel_call(
                    functools.partial(stem_inner_kernel, job * chunk),
                    in_vmem((chunk, height, width), f32),
                    2,
                    norm, beside, kf, vec, const["band"],
                )
                result, part = lax.optimization_barrier((result, part))
                parts.append(part)
        if n < len(stages) - 1:
            result = sum(others, result)

    taps = side * side
    outs = kernel_call(
        functools.partial(last_kernel, colors),
        (shaped((colors, channels), f32),) + (shaped((channels,), f32),) * 4 + (shaped((taps, channels), f32),),
        1,
        result, *others,
    )
    return (stem_output, outs[0].T, outs[1], outs[2], outs[3], outs[5].T, outs[4])


def solution(mesh):
    return jax.shard_map(
        per_device,
        mesh=mesh,
        in_specs=(
            P(None, ("rows", "cols"), None),
            P(),
            P(),
            P(),
            P(),
            P(),
            P(),
            P(None, "rows", "cols"),
        ),
        out_specs=(P(None, "rows", "cols"), P(), P(), P(), P(), P(), P()),
        check_vma=False,
    )
```

```python
import functools
import math

import jax
import jax.numpy as jnp
import numpy as np
from jax import lax
from jax.experimental import pallas as pl
from jax.experimental.pallas import tpu as pltpu
from jax.sharding import PartitionSpec as P

norm_eps = 1e-06
side = 7
LANES = 128
GROUP = 8
OUTER = 8 * 16
VMEM = 20 * 1024 * 1024
UNROLL = 64
bf16, f32 = jnp.bfloat16, jnp.float32

NN = (((1,), (0,)), ((), ()))
NT = (((1,), (1,)), ((), ()))
TN = (((0,), (0,)), ((), ()))


def mm(a, b, dims=NN):
    return lax.dot_general(a, b, dims, preferred_element_type=f32)


def iota(shape, axis):
    return lax.broadcasted_iota(jnp.int32, shape, axis)


def split2(x):
    high = x.astype(bf16)
    return high, (x - high.astype(f32)).astype(bf16)


def one_hot(cond):
    return jnp.where(cond, 1.0, 0.0).astype(bf16)


def cdiv(a, b):
    return -(-a // b)


def constants(colors, file_rows, channels, height):
    block = colors * file_rows
    per = GROUP // file_rows
    rows = channels * GROUP
    out = {}
    at = np.arange(per * block)
    out["spread"] = (at % colors)[None, :] == np.arange(colors)[:, None]
    out["keep"] = (at // colors)[None, :] == (np.arange(rows) % GROUP)[:, None]
    out["tall"] = (np.arange(rows) // GROUP)[:, None] == np.arange(channels)[None, :]
    inner = 8 * height
    count = side * side
    forward = np.zeros((count, inner + 2 * OUTER), bool)
    taps = np.zeros((56, inner + OUTER), bool)
    for tap in range(count):
        down, copy = divmod(tap, side)
        own, above, below = height * copy + down - 3, 16 * copy + down + 5, 16 * copy + down - 3
        forward[tap, own % inner] = True
        forward[tap, inner + above] = True
        forward[tap, inner + OUTER + below % OUTER] = True
        taps[count - 1 - tap, own % inner] = True
        taps[count - 1 - tap, inner + above] = True
    out["forward"], out["backward"], out["taps"] = forward, forward[::-1], taps
    lane, row = np.arange(inner)[None, :], np.arange(height)[:, None]
    out["band"] = (abs(lane % height - row) <= 3) & (lane < height * side)
    lane, row = np.arange(OUTER)[None, :], np.arange(8)[:, None]
    at = lane % 16
    out["fringe"] = np.concatenate([(at < 8) & (at >= row + 5), (at >= 8) & (at <= row + 3)]) & (lane < 16 * side)
    pick = np.zeros((3, 56, LANES), bool)
    for n in range(3):
        pick[n, colors + 1 + n] = True
    out["pick"] = np.concatenate(list(pick), axis=1)
    return {k: jnp.asarray(v, f32 if k in ("band", "fringe") else bf16) for k, v in out.items()}


def params_kernel(wt_ref, taps_ref, bias_ref, gain_ref, off_ref, koff_ref, spread_ref, keep_ref, tall_ref, forward_ref,
                  backward_ref, wk_ref, kb_ref, kf_ref, vec_ref):
    channels = wt_ref.shape[1]
    wide = mm(wt_ref[...], spread_ref[...], TN).astype(bf16)
    wk_ref[...] = mm(tall_ref[...], wide).astype(bf16) * keep_ref[...]
    parts = split2(taps_ref[...])
    for place, out_ref in ((forward_ref, kf_ref), (backward_ref, kb_ref)):
        out_ref[...] = sum(mm(part, place[...], TN) for part in parts)
    eye = iota((channels, channels), 0) == iota((channels, channels), 1)
    for n, ref in enumerate((bias_ref, gain_ref, off_ref, koff_ref)):
        row = jnp.broadcast_to(ref[...].reshape(1, channels), (channels, channels))
        column = jnp.sum(jnp.where(eye, row, 0.0), axis=1, keepdims=True)
        vec_ref[n] = jnp.broadcast_to(column, (channels, LANES))


def pack_kernel(at_ref, x_hbm, cot_hbm, cot_ref, keep_ref, give_ref, edge_ref, edge_s, x_ref, y_ref, sems):
    colors, file_rows, width = x_ref.shape
    channels, height, _ = cot_ref.shape
    chips, block_rows, _ = keep_ref.shape
    count = width // LANES
    block = colors * file_rows
    core, chip = at_ref[0, 0], at_ref[1, 0]
    load_x = pltpu.make_async_copy(x_hbm, x_ref, sems.at[0])
    load_cot = pltpu.make_async_copy(cot_hbm, cot_ref, sems.at[1])
    load_x.start()
    load_cot.start()
    row, src = iota((block, block), 0), iota((block, block), 1)
    part = sum((row >= colors * n).astype(jnp.int32) for n in range(1, file_rows)) if file_rows > 1 else 0
    move = one_hot(src == (row - colors * part) * file_rows + part)
    load_x.wait()
    y_ref[...] = mm(move, x_ref[...].reshape(block, width)).astype(bf16)

    row, lane = iota((16, LANES), 0), iota((16, LANES), 1)
    pick = one_hot(((row < 3) & (lane == row + LANES - 3)) | ((row >= 11) & (row < 14) & (lane == row - 11)))
    zeros = jnp.zeros((16, block), f32)
    edge_s[0] = zeros
    edge_s[count + 1] = zeros
    for d in range(count):
        tile = y_ref[:, d * LANES:(d + 1) * LANES]
        edge_s[d + 1] = mm(pick, tile, NT)

    def halo(d):
        both = edge_s[d][:8] + edge_s[d + 2][8:]
        chunks = []
        for start in range(0, 2 * LANES, LANES):
            stop = min(start + LANES, block)
            if stop <= start:
                chunks.append(jnp.zeros((8, LANES), f32))
            elif stop - start < LANES:
                chunks.append(jnp.concatenate(
                    [both[:, start:stop], jnp.zeros((8, LANES - stop + start), f32)], axis=1))
            else:
                chunks.append(both[:, start:stop])
        return jnp.concatenate(chunks, axis=0).astype(bf16)

    for away in range(chips):
        there = lax.bitwise_xor(chip, away)
        for other in range(2):
            d = 2 * there + (core if (other == 0) == (away == 0) else 1 - core)
            tile = y_ref[:, pl.ds(pl.multiple_of(d * LANES, LANES), LANES)]
            if other == 0:
                keep_ref[away, :block, :] = tile
                keep_ref[away, block:, :] = halo(d)
            else:
                start = away * block_rows
                give_ref[start:start + block, :] = tile
                give_ref[start + block:start + block_rows, :] = halo(d)

    load_cot.wait()

    row, lane = iota((8, LANES), 0), iota((8, LANES), 1)
    pick = one_hot(((row < 3) & (lane == row)) | ((row >= 3) & (row < 6) & (lane == row + LANES - 6)))
    edges = mm(pick, cot_ref[...].reshape(channels * height, LANES), NT)
    edges = jnp.concatenate(
        [edges[:, n:n + LANES] for n in range(0, channels * height, LANES)], axis=0).astype(bf16)
    edge_ref[:edges.shape[0]] = edges
    edge_ref[edges.shape[0]:] = edges[:edge_ref.shape[0] - edges.shape[0]]
    give_ref[chips * block_rows:, :] = edges


def pair_kernel(keep_ref, got_ref, *pair_refs):
    _, block_rows, _ = keep_ref.shape
    for away, ref in enumerate(pair_refs):
        ref[0] = keep_ref[away]
        ref[1] = got_ref[away * block_rows:(away + 1) * block_rows, :]


def strips_kernel(at_ref, cot_ref, near_ref, far_ref, halo_ref, one_ref, two_ref):
    channels, height, width = cot_ref.shape
    size = channels * height // 16
    core = at_ref[0, 0]
    near = near_ref[near_ref.shape[0] - size:, :].astype(f32)
    far = far_ref[:size, :].astype(f32)
    left = jnp.where(core == 0, far, near)
    right = jnp.where(core == 0, near, far)
    sides = jnp.concatenate(
        [jnp.concatenate([side[n:n + 8] for n in range(0, size, 8)], axis=1) for side in (left, right)], axis=0)
    row, lane = iota((16, width), 0), iota((16, width), 1)
    from_left = (row >= 3) & (row < 6) & (lane == row + width - 6) & (at_ref[4, 0] == 0)
    from_right = (row >= 8) & (row < 11) & (lane == row - 8) & (at_ref[5, 0] == 0)
    halo = mm(sides.astype(bf16), one_hot(from_left | from_right), TN).reshape(channels, height, width)
    halo_ref[...] = halo.astype(bf16)
    write_strips(at_ref, cot_ref[...].astype(f32), halo, one_ref, two_ref)


def write_strips(at_ref, own, halo, one_ref, two_ref):
    channels, height, width = own.shape
    row, lane = iota((8, width), 0), iota((8, width), 1)
    pick = one_hot((lane == row + width - 3) & (row < 3) | (lane == row - 3) & (row >= 3) & (row < 6))
    up, down = own[:, :4], own[:, height - 4:]
    up_halo, down_halo = halo[:, :4], halo[:, height - 4:]
    even = at_ref[6, 0] == 0
    for ref, rows, beside in (
        (one_ref, jnp.where(even, down, up), jnp.where(even, down_halo, up_halo)),
        (two_ref, jnp.where(even, up, down), jnp.where(even, up_halo, down_halo)),
    ):
        ref[:channels] = rows.astype(bf16)
        dense = mm(pick, beside.reshape(channels * 4, width).astype(bf16), NT)
        for n in range(0, channels * 4, LANES):
            for q in range(2):
                ref[channels + n // 64 + q] = dense[4 * q:4 * q + 4, n:n + LANES].astype(bf16)


def read_strips(at_ref, one_ref, two_ref, plane_ref, halo_ref):
    channels, _, width = plane_ref.shape
    even = at_ref[6, 0] == 0
    one, two = one_ref[...].astype(f32), two_ref[...].astype(f32)
    top = jnp.where(at_ref[2, 0] == 0, jnp.where(even, two, one), 0.0)
    bot = jnp.where(at_ref[3, 0] == 0, jnp.where(even, one, two), 0.0)
    row, lane = iota((8, width), 0), iota((8, width), 1)
    place = one_hot((lane == row + width - 3) & (row < 3) | (lane == row - 3) & (row >= 3) & (row < 6))

    def beside(part):
        dense = jnp.concatenate(
            [
                jnp.concatenate([part[channels + n // 64 + q] for q in range(2)], axis=0)
                for n in range(0, channels * 4, LANES)
            ],
            axis=1,
        )
        return mm(dense.astype(bf16), place, TN).reshape(channels, 4, width)

    none = jnp.zeros((channels, 4, width), f32)
    plane_ref[...] = jnp.concatenate([none, top[:channels], bot[:channels], none], axis=1).astype(bf16)
    halo_ref[...] = jnp.concatenate([none, beside(top), beside(bot), none], axis=1).astype(bf16)


def shifted(center, halo):
    rows, width = center.shape
    lane = iota((rows, width), 1)
    copies = []
    for move in range(-3, 4):
        if move == 0:
            copies.append(center)
        elif move > 0:
            copies.append(pltpu.roll(jnp.where(lane < move, halo, center), width - move, 1))
        else:
            copies.append(pltpu.roll(jnp.where(lane >= width + move, halo, center), -move, 1))
    copies.append(jnp.zeros((rows, width), center.dtype))
    return jnp.concatenate(copies, axis=0)


def toeplitz(base, mask):
    return pltpu.roll(jnp.broadcast_to(base, mask.shape), 0, 1, stride=1, stride_axis=0) * mask


def inner_taps(base_ref, k, band_ref):
    inner = band_ref.shape[1]
    base = base_ref[pl.ds(k, 1), :]
    return jnp.concatenate(split2(toeplitz(base[:, :inner], band_ref[...])), axis=0)


def outer_taps(base_ref, k, inner, fringe_ref):
    base = base_ref[pl.ds(k, 1), :]
    above = toeplitz(base[:, inner:inner + OUTER], fringe_ref[:8])
    below = toeplitz(base[:, inner + OUTER:], fringe_ref[8:])
    return jnp.concatenate(split2(jnp.concatenate([above, below], axis=0)), axis=0)


def back_inner_kernel(factor, cot_ref, beside_ref, kb_ref, band_ref, stack_ref, grad_ref, total_ref, sum_ref):
    channels, height, width = cot_ref.shape

    def one(k, carry):
        plane = cot_ref[k]
        stack = shifted(plane, beside_ref[k])
        stack_ref[k] = stack
        both = mm(inner_taps(kb_ref, k, band_ref), stack)
        grad_ref[k] = (both[:height] + both[height:]) * factor
        sum_ref[k] = jnp.sum(plane.astype(f32).reshape(height // 8, 8, width), axis=0)
        return carry

    lax.fori_loop(0, channels, one, 0, unroll=UNROLL)
    total_ref[...] = sum(sum_ref[:, b, :] for b in range(8)) * factor


def back_outer_kernel(factor, at_ref, one_ref, two_ref, grad_ref, kb_ref, fringe_ref,
                      stack_ref, edge_ref, plane_ref, halo_ref):
    channels, height, width = grad_ref.shape
    read_strips(at_ref, one_ref, two_ref, plane_ref, halo_ref)

    def one(k, carry):
        stack = shifted(plane_ref[k], halo_ref[k])
        stack_ref[k] = stack
        both = mm(outer_taps(kb_ref, k, 8 * height, fringe_ref), stack)
        edge = (both[:16] + both[16:]) * factor
        edge_ref[k] = edge + jnp.concatenate([grad_ref[k, :8, :], grad_ref[k, height - 8:, :]], axis=0)
        return carry

    lax.fori_loop(0, channels, one, 0, unroll=UNROLL)


def layer_norm(patch, channels):
    values = patch.astype(bf16).astype(f32).reshape(channels, GROUP, LANES)
    center = values - jnp.mean(values, axis=0, keepdims=True)
    spread = jnp.mean(center * center, axis=0, keepdims=True)
    inverse = lax.rsqrt(spread + norm_eps)
    return center * inverse, inverse


def per_row(vec_ref, n):
    return vec_ref[n][:, None, :]


def order_kernel(at_ref, *refs):
    pair_refs, x_ref = refs[:-1], refs[-1]
    chips = len(pair_refs)
    core, chip = at_ref[0, 0], at_ref[1, 0]
    for away, ref in enumerate(pair_refs):
        there = lax.bitwise_xor(chip, away)
        x_ref[2 * there + core] = ref[0 if away == 0 else 1]
        x_ref[2 * there + 1 - core] = ref[1 if away == 0 else 0]


def main_kernel(colors, file_rows, factor, x_ref, wk_ref, vec_ref, grad_ref, edge_ref, total_ref, stack_ref, rim_ref,
                taps_ref, pick_ref, band_ref, fringe_ref, norm_ref, out_ref, norm_s, grad_s, diag_s):
    channels, height, width = grad_ref.shape
    block = colors * file_rows
    per = GROUP // file_rows
    rows = channels * GROUP
    bias, gain, offset = per_row(vec_ref, 0), per_row(vec_ref, 1), per_row(vec_ref, 2)
    scale_part = jnp.zeros((channels, GROUP, width), f32)
    shift_part = jnp.zeros((channels, GROUP, width), f32)
    inner = 8 * height
    ones = jnp.where(iota((16, width), 0) == 0, 1.0, 0.0).astype(bf16)
    by_color = jnp.zeros((colors + 16, channels), f32)
    for g in range(height // GROUP):
        if g == 0:
            pixels = [[x_ref[per * n + a, :block, :] for a in range(per)] for n in range(height // GROUP)]
            patches = mm(wk_ref[...], jnp.concatenate([jnp.concatenate(x, axis=0) for x in pixels], axis=1))
        blocks = pixels[g]
        patch = patches[:, g * width:(g + 1) * width].reshape(channels, GROUP, width) + bias
        xhat, inverse = layer_norm(patch, channels)
        norm_s[:, g * GROUP:(g + 1) * GROUP, :] = xhat * gain + offset
        if g == 0:
            grad = edge_ref[:, :8, :]
        elif g == height // GROUP - 1:
            grad = edge_ref[:, 8:, :]
        else:
            grad = grad_ref[:, g * GROUP:(g + 1) * GROUP, :]
        scale_part += grad * xhat
        shift_part += grad
        inside = grad * gain
        mean_a = jnp.mean(inside, axis=0, keepdims=True)
        mean_b = jnp.mean(inside * xhat, axis=0, keepdims=True)
        grad_s[g] = (inverse * (inside - mean_a - xhat * mean_b)).reshape(rows, width)
        left, right = [], []
        for h in range(GROUP):
            start = h % file_rows * colors
            left.append(jnp.concatenate([blocks[h // file_rows][start:start + colors], ones], axis=0))
            right.append(grad_s[g, pl.ds(h, channels, stride=GROUP), :].astype(bf16))
        by_color += mm(jnp.concatenate(left, axis=1), jnp.concatenate(right, axis=1), NT)

    band, fringe = band_ref[...], fringe_ref[...]
    none = jnp.zeros((height, width), bf16)

    def one(n, carry):
        planes, stacks = [], []
        for m in range(2):
            k = 2 * n + m
            plane = norm_s[k].astype(bf16)
            norm_ref[k] = plane
            planes.append(jnp.concatenate([plane, none] if m == 0 else [none, plane], axis=1))
            stacks.append(jnp.concatenate([stack_ref[k], rim_ref[k]], axis=0))
        both = mm(jnp.concatenate(planes, axis=0), jnp.concatenate(stacks, axis=1), NT)
        for m in range(2):
            cross = both[m * height:(m + 1) * height, :inner]
            total = cross[:8] * band[:8]
            for a in range(1, height // 8):
                rows = cross[8 * a:8 * a + 8]
                if a == height // 8 - 1:
                    rows = rows * band[8 * a:]
                total += pltpu.roll(rows, inner - 8 * a, 1)
            cross = both[m * height:(m + 1) * height, inner:]
            rim = cross[:8] * fringe[:8] + pltpu.roll(cross[height - 8:] * fringe[8:], 8, 1)
            diag_s[2 * n + m] = jnp.concatenate([total, rim], axis=1)
        return carry

    lax.fori_loop(0, channels // 2, one, 0, unroll=UNROLL // 2)

    line, rim = diag_s[:, 0, :inner], diag_s[:, 0, inner:]
    for b in range(1, 8):
        line += pltpu.roll(diag_s[:, b, :inner], inner - b, 1)
        rim += pltpu.roll(diag_s[:, b, inner:], OUTER - b, 1)
    line = jnp.concatenate([line, rim], axis=1) * factor
    line = jnp.concatenate([jnp.zeros((LANES - channels, line.shape[1]), f32), line], axis=0)
    out_ref[...] = mm(jnp.concatenate([taps_ref[...]] * 2, axis=1), jnp.concatenate(split2(line), axis=1), NT)
    parts = jnp.concatenate([jnp.sum(scale_part, axis=1), jnp.sum(shift_part, axis=1), total_ref[...]], axis=1)
    first = mm(jnp.concatenate([pick_ref[...]] * 2, axis=1), jnp.concatenate(split2(parts), axis=1), NT)
    out_ref[:, :channels] = first + by_color[:56]


def side_line(pieces, block):
    parts = []
    for piece in pieces:
        piece = piece.astype(f32)
        for start in range(0, block, LANES):
            at = start // LANES * 8
            parts.append(piece[at:at + 8, :min(LANES, block - start)])
    return jnp.concatenate(parts, axis=1)


def stem_side_kernel(colors, file_rows, at_ref, x_ref, norm_ref, wk_ref, vec_ref, halo_ref, one_ref, two_ref):
    channels, height, width = halo_ref.shape
    block = colors * file_rows
    per = GROUP // file_rows
    groups = height // GROUP
    shape = (channels, GROUP, LANES)
    bias, gain, offset = per_row(vec_ref, 0), per_row(vec_ref, 1), per_row(vec_ref, 2)
    lines = [side_line([x_ref[per * g + a, block:block + 16, :] for a in range(per)], block) for g in range(groups)]
    lines.append(jnp.zeros((LANES - 8 * groups, wk_ref.shape[1]), f32))
    lines = jnp.concatenate(lines, axis=0).astype(bf16)
    xhat, _ = layer_norm(mm(wk_ref[...], lines, NT).reshape(shape) + bias, channels)
    column = lax.bitwise_and(iota(shape, 2), 7)
    ok = jnp.where(column < 3, 1 - at_ref[4, 0], 1 - at_ref[5, 0]) > 0
    halo = jnp.where(ok, xhat * gain + offset, 0.0).astype(bf16).reshape(channels * GROUP, LANES)
    for g in range(groups):
        moved = pltpu.roll(halo, width - 8 * g - 3, 1).reshape(channels, GROUP, width)
        halo_ref[:, 8 * g:8 * g + 8, :] = moved
    write_strips(at_ref, norm_ref[...].astype(f32), halo_ref[...].astype(f32), one_ref, two_ref)


def stem_inner_kernel(start, norm_ref, side_ref, kf_ref, vec_ref, band_ref, out_ref):
    count, height, _ = out_ref.shape

    def one(n, carry):
        k = start + n
        both = mm(inner_taps(kf_ref, k, band_ref), shifted(norm_ref[k], side_ref[k]))
        out_ref[n] = both[:height] + both[height:] + vec_ref[3, pl.ds(k, 1), :]
        return carry

    lax.fori_loop(0, count, one, 0, unroll=min(UNROLL, count))


def stem_outer_kernel(at_ref, one_ref, two_ref, norm_ref, side_ref, kf_ref, vec_ref, band_ref, fringe_ref, inner_ref,
                      out_ref, plane_s, halo_s, out_s, sems):
    channels, height, _ = out_s.shape
    done = inner_ref.shape[0]
    read_strips(at_ref, one_ref, two_ref, plane_s, halo_s)

    def one(k, own):
        both = mm(outer_taps(kf_ref, k, 8 * height, fringe_ref), shifted(plane_s[k], halo_s[k]))
        edge = both[:16] + both[16:]
        out_s[k] = jnp.concatenate(
            [own[:8] + edge[:8], own[8:height - 8], own[height - 8:] + edge[8:]], axis=0).astype(bf16)

    def first(k, carry):
        one(k, inner_ref[k])
        return carry

    def second(n, carry):
        k = done + n
        both = mm(inner_taps(kf_ref, k, band_ref), shifted(norm_ref[k], side_ref[k]))
        one(k, both[:height] + both[height:] + vec_ref[3, pl.ds(k, 1), :])
        return carry

    copies = []
    for start, count, body in ((0, done, first), (done, channels - done, second)):
        lax.fori_loop(0, count, body, 0, unroll=min(UNROLL, count))
        here = pl.ds(start, count)
        copies.append(pltpu.make_async_copy(out_s.at[here], out_ref.at[here], sems.at[len(copies)]))
        copies[-1].start()
    for copy in copies:
        copy.wait()


def last_kernel(colors, *refs):
    parts, outs = refs[:-6], refs[-6:]
    total = sum(part[...] for part in parts)
    channels = outs[1].shape[0]
    first = total[:, :channels]
    second = total[:, channels:2 * channels]
    outs[0][...] = first[:colors]
    for n in range(4):
        outs[1 + n][...] = first[colors + n]
    outs[5][...] = second[:outs[5].shape[0]]


def in_vmem(shape, dtype):
    return pltpu.VMEM(shape, dtype)


def kernel_call(body, out_shape, us, *args, loose=(), **kw):
    loose = tuple(loose) + tuple(kw.get("input_output_aliases", {}))
    args = [
        arg if n in loose else pltpu.with_memory_space_constraint(arg, pltpu.VMEM)
        for n, arg in enumerate(args)
    ]
    return pl.pallas_call(
        body,
        out_shape=out_shape,
        compiler_params=pltpu.CompilerParams(vmem_limit_bytes=VMEM),
        cost_estimate=pl.CostEstimate(flops=int(us * 1e9), bytes_accessed=int(us * 3e6), transcendentals=0),
        **kw,
    )(*args)


def shaped(shape, dtype):
    return jax.ShapeDtypeStruct(shape, dtype)


def pairing(count, odd):
    return [(i, (i + 1 if (i + odd) % 2 == 0 else i - 1) % count) for i in range(count)]


def swap(parts, axis):
    return [lax.ppermute(part, axis, pairing(lax.axis_size(axis), n)) for n, part in enumerate(parts)]


def per_device(
    file_pixels,
    patchify_weight,
    patchify_bias,
    norm_gain,
    norm_offset_vector,
    kernel,
    kernel_offset,
    cotangent,
):
    colors, file_rows, _ = file_pixels.shape
    channels, height, width = cotangent.shape
    n_rows, n_cols = lax.axis_size("rows"), lax.axis_size("cols")
    factor = 1.0 / math.sqrt(height * n_rows * width * n_cols)
    block = colors * file_rows
    per = GROUP // file_rows
    block_rows = block + 16
    rows = channels * GROUP
    tile = (channels, height, width)
    inner = 8 * height
    const = constants(colors, file_rows, channels, height)

    row_at, col_at = lax.axis_index("rows"), lax.axis_index("cols")
    chips = n_cols // 2
    at = (col_at % 2, col_at // 2, row_at == 0, row_at == n_rows - 1, col_at == 0, col_at == n_cols - 1, row_at % 2)
    at = sum(jnp.where(iota((8, LANES), 0) == n, x.astype(jnp.int32), 0) for n, x in enumerate(at))
    vmem = pl.BlockSpec(memory_space=pltpu.VMEM)
    edge_rows = channels * height // 16

    beyond = pl.BlockSpec(memory_space=pl.ANY)
    cot, keep, give, edges = kernel_call(
        pack_kernel,
        (
            in_vmem(tile, bf16),
            in_vmem((chips, block_rows, LANES), bf16),
            in_vmem((chips * block_rows + edge_rows, LANES), bf16),
            in_vmem((edge_rows + 32, LANES), bf16),
        ),
        2,
        at, *(pltpu.with_memory_space_constraint(arg, pltpu.HBM) for arg in (file_pixels, cotangent)),
        loose=(1, 2),
        in_specs=[vmem] + [beyond] * 2,
        scratch_shapes=[
            pltpu.VMEM((n_cols + 2, 16, block), f32),
            pltpu.VMEM(file_pixels.shape, bf16),
            pltpu.VMEM((block, n_cols * LANES), bf16),
            pltpu.SemaphoreType.DMA((2,)),
        ],
    )
    got = lax.ppermute(give, "cols", [(i, i ^ 1) for i in range(n_cols)])
    far = lax.ppermute(edges, "cols", pairing(n_cols, 1))
    pairs = kernel_call(pair_kernel, (in_vmem((2, block_rows, LANES), bf16),) * chips, 0.5, keep, got)
    pairs = [pairs[0]] + [
        lax.ppermute(pairs[n], "cols", [(i, i ^ (2 * n + 1)) for i in range(n_cols)])
        for n in range(1, chips)
    ]

    kept, far = lax.optimization_barrier((pairs[0], far))
    pairs[0] = kept
    beside, *strips = kernel_call(
        strips_kernel,
        (in_vmem(tile, bf16), in_vmem((channels + channels // 16, 4, width), bf16), in_vmem((channels + channels // 16, 4, width), bf16)),
        0.01,
        at, cot, got, far,
        in_specs=[vmem] + [vmem] * 3,
    )
    beside, taps = lax.optimization_barrier((beside, kernel))
    strips = swap(strips, "rows")
    wk, kb, kf, vec = kernel_call(
        params_kernel,
        (
            in_vmem((rows, per * block), bf16),
            in_vmem((channels, inner + 2 * OUTER), f32),
            in_vmem((channels, inner + 2 * OUTER), f32),
            in_vmem((4, channels, LANES), f32),
        ),
        0.01,
        patchify_weight.T, taps.T, patchify_bias, norm_gain, norm_offset_vector, kernel_offset,
        const["spread"], const["keep"], const["tall"], const["forward"], const["backward"],
    )
    stack, grad, total = kernel_call(
        functools.partial(back_inner_kernel, factor),
        (in_vmem((channels, inner, width), bf16), in_vmem(tile, f32), in_vmem((channels, width), f32)),
        0.01,
        cot, beside, kb, const["band"],
        scratch_shapes=[pltpu.VMEM((channels, 8, width), f32)],
    )
    rim, edge = kernel_call(
        functools.partial(back_outer_kernel, factor),
        (in_vmem((channels, OUTER, width), bf16), in_vmem((channels, 16, width), f32)),
        0.01,
        at, *strips, grad, kb, const["fringe"],
        scratch_shapes=[pltpu.VMEM((channels, 16, width), bf16)] * 2,
    )

    edge, *pairs = lax.optimization_barrier((edge, *pairs))
    pixels = kernel_call(order_kernel, in_vmem((n_cols, block_rows, LANES), bf16), 0.01, at, *pairs)
    norm, result = kernel_call(
        functools.partial(main_kernel, colors, file_rows, factor),
        (in_vmem(tile, bf16), in_vmem((56, LANES), f32)),
        6,
        pixels, wk, vec, grad, edge, total, stack, rim, const["taps"], const["pick"], const["band"], const["fringe"],
        scratch_shapes=[
            pltpu.VMEM(tile, f32),
            pltpu.VMEM((height // GROUP, rows, width), f32),
            pltpu.VMEM((channels, 8, inner + OUTER), f32),
        ],
    )

    size = n_rows * n_cols
    chunk = channels // 4
    stages = [[1], [3, 5, 7], [9, 17, 25]]
    jobs = {0: ["side"], 1: ["one", "two", 0], 2: ["outer"]}
    parts = []
    for n, steps in enumerate(stages):
        others = [lax.ppermute(result, ("rows", "cols"), [(i, i ^ step) for i in range(size)]) for step in steps]
        for job in jobs.get(n, []):
            if job in ("one", "two"):
                which = ("one", "two").index(job)
                result, end = lax.optimization_barrier((result, ends[which]))
                ends[which] = lax.ppermute(end, "rows", pairing(n_rows, which))
            elif job == "side":
                result, norm = lax.optimization_barrier((result, norm))
                beside, *ends = kernel_call(
                    functools.partial(stem_side_kernel, colors, file_rows),
                    (in_vmem(tile, bf16),) + (in_vmem((channels + channels // 16, 4, width), bf16),) * 2,
                    1,
                    at, pixels, norm, wk, vec,
                )
                result, beside = lax.optimization_barrier((result, beside))
            elif job == "outer":
                result, *parts = lax.optimization_barrier((result, *parts))
                stem_output = kernel_call(
                    stem_outer_kernel,
                    shaped(tile, bf16),
                    3,
                    at, *ends, norm, beside, kf, vec, const["band"], const["fringe"], *parts,
                    in_specs=[vmem] * 10,
                    out_specs=beyond,
                    scratch_shapes=[
                        pltpu.VMEM((channels, 16, width), bf16),
                        pltpu.VMEM((channels, 16, width), bf16),
                        pltpu.VMEM(tile, bf16),
                        pltpu.SemaphoreType.DMA((2,)),
                    ],
                )
                result, stem_output = lax.optimization_barrier((result, stem_output))
            else:
                result, norm = lax.optimization_barrier((result, norm))
                part = kernel_call(
                    functools.partial(stem_inner_kernel, job * chunk),
                    in_vmem((chunk, height, width), f32),
                    2,
                    norm, beside, kf, vec, const["band"],
                )
                result, part = lax.optimization_barrier((result, part))
                parts.append(part)
        if n < len(stages) - 1:
            result = sum(others, result)

    taps = side * side
    outs = kernel_call(
        functools.partial(last_kernel, colors),
        (shaped((colors, channels), f32),) + (shaped((channels,), f32),) * 4 + (shaped((taps, channels), f32),),
        1,
        result, *others,
    )
    return (stem_output, outs[0].T, outs[1], outs[2], outs[3], outs[5].T, outs[4])


def solution(mesh):
    return jax.shard_map(
        per_device,
        mesh=mesh,
        in_specs=(
            P(None, ("rows", "cols"), None),
            P(),
            P(),
            P(),
            P(),
            P(),
            P(),
            P(None, "rows", "cols"),
        ),
        out_specs=(P(None, "rows", "cols"), P(), P(), P(), P(), P(), P()),
        check_vma=False,
    )
```
